32 devices in a mesh: pipe: 2 (over y), dp: 16 (over z, x, core).
Axes of the slice: x: 2, y: 2, z: 4, core: 2. Of those that a mesh axis runs over, the one named last changes fastest.
Arguments:
- features: bfloat16 [32, 336, 512], P('dp'), may hold values from -6 to 6
- plan: int32 [16, 2], P('dp'), may hold values from 0 to 1, each once within a row
- trunk_weight: bfloat16 [2, 3, 3, 512, 512], replicated, may hold values from -0.125 to 0.125
- trunk_gain: float32 [2, 512], replicated, may hold values from 0.1 to 1.9
- trunk_shift: float32 [2, 512], replicated, may hold values from -3 to 3
- head_weight: bfloat16 [2, 512, 1792], replicated, may hold values from -0.25 to 0.25
- norm_scale: float32 [2, 512], replicated, may hold values from 0.1 to 1.9
- merging_weight: float32 [2, 3, 1792], replicated, may hold values from -3 to 3
- merged_cotangent: bfloat16 [32, 64, 1792], P('dp'), may hold values from -6 to 6
Outputs:
- merged_maps: bfloat16 [32, 64, 1792], P('dp', None, 'pipe')
- features_grad: float32 [32, 336, 512], P('dp', None, 'pipe')
- trunk_weight_grad: float32 [2, 3, 3, 512, 512], replicated
- head_weight_grad: float32 [2, 512, 1792], replicated
- norm_scale_grad: float32 [2, 512], replicated
- merging_weight_grad: float32 [2, 3, 1792], replicated
The draws below stay inside these ranges and needn't reach their ends.
Inputs may be any that keep to these rules, and one draw needn't show every extreme that they name: `plan`: each row names every micro-batch's image once.
All inputs are finite; a program needn't handle non-finite values.
Results may differ from the reference program's by a relative error of at most 0.0074.
Values may be sent and summed in bfloat16 or wider, within the bound.
No kernel may reach another device: no remote copies, remote signals or barrier semaphores. Data moves between devices by JAX's collectives and lax.ppermute only.
A program may use at most 192 MiB of HBM per device.

```python
import jax
import jax.numpy as jnp
from jax import lax

C = 512
LAYERS = 2
TAPS = 2
SCALES = 3
MICRO = 2
SIDE = 16
HC = 1792
MID = 8
PIX = 336
GROUPS = 16
IMAGES = 32


def steps_of(key, shape, split, least, top_value):
    loudness, own = 1.0, jax.random.fold_in(key, 6)
    for dim, shards_of in split:
        draws = jnp.exp(jax.random.uniform(jax.random.fold_in(own, dim), (shards_of,), jnp.float32, least / len(split), top_value / len(split)))
        loudness = loudness * jnp.repeat(draws, shape[dim] // shards_of).reshape([-1 if axis == dim else 1 for axis in range(len(shape))])
    return loudness


def scatter_about(key, shape, scale, most, shards=(), kind=jnp.bfloat16):
    entries = jax.random.normal(key, shape, jnp.float32) * scale
    if len(shards) > 0:
        entries = steps_of(key, shape, shards, -0.22, 0.18) * entries
    return jnp.clip(entries, min=-most, max=most).astype(kind)


def setup_inputs(seed: int = 0) -> dict:
    arg_keys = jax.random.split(jax.random.key(seed), 10)
    features = scatter_about(arg_keys[0], (IMAGES, PIX, C), 1.0, 6.0, ((0, 16),))
    plan = jax.vmap(lambda own: jax.random.permutation(own, MICRO))(jax.random.split(arg_keys[1], GROUPS)).reshape((GROUPS, MICRO)).astype(jnp.int32)
    trunk_weight = scatter_about(arg_keys[2], (LAYERS, 3, 3, C, C), (9 * C // 2) ** -0.5, 0.125)
    trunk_gain = jnp.clip(1.0 + 0.18 * jax.random.normal(arg_keys[3], (LAYERS, C), jnp.float32), 0.1, 1.9)
    trunk_shift = scatter_about(arg_keys[4], (LAYERS, C), 0.5, 3.0, (), jnp.float32)
    head_weight = scatter_about(arg_keys[5], (TAPS, C, HC), C ** -0.5, 0.25)
    norm_scale = jnp.clip(1.0 + 0.18 * jax.random.normal(arg_keys[6], (TAPS, C), jnp.float32), 0.1, 1.9)
    merging_weight = scatter_about(arg_keys[7], (TAPS, SCALES, HC), 0.5, 3.0, (), jnp.float32)
    merged_cotangent = scatter_about(arg_keys[8], (IMAGES, MID * MID, HC), 1.0, 6.0, ((0, 16),))
    return {"features": features, "plan": plan, "trunk_weight": trunk_weight, "trunk_gain": trunk_gain, "trunk_shift": trunk_shift, "head_weight": head_weight, "norm_scale": norm_scale, "merging_weight": merging_weight, "merged_cotangent": merged_cotangent}


@jax.custom_vjp
def low(v):
    return lax.optimization_barrier(v.astype(jnp.bfloat16)).astype(jnp.float32)

@jax.custom_vjp
def low_back(v):
    return v

def low_keep(v):
    return (low(v), None)

def low_pass(kept, grad):
    return (grad,)

def back_keep(v):
    return (v, None)

def back_low(kept, grad):
    return (low(grad),)
low.defvjp(low_keep, low_pass)
low_back.defvjp(back_keep, back_low)
epsilon = 1e-06
highest = lax.Precision.HIGHEST

def split_scales(flat_rows, grid_side):
    finest_end = grid_side * grid_side
    middle_end = finest_end + (grid_side // 2) ** 2
    return [flat_rows[:finest_end].reshape(grid_side, grid_side, -1), flat_rows[finest_end:middle_end].reshape(grid_side // 2, grid_side // 2, -1), flat_rows[middle_end:].reshape(grid_side // 4, grid_side // 4, -1)]

def patches(scale_grid):
    extent = scale_grid.shape[0]
    padded = jnp.pad(scale_grid, ((1, 1), (1, 1), (0, 0)))
    pieces = [padded[row_off:row_off + extent, col_off:col_off + extent] for row_off in range(3) for col_off in range(3)]
    return jnp.concatenate(pieces, axis=-1).reshape(extent * extent, -1)

def norm_fn(tap_value, scale_row):
    return tap_value * lax.rsqrt(lax.optimization_barrier(jnp.mean(tap_value * tap_value, axis=-1, keepdims=True)) + epsilon) * scale_row

def merge_maps(head_maps, weights_merge, grid_side):
    middle = grid_side // 2
    summed = 0.0
    for tap_num in range(len(head_maps)):
        finest, medium, coarse = split_scales(head_maps[tap_num], grid_side)
        pooled = finest.reshape(middle, 2, middle, 2, -1).mean(axis=(1, 3))
        spread = jnp.repeat(jnp.repeat(coarse, 2, axis=0), 2, axis=1)
        summed = summed + weights_merge[tap_num, 0] * pooled + weights_merge[tap_num, 1] * medium + weights_merge[tap_num, 2] * spread
    return summed.reshape(middle * middle, -1)

def one_image(sample, params):
    weights, gain_rows, shifts, head_weight, norm_scale, merging_weight = params
    tap_parts = []
    for scale_grid in split_scales(sample, SIDE):
        extent = scale_grid.shape[0]
        hidden = scale_grid
        for layer_num in range(LAYERS):
            pre_act = low_back(jnp.dot(patches(hidden), weights[layer_num], precision=highest))
            activated = jax.nn.gelu(gain_rows[layer_num] * pre_act + shifts[layer_num], approximate=True)
            if layer_num + 1 < LAYERS:
                hidden = low(activated)
            else:
                hidden = low(low_back(activated))
            hidden = hidden.reshape(extent, extent, -1)
        tap_parts.append(hidden.reshape(extent * extent, -1))
    tap_list = [sample, jnp.concatenate(tap_parts, axis=0)]
    head_maps = []
    for tap_num in range(TAPS):
        normed = low(norm_fn(tap_list[tap_num], norm_scale[tap_num]))
        head_maps.append(low_back(jnp.dot(normed, head_weight[tap_num], precision=highest)))
    return merge_maps(head_maps, merging_weight, SIDE)

def reference(features, plan, trunk_weight, trunk_gain, trunk_shift, head_weight, norm_scale, merging_weight, merged_cotangent):
    groups = jnp.arange(GROUPS, dtype=jnp.int32)[:, None] * MICRO
    picked = (groups + plan.astype(jnp.int32)).reshape(-1).astype(jnp.int32)
    params = (trunk_weight.astype(jnp.float32).reshape(LAYERS, 9 * C, C), trunk_gain.astype(jnp.float32), trunk_shift.astype(jnp.float32), head_weight.astype(jnp.float32), norm_scale.astype(jnp.float32), merging_weight.astype(jnp.float32))

    def forward(inputs, params):
        ordered = jnp.take(inputs, picked, axis=0)
        return lax.map(jax.checkpoint(lambda sample: one_image(sample, params)), ordered)
    merged_sum, pullback = jax.vjp(forward, features.astype(jnp.float32), params)
    feature_grad, param_grads = pullback(merged_cotangent.astype(jnp.float32))
    return (merged_sum.astype(jnp.bfloat16), feature_grad, param_grads[0].reshape(LAYERS, 3, 3, C, C), param_grads[3], param_grads[4], param_grads[5])
```

```python
from functools import partial

import jax
import jax.numpy as jnp
from jax import lax
from jax.experimental import pallas as pl
from jax.experimental.pallas import tpu as pltpu
from jax.sharding import PartitionSpec as P

SIDE = 16
EPSILON = 1e-06
F32 = jnp.float32
BF16 = jnp.bfloat16
AXES = ("pipe", "dp")
VMEM_BYTES = 50 * 1024 * 1024


def spec(memory):
    return pl.BlockSpec(memory_space=memory)


def params():
    return pltpu.CompilerParams(vmem_limit_bytes=VMEM_BYTES)


def grids(side):
    first = 0
    found = []
    for extent in (side, side // 2, side // 4):
        found.append((first, extent))
        first += extent * extent
    return found


def rows_of(side):
    return side * side + (side // 2) ** 2 + (side // 4) ** 2


def iota(shape, dim):
    return lax.broadcasted_iota(jnp.int32, shape, dim)


def edge_masks(side):
    row = iota((rows_of(side), 1), 0)
    first = jnp.zeros(row.shape, jnp.bool_)
    last = jnp.zeros(row.shape, jnp.bool_)
    for start, extent in grids(side):
        inside = (row >= start) & (row < start + extent * extent)
        column = (row - start) & (extent - 1)
        first = first | (inside & (column == 0))
        last = last | (inside & (column == extent - 1))
    return first, last


def column_shifts(value, side, target):
    first, last = edge_masks(side)
    rows = value.shape[0]
    target[0] = jnp.where(first, 0.0, pltpu.roll(value, 1, 0))
    target[1] = value
    target[2] = jnp.where(last, 0.0, pltpu.roll(value, rows - 1, 0))


def row_shift(shifted, b, a, side):
    parts = []
    width = shifted.shape[2]
    for start, extent in grids(side):
        count = extent * extent
        if a == 1:
            part = shifted[b, start : start + count, :]
        elif extent % 8 == 0:
            blank = jnp.zeros((extent, width), F32)
            if a == 0:
                part = jnp.concatenate([blank, shifted[b, start : start + count - extent, :]], axis=0)
            else:
                part = jnp.concatenate([shifted[b, start + extent : start + count, :], blank], axis=0)
        else:
            whole = shifted[b, start : start + count, :]
            row = iota((count, 1), 0)
            if a == 0:
                part = jnp.where(row < extent, 0.0, pltpu.roll(whole, extent, 0))
            else:
                part = jnp.where(row >= count - extent, 0.0, pltpu.roll(whole, count - extent, 0))
        parts.append(part.astype(BF16))
    return parts


def put_row_shift(target, row_start, lane_start, shifted, b, a, side):
    width = shifted.shape[2]
    for (start, extent), part in zip(grids(side), row_shift(shifted, b, a, side)):
        target[
            row_start + start : row_start + start + extent * extent, lane_start : lane_start + width
        ] = part


def dot(left, right):
    return lax.dot_general(left, right, (((1,), (0,)), ((), ())), preferred_element_type=F32)


def dot_last(left, right):
    return lax.dot_general(left, right, (((1,), (1,)), ((), ())), preferred_element_type=F32)


def block_of(index, extent):
    return (index // extent // 2) * (extent // 2) + (index % extent) // 2


def pool_matrix(extent, value):
    count = extent * extent
    shape = (count // 4, count)
    return jnp.where(block_of(iota(shape, 1), extent) == iota(shape, 0), value, 0.0).astype(BF16)


def spread_matrix(extent):
    count = extent * extent
    shape = (count, count // 4)
    return jnp.where(block_of(iota(shape, 0), extent) == iota(shape, 1), 1.0, 0.0).astype(BF16)


def spread(matrix, value):
    high = value.astype(BF16)
    low = (value - high.astype(F32)).astype(BF16)
    return dot(matrix, high) + dot(matrix, low)


def gelu_and_slope(z):
    root = 0.7978845608028654
    inner = root * (z + 0.044715 * z * z * z)
    t = jnp.tanh(inner)
    half = 0.5 * (1.0 + t)
    slope = half + 0.5 * z * (1.0 - t * t) * (root * (1.0 + 3 * 0.044715 * z * z))
    return z * half, slope


def head_cotangents(cot, coarse_cot, weights):
    return jnp.concatenate(
        [
            (weights[0:1] * cot).astype(BF16),
            (weights[1:2] * cot).astype(BF16),
            (weights[2:3] * coarse_cot).astype(BF16),
        ],
        axis=0,
    )


def copies(pairs, sems):
    made = [
        pltpu.make_async_copy(source, target, sems.at[num])
        for num, (source, target) in enumerate(pairs)
    ]
    for one in made:
        one.start()
    return made


def section_kernel(
    side,
    info,
    features,
    trunk_weight,
    head_weight,
    cotangent,
    gain,
    shift,
    scale,
    merging,
    own_out,
    send_out,
    slope_out,
    tap_grad_out,
    merged_out,
    small_out,
    feed,
    weights,
    heads,
    cot_ref,
    shifted,
    patch,
    sems,
):
    rows = rows_of(side)
    mid = (side // 2) ** 2
    fine = side * side
    coarse = (side // 4) ** 2
    channels = feed.shape[1]
    half = channels // 2
    width = heads.shape[2]
    core = info[1]
    made = copies(
        [(features.at[info[0]], feed)]
        + [
            (
                trunk_weight.at[num // 3, pl.ds(num % 3 * 3 * channels, 3 * channels)],
                weights.at[num],
            )
            for num in range(6)
        ]
        + [(cotangent.at[info[2]], cot_ref)]
        + [(head_weight.at[num], heads.at[num]) for num in range(2)],
        sems,
    )
    made[0].wait()

    def conv(value, layer):
        column_shifts(value, side, shifted)
        total = jnp.zeros((rows, channels), F32)
        for a in range(3):
            for b in range(3):
                put_row_shift(patch, 0, b * channels, shifted, b, a, side)
            made[1 + 3 * layer + a].wait()
            total = total + dot(patch[...], weights[3 * layer + a])
        return total

    def put_halves(first, value):
        count = value.shape[0]
        left = value[:, :half]
        right = value[:, half:]
        own_out[first : first + count, :] = jnp.where(core == 0, left, right)
        send_out[first : first + count, :] = jnp.where(core == 0, right, left)

    low_feed = feed[...]
    feed_value = low_feed.astype(F32)
    put_halves(0, low_feed)
    z1 = gain[0:1, :] * conv(feed_value, 0) + shift[0:1, :]
    act1, slope1 = gelu_and_slope(z1)
    slope_out[...] = slope1 * gain[0:1, :]
    low_act = act1.astype(BF16)
    put_halves(rows, low_act)
    z2 = gain[1:2, :] * conv(low_act.astype(F32), 1) + shift[1:2, :]
    trunk_out, slope2 = gelu_and_slope(z2)
    taps = [feed_value, trunk_out.astype(BF16).astype(F32)]

    made[7].wait()
    cot_low = cot_ref[...]
    cot = cot_low.astype(F32)
    coarse_cot = dot(pool_matrix(side // 2, 1.0), cot_low)
    pool = pool_matrix(side, 0.25)
    wide = spread_matrix(side)
    merged = jnp.zeros((mid, width), F32)
    coarse_merged = jnp.zeros((coarse, width), F32)
    scale_rows = []
    stacked = 2 * mid + coarse
    for k in range(2):
        tap = taps[k]
        scale_row = scale[k : k + 1, :]
        r = lax.rsqrt(jnp.mean(tap * tap, axis=-1, keepdims=True) + EPSILON)
        normed = (tap * r * scale_row).astype(BF16)
        pooled = dot(pool, normed[:fine]).astype(BF16)
        rows_k = jnp.concatenate([pooled, normed[fine:]], axis=0)
        put_halves(2 * rows + k * stacked, rows_k)
        made[8 + k].wait()
        product = dot(rows_k, heads[k])
        weights_k = merging[k]
        merged = merged + weights_k[0:1] * product[:mid] + weights_k[1:2] * product[mid : 2 * mid]
        coarse_merged = coarse_merged + weights_k[2:3] * product[2 * mid :]
        small_out[3 * k : 3 * k + 1, :] = jnp.sum(cot * product[:mid], axis=0, keepdims=True)
        small_out[3 * k + 1 : 3 * k + 2, :] = jnp.sum(
            cot * product[mid : 2 * mid], axis=0, keepdims=True
        )
        small_out[3 * k + 2 : 3 * k + 3, :] = jnp.sum(
            coarse_cot * product[2 * mid :], axis=0, keepdims=True
        )
        grads = head_cotangents(cot, coarse_cot, weights_k)
        back = dot_last(grads, heads[k])
        back = jnp.concatenate([spread(wide, 0.25 * back[:mid]), back[mid:]], axis=0)
        upstream = back * scale_row
        tap_grad = r * (
            upstream - tap * (r * r) * jnp.mean(upstream * tap, axis=-1, keepdims=True)
        )
        scale_rows.append(jnp.sum(back * tap * r, axis=0, keepdims=True))
        if k == 0:
            tap_grad_out[...] = tap_grad
    small_out[6:7, :] = jnp.concatenate(
        scale_rows + [jnp.zeros((1, width - 2 * channels), F32)], axis=1
    )
    small_out[7:8, :] = jnp.zeros((1, width), F32)
    merged = merged + spread(spread_matrix(side // 2), coarse_merged)
    merged_out[...] = merged.astype(BF16)
    grad2 = (tap_grad.astype(BF16).astype(F32) * slope2 * gain[1:2, :]).astype(BF16)
    first = 2 * rows + 2 * stacked
    for target in (own_out, send_out):
        target[first : first + rows, :] = grad2[:, :half]
        target[first + rows : first + 2 * rows, :] = grad2[:, half:]
        for num in range(width // half):
            target[first + 2 * rows + num * mid : first + 2 * rows + (num + 1) * mid, :] = cot_low[
                :, num * half : (num + 1) * half
            ]


def section(info, features, trunk_weight, head_weight, cotangent, gain, shift, scale, merging):
    side = SIDE
    rows = rows_of(side)
    channels = features.shape[2]
    half = channels // 2
    width = head_weight.shape[2]
    mid = cotangent.shape[1]
    sent = 2 * rows + 2 * (2 * mid + (side // 4) ** 2) + 2 * rows + width // half * mid
    vmem = spec(pltpu.VMEM)
    hbm = spec(pl.ANY)
    return pl.pallas_call(
        partial(section_kernel, side),
        out_shape=(
            jax.ShapeDtypeStruct((sent, half), BF16),
            jax.ShapeDtypeStruct((sent, half), BF16),
            jax.ShapeDtypeStruct((rows, channels), F32),
            jax.ShapeDtypeStruct((rows, channels), F32),
            jax.ShapeDtypeStruct((mid, width), BF16),
            jax.ShapeDtypeStruct((8, width), F32),
        ),
        in_specs=[spec(pltpu.SMEM), hbm, hbm, hbm, hbm, vmem, vmem, vmem, vmem],
        out_specs=(vmem,) * 6,
        scratch_shapes=[
            pltpu.VMEM((rows, channels), BF16),
            pltpu.VMEM((6, 3 * channels, channels), BF16),
            pltpu.VMEM((2, channels, width), BF16),
            pltpu.VMEM((mid, width), BF16),
            pltpu.VMEM((3, rows, channels), F32),
            pltpu.VMEM((rows, 3 * channels), BF16),
            pltpu.SemaphoreType.DMA((10,)),
        ],
        compiler_params=params(),
        name="section",
    )(info, features, trunk_weight, head_weight, cotangent, gain, shift, scale, merging)


def back_kernel(side, layer, grad, trunk_weight, factor, *rest):
    if layer == 0:
        pick, own_out, send_out, weights, shifted, patch, sems = rest
    else:
        grad_out, weights, shifted, patch, sems = rest
    channels = trunk_weight.shape[2]
    half = channels // 2
    rows = rows_of(side)
    made = copies(
        [
            (trunk_weight.at[layer, pl.ds(num * 3 * channels, 3 * channels)], weights.at[num])
            for num in range(3)
        ],
        sems,
    )
    value = jnp.concatenate([grad[:rows, :], grad[rows:, :]], axis=1).astype(F32)
    column_shifts(value, side, shifted)
    total = jnp.zeros((rows, channels), F32)
    for a in range(3):
        for b in range(3):
            put_row_shift(patch, 0, b * channels, shifted, 2 - b, 2 - a, side)
        made[a].wait()
        for b in range(3):
            total = total + dot_last(
                patch[:, b * channels : (b + 1) * channels],
                weights[a, b * channels : (b + 1) * channels, :],
            )
    if layer == 0:
        total = total + factor[...]
        left, right = total[:, :half], total[:, half:]
        own_out[...] = jnp.where(pick[0] == 0, left, right)
        send_out[...] = jnp.where(pick[0] == 0, right, left).astype(BF16)
    else:
        low = (total * factor[...]).astype(BF16)
        grad_out[:rows, :] = low[:, :half]
        grad_out[rows:, :] = low[:, half:]


def back(layer, grad, trunk_weight, factor, pick=None):
    side = SIDE
    rows = rows_of(side)
    channels = trunk_weight.shape[2]
    half = channels // 2
    vmem = spec(pltpu.VMEM)
    in_specs = [vmem, spec(pl.ANY), vmem]
    operands = [grad, trunk_weight, factor]
    if layer == 0:
        in_specs.append(spec(pltpu.SMEM))
        operands.append(pick)
        out_shape = (
            jax.ShapeDtypeStruct((rows, half), F32),
            jax.ShapeDtypeStruct((rows, half), BF16),
        )
        out_specs = (vmem, vmem)
    else:
        out_shape = jax.ShapeDtypeStruct((2 * rows, half), BF16)
        out_specs = vmem
    return pl.pallas_call(
        partial(back_kernel, side, layer),
        out_shape=out_shape,
        in_specs=in_specs,
        out_specs=out_specs,
        scratch_shapes=[
            pltpu.VMEM((3, 3 * channels, channels), BF16),
            pltpu.VMEM((3, rows, channels), F32),
            pltpu.VMEM((rows, 3 * channels), BF16),
            pltpu.SemaphoreType.DMA((3,)),
        ],
        compiler_params=params(),
        name="back",
    )(*operands)


def trunk_grad_kernel(
    side, parts, at_x, at_g, info, own_x, other_x, own_g, other_g, out, xs, gs, shifted, patch, sems
):
    rows = rows_of(side)
    half = xs.shape[1]
    first = at_g + info[0] * rows
    made = copies(
        [
            (own_g.at[pl.ds(first, rows)], gs.at[pl.ds(0, rows)]),
            (other_g.at[pl.ds(first, rows)], gs.at[pl.ds(rows, rows)]),
            (own_x.at[pl.ds(at_x, rows)], xs.at[pl.ds(0, rows)]),
            (other_x.at[pl.ds(at_x, rows)], xs.at[pl.ds(rows, rows)]),
        ],
        sems,
    )
    for image in range(2):
        made[image].wait()
        column_shifts(gs[image * rows : (image + 1) * rows, :].astype(F32), side, shifted)
        for a in range(3):
            for b in range(3):
                put_row_shift(
                    patch, image * rows, (3 * a + b) * half, shifted, 2 - b, 2 - a, side
                )
    made[2].wait()
    made[3].wait()
    turned = xs[...].T
    size = half // parts
    for offset in range(9):
        product = dot(turned, patch[:, offset * half : (offset + 1) * half]).astype(BF16)
        for lane in range(2):
            for part in range(parts):
                place = (lane * parts + part) ^ info[1]
                out[place, offset * size : (offset + 1) * size, :] = product[
                    part * size : (part + 1) * size, lane * (half // 2) : (lane + 1) * (half // 2)
                ]


def trunk_grad(blocks, at_x, at_g, pick, low_bits, own_x, other_x, own_g, other_g):
    side = SIDE
    rows = rows_of(side)
    half = own_x.shape[1]
    parts = blocks // 4
    hbm = spec(pl.ANY)
    return pl.pallas_call(
        partial(trunk_grad_kernel, side, parts, at_x, at_g),
        out_shape=jax.ShapeDtypeStruct((blocks // 2, 9 * (half // parts), half // 2), BF16),
        in_specs=[spec(pltpu.SMEM), hbm, hbm, hbm, hbm],
        out_specs=spec(pltpu.VMEM),
        scratch_shapes=[
            pltpu.VMEM((2 * rows, half), BF16),
            pltpu.VMEM((2 * rows, half), BF16),
            pltpu.VMEM((3, rows, half), F32),
            pltpu.VMEM((2 * rows, 9 * half), BF16),
            pltpu.SemaphoreType.DMA((4,)),
        ],
        compiler_params=params(),
        name="trunk_grad",
    )(jnp.stack([pick, low_bits]), own_x, other_x, own_g, other_g)


def head_grad_kernel(
    side, parts, at_n, at_c, info, own, other, merging, out, ns, cots, sems
):
    mid = (side // 2) ** 2
    stacked = 2 * mid + (side // 4) ** 2
    half = ns.shape[1]
    width = out.shape[2] * 2
    lanes = width // half
    pick = info[0]
    made = copies(
        [
            (source.at[pl.ds(at_c, lanes * mid)], cots.at[num])
            for num, source in enumerate((own, other))
        ]
        + [
            (
                source.at[pl.ds(at_n + pick * stacked, stacked)],
                ns.at[pl.ds(num * stacked, stacked)],
            )
            for num, source in enumerate((own, other))
        ],
        sems,
    )
    weights = merging[pick]
    sums = pool_matrix(side // 2, 1.0)
    grads = []
    for image in range(2):
        made[image].wait()
        cot_low = jnp.concatenate(
            [cots[image, num * mid : (num + 1) * mid, :] for num in range(lanes)], axis=1
        )
        grads.append(head_cotangents(cot_low.astype(F32), dot(sums, cot_low), weights))
    made[2].wait()
    made[3].wait()
    product = dot(ns[...].T, jnp.concatenate(grads, axis=0)).astype(BF16)
    size = half // parts
    for lane in range(2):
        for part in range(parts):
            place = (lane * parts + part) ^ info[1]
            out[place] = product[
                part * size : (part + 1) * size, lane * (width // 2) : (lane + 1) * (width // 2)
            ]


def head_grad(blocks, at_n, at_c, pick, low_bits, own, other, merging, mid):
    side = SIDE
    half = own.shape[1]
    width = merging.shape[2]
    parts = blocks // 4
    hbm = spec(pl.ANY)
    stacked = 2 * mid + (side // 4) ** 2
    return pl.pallas_call(
        partial(head_grad_kernel, side, parts, at_n, at_c),
        out_shape=jax.ShapeDtypeStruct((blocks // 2, half // parts, width // 2), BF16),
        in_specs=[spec(pltpu.SMEM), hbm, hbm, spec(pltpu.VMEM)],
        out_specs=spec(pltpu.VMEM),
        scratch_shapes=[
            pltpu.VMEM((2 * stacked, half), BF16),
            pltpu.VMEM((2, width // half * mid, half), BF16),
            pltpu.SemaphoreType.DMA((4,)),
        ],
        compiler_params=params(),
        name="head_grad",
    )(jnp.stack([pick, low_bits]), own, other, merging)


def widen_trunk_kernel(parts, place, own, other, *rest):
    out = rest[-1]
    size = out.shape[2] // parts

    def write(source, low):
        for part in range(parts):
            start = pl.multiple_of((part ^ low) * size, size)
            for offset in range(9):
                out[0, offset, pl.ds(start, size), :] = source[
                    part, offset * size : (offset + 1) * size, :
                ].astype(F32)

    @pl.when(pl.program_id(0) == 0)
    def _():
        write(own, place[2])

    @pl.when(pl.program_id(0) == 1)
    def _():
        write(other, place[5])


def widen_heads_kernel(parts, place, own, other, out):
    size = out.shape[1] // parts

    def write(source, low):
        for part in range(parts):
            start = pl.multiple_of((part ^ low) * size, size)
            out[0, pl.ds(start, size), :] = source[part].astype(F32)

    @pl.when(pl.program_id(0) == 0)
    def _():
        write(own, place[2])

    @pl.when(pl.program_id(0) == 1)
    def _():
        write(other, place[5])


def source_specs(parts, shape):
    return [
        pl.BlockSpec((parts,) + shape, lambda i, j, place: (jnp.where(i == 0, j, 3), 0, 0)),
        pl.BlockSpec((parts,) + shape, lambda i, j, place: (jnp.where(i == 1, j, 0), 0, 0)),
    ]


def widen_trunk(place, own, other, layer, layers, before):
    parts = own.shape[0] // 4
    lanes = own.shape[2]
    half = 2 * lanes
    operands = [place, own, other]
    in_specs = source_specs(parts, own.shape[1:])
    aliases = {}
    if before is not None:
        operands.append(before)
        in_specs.append(spec(pl.ANY))
        aliases = {3: 0}
    return pl.pallas_call(
        partial(widen_trunk_kernel, parts),
        grid_spec=pltpu.PrefetchScalarGridSpec(
            num_scalar_prefetch=1,
            grid=(2, 4),
            in_specs=in_specs,
            out_specs=pl.BlockSpec(
                (1, 9, half, lanes),
                lambda i, j, place: (layer, 0, place[3 * i], j ^ place[3 * i + 1]),
            ),
        ),
        out_shape=jax.ShapeDtypeStruct((layers, 9, 2 * half, 2 * half), F32),
        input_output_aliases=aliases,
        compiler_params=params(),
        name="widen_trunk",
    )(*operands)


def widen_heads(place, own, other):
    parts = own.shape[0] // 4
    size, lanes = own.shape[1:]
    half = size * parts
    return pl.pallas_call(
        partial(widen_heads_kernel, parts),
        grid_spec=pltpu.PrefetchScalarGridSpec(
            num_scalar_prefetch=1,
            grid=(2, 4),
            in_specs=source_specs(parts, own.shape[1:]),
            out_specs=pl.BlockSpec(
                (1, half, lanes),
                lambda i, j, place: (
                    (j ^ place[3 * i + 1]) // 2,
                    place[3 * i],
                    (j ^ place[3 * i + 1]) % 2,
                ),
            ),
        ),
        out_shape=jax.ShapeDtypeStruct((2, 2 * half, 2 * lanes), F32),
        compiler_params=params(),
        name="widen_heads",
    )(place, own, other)


def stage_bits(dp):
    size = dp.bit_length() - 1
    bits = [1, size] + list(range(2, size))
    stages = []
    for num in range(0, len(bits), 2):
        pair = bits[num : num + 2]
        stages += [tuple(pair), tuple(pair[::-1])] if len(pair) == 2 else [(pair[0], pair[0])]
    return stages


def swap_over(block, devices, bits):
    route = [(i, i ^ (1 << bits[i & 1])) for i in range(devices)]
    return lax.ppermute(block, AXES, route)


def summed(keep, received):
    return (keep.astype(F32) + received.astype(F32)).astype(BF16)


def body(
    features,
    plan,
    trunk_weight,
    trunk_gain,
    trunk_shift,
    head_weight,
    norm_scale,
    merging_weight,
    merged_cotangent,
):
    dp = lax.axis_size("dp")
    devices = lax.axis_size("pipe") * dp
    layers = trunk_weight.shape[0]
    channels = features.shape[2]
    rows = features.shape[1]
    half = channels // 2
    mid = merged_cotangent.shape[1]
    width = head_weight.shape[2]
    pipe = lax.axis_index("pipe")
    index = pipe * dp + lax.axis_index("dp")
    core = index & 1
    stages = stage_bits(dp)
    blocks = 1 << len(stages)

    def bits_of(which):
        total = 0
        for stage in stages:
            total = total * 2 + ((index >> stage[which]) & 1)
        return total

    own_bits = jnp.where(core == 0, bits_of(0), bits_of(1))
    other_bits = jnp.where(core == 0, bits_of(1), bits_of(0))
    top_bit = own_bits // (blocks // 2)
    low_bits = own_bits % (blocks // 2)
    parts = blocks // 4
    place = jnp.stack(
        [core, own_bits // parts, own_bits % parts, 1 - core, other_bits // parts, other_bits % parts]
    )
    weights = trunk_weight.reshape(layers, 9 * channels, channels)
    slot = plan[0, pipe]

    own, send, slope, tap_grad, merged, small = section(
        jnp.stack([slot, core, pipe]),
        features,
        weights,
        head_weight,
        merged_cotangent,
        trunk_gain,
        trunk_shift,
        norm_scale,
        merging_weight,
    )
    other = swap_over(send, devices, (0, 0))
    at_n = 2 * rows
    stacked = 2 * mid + (SIDE // 4) ** 2
    at_g = at_n + 2 * stacked
    at_c = at_g + 2 * rows

    def first_stage(make):
        return make(1 - top_bit), make(top_bit)

    def scatter(send, keep):
        received = swap_over(send, devices, stages[0])
        for stage in stages[1:]:
            count = keep.shape[0] // 2
            total = summed(keep, received)
            keep = total[:count]
            received = swap_over(total[count:], devices, stage)
        return summed(keep, received)

    def gather(block):
        for stage in reversed(stages):
            block = jnp.concatenate([block, swap_over(block, devices, stage)], axis=0)
        return block, swap_over(block, devices, (0, 0))

    head_parts = first_stage(
        lambda pick: head_grad(
            blocks, at_n, at_c, pick, low_bits, own, other, merging_weight, mid
        )
    )
    last_parts = first_stage(
        lambda pick: trunk_grad(blocks, rows, at_g, pick, low_bits, own, other, own, other)
    )
    grad1 = back(1, lax.slice_in_dim(own, at_g, at_g + 2 * rows), weights, slope)
    other_grad1 = swap_over(grad1, devices, (0, 0))
    first_parts = first_stage(
        lambda pick: trunk_grad(blocks, 0, 0, pick, low_bits, own, other, grad1, other_grad1)
    )
    own_feed, sent_feed = back(0, grad1, weights, tap_grad, pipe[None])

    heads = gather(scatter(*head_parts))
    last = gather(scatter(*last_parts))
    first = gather(scatter(*first_parts))

    small_all = lax.all_gather(small, AXES, axis=0, tiled=False)
    small_sum = jnp.sum(small_all, axis=0)

    trunk_out = widen_trunk(place, *last, 1, layers, None)
    trunk_out = widen_trunk(place, *first, 0, layers, trunk_out)
    head_out = widen_heads(place, *heads)

    over_pipe = [(0, 1), (1, 0)]
    left, right = merged[:, : width // 2], merged[:, width // 2 :]
    own_merged = jnp.where(pipe == 0, left, right)
    other_merged = lax.ppermute(jnp.where(pipe == 0, right, left), "pipe", over_pipe)
    other_feed = lax.ppermute(sent_feed, "pipe", over_pipe).astype(F32)

    def in_order(is_first, one, two):
        return jnp.where(is_first, jnp.stack([one, two]), jnp.stack([two, one]))

    return (
        in_order(pipe == 0, own_merged, other_merged),
        in_order(slot == 0, own_feed, other_feed),
        trunk_out.reshape(trunk_weight.shape),
        head_out,
        small_sum[6, : 2 * channels].reshape(2, channels),
        small_sum[:6].reshape(2, 3, width),
    )


def solution(mesh):
    placed = (P("dp", None, None), P("dp", None), P(), P(), P(), P(), P(), P(), P("dp", None, None))
    return jax.shard_map(
        body,
        mesh=mesh,
        in_specs=placed,
        out_specs=(P("dp", None, "pipe"), P("dp", None, "pipe"), P(), P(), P(), P()),
        check_vma=False,
    )
```

```python
from functools import partial

import jax
import jax.numpy as jnp
from jax import lax
from jax.experimental import pallas as pl
from jax.experimental.pallas import tpu as pltpu
from jax.sharding import PartitionSpec as P

SIDE = 16
EPSILON = 1e-06
F32 = jnp.float32
BF16 = jnp.bfloat16
AXES = ("pipe", "dp")
MIB = 1024 * 1024


def device_index(dp):
    return lax.axis_index("pipe") * dp + lax.axis_index("dp")


HEAD, LATE, EARLY = 0, 1, 2


def stage_bits(dp, piece):
    size = dp.bit_length() - 1
    one, two, three, four = 1, size, 2, 3
    if piece == HEAD:
        stages = [(two, three), (one, two), (three, one), (four, four)]
    elif piece == LATE:
        stages = [(one, two), (two, one), (three, three), (four, four)]
    else:
        stages = [(three, one), (one, two), (two, three), (four, four)]
    return stages + [(bit, bit) for bit in range(4, size)]


def block_bits(dp, core, piece):
    index = device_index(dp)
    return [
        jnp.where(core == 0, (index >> first) & 1, (index >> second) & 1)
        for first, second in stage_bits(dp, piece)[:3]
    ]


def own_core(dp):
    return device_index(dp) & 1


class Layout:
    def __init__(self, side, channels, width):
        rows = rows_of(side)
        self.rows = rows
        self.mid = (side // 2) ** 2
        self.stacked = 2 * self.mid + (side // 4) ** 2
        self.lanes = width // (channels // 2)
        self.act = rows
        self.skip = rows
        self.span = 2 * rows
        self.grad = (0, self.span)
        self.normed = self.span + rows
        self.cot = self.normed + 2 * self.stacked
        self.small = self.cot + self.lanes * self.mid
        self.feed = self.small + 16 * self.lanes
        self.total = self.feed + rows


def spec(memory):
    return pl.BlockSpec(memory_space=memory)


def call(
    kernel, name, mib, cost, operands, in_specs, out_shape, out_specs, scratch=(), after=(), aliases=None
):
    count = len(operands)
    extra = len(after)

    def run(*refs):
        kernel(*refs[:count], *refs[count + extra :])

    return pl.pallas_call(
        run,
        out_shape=out_shape,
        in_specs=list(in_specs) + [spec(pl.ANY)] * extra,
        out_specs=out_specs,
        scratch_shapes=list(scratch),
        input_output_aliases=aliases or {},
        compiler_params=pltpu.CompilerParams(vmem_limit_bytes=mib * MIB),
        cost_estimate=pl.CostEstimate(flops=cost, bytes_accessed=1024, transcendentals=0),
        name=name,
    )(*operands, *after)


def grids(side):
    first = 0
    found = []
    for extent in (side, side // 2, side // 4):
        found.append((first, extent))
        first += extent * extent
    return found


def rows_of(side):
    return side * side + (side // 2) ** 2 + (side // 4) ** 2


def iota(shape, dim):
    return lax.broadcasted_iota(jnp.int32, shape, dim)


def edge_masks(side):
    row = iota((rows_of(side), 1), 0)
    first = jnp.zeros(row.shape, jnp.bool_)
    last = jnp.zeros(row.shape, jnp.bool_)
    for start, extent in grids(side):
        inside = (row >= start) & (row < start + extent * extent)
        column = (row - start) & (extent - 1)
        first = first | (inside & (column == 0))
        last = last | (inside & (column == extent - 1))
    return first, last


def column_shifts(value, side, target):
    first, last = edge_masks(side)
    rows = value.shape[0]
    target[0] = jnp.where(first, 0.0, pltpu.roll(value, 1, 0))
    target[1] = value
    target[2] = jnp.where(last, 0.0, pltpu.roll(value, rows - 1, 0))


def row_shift(shifted, b, a, side):
    parts = []
    width = shifted.shape[2]
    for start, extent in grids(side):
        count = extent * extent
        if a == 1:
            part = shifted[b, start : start + count, :]
        elif extent % 8 == 0:
            blank = jnp.zeros((extent, width), F32)
            if a == 0:
                part = jnp.concatenate([blank, shifted[b, start : start + count - extent, :]], axis=0)
            else:
                part = jnp.concatenate([shifted[b, start + extent : start + count, :], blank], axis=0)
        else:
            whole = shifted[b, start : start + count, :]
            row = iota((count, 1), 0)
            if a == 0:
                part = jnp.where(row < extent, 0.0, pltpu.roll(whole, extent, 0))
            else:
                part = jnp.where(row >= count - extent, 0.0, pltpu.roll(whole, count - extent, 0))
        parts.append(part.astype(BF16))
    return parts


def put_row_shift(target, row_start, lane_start, shifted, b, a, side):
    width = shifted.shape[2]
    for (start, extent), part in zip(grids(side), row_shift(shifted, b, a, side)):
        target[
            row_start + start : row_start + start + extent * extent, lane_start : lane_start + width
        ] = part


def dot(left, right):
    return lax.dot_general(left, right, (((1,), (0,)), ((), ())), preferred_element_type=F32)


def dot_last(left, right):
    return lax.dot_general(left, right, (((1,), (1,)), ((), ())), preferred_element_type=F32)


def block_of(index, extent):
    return (index // extent // 2) * (extent // 2) + (index % extent) // 2


def pool_matrix(extent, value):
    count = extent * extent
    shape = (count // 4, count)
    return jnp.where(block_of(iota(shape, 1), extent) == iota(shape, 0), value, 0.0).astype(BF16)


def spread_matrix(extent):
    count = extent * extent
    shape = (count, count // 4)
    return jnp.where(block_of(iota(shape, 0), extent) == iota(shape, 1), 1.0, 0.0).astype(BF16)


def spread(matrix, value):
    high = value.astype(BF16)
    low = (value - high.astype(F32)).astype(BF16)
    return dot(matrix, high) + dot(matrix, low)


def gelu_and_slope(z):
    root = 0.7978845608028654
    inner = root * (z + 0.044715 * z * z * z)
    t = jnp.tanh(inner)
    half = 0.5 * (1.0 + t)
    slope = half + 0.5 * z * (1.0 - t * t) * (root * (1.0 + 3 * 0.044715 * z * z))
    return z * half, slope


def head_cotangents(cot, coarse_cot, weights):
    return jnp.concatenate(
        [
            (weights[0] * cot).astype(BF16),
            (weights[1] * cot).astype(BF16),
            (weights[2] * coarse_cot).astype(BF16),
        ],
        axis=0,
    )


def copies(pairs, sems):
    made = [
        pltpu.make_async_copy(source, target, sems.at[num])
        for num, (source, target) in enumerate(pairs)
    ]
    for one in made:
        one.start()
    return made


def section_kernel(
    side,
    dp,
    plan,
    features,
    trunk_weight,
    head_weight,
    cotangent,
    gain_in,
    shift_in,
    scale_in,
    merging_in,
    own_out,
    send_out,
    pass_out,
    grad_out,
    slope_out,
    tap_grad_out,
    merged_out,
    feed,
    weights,
    heads,
    cot_ref,
    gain,
    shift,
    scale,
    merging,
    shifted,
    patch,
    sems,
):
    rows = rows_of(side)
    fine = side * side
    channels = feed.shape[1]
    half = channels // 2
    width = heads.shape[2]
    at = Layout(side, channels, width)
    mid = at.mid
    pipe = lax.axis_index("pipe")
    core = own_core(dp)
    pick = block_bits(dp, core, LATE)[0]
    made = copies(
        [(features.at[plan[0, pipe]], feed)]
        + [
            (
                trunk_weight.at[num // 3, pl.ds(num % 3 * 3 * channels, 3 * channels)],
                weights.at[num],
            )
            for num in range(6)
        ]
        + [(cotangent.at[pipe], cot_ref)]
        + [(head_weight.at[num], heads.at[num]) for num in range(2)]
        + [(gain_in, gain), (shift_in, shift), (scale_in, scale), (merging_in, merging)],
        sems,
    )
    made[0].wait()

    def conv(value, layer):
        column_shifts(value, side, shifted)
        total = jnp.zeros((rows, channels), F32)
        for a in range(3):
            for b in range(3):
                put_row_shift(patch, 0, b * channels, shifted, b, a, side)
            made[1 + 3 * layer + a].wait()
            total = total + dot(patch[...], weights[3 * layer + a])
        return total

    def put_halves(first, value):
        count = value.shape[0]
        left = value[:, :half]
        right = value[:, half:]
        own_out[first : first + count, :] = jnp.where(core == 0, left, right)
        send_out[first : first + count, :] = jnp.where(core == 0, right, left)

    low_feed = feed[...]
    feed_value = low_feed.astype(F32)
    put_halves(at.feed, low_feed)
    first_pre = conv(feed_value, 0)
    for num in range(10, 14):
        made[num].wait()
    act1, slope1 = gelu_and_slope(gain[0:1, :] * first_pre + shift[0:1, :])
    slope_out[...] = slope1 * gain[0:1, :]
    low_act = act1.astype(BF16)
    put_halves(at.act, low_act)
    z2 = gain[1:2, :] * conv(low_act.astype(F32), 1) + shift[1:2, :]
    trunk_out, slope2 = gelu_and_slope(z2)
    taps = [feed_value, trunk_out.astype(BF16).astype(F32)]

    made[7].wait()
    cot_low = cot_ref[...]
    cot = cot_low.astype(F32)
    coarse_cot = dot(pool_matrix(side // 2, 1.0), cot_low)
    pool = pool_matrix(side, 0.25)
    wide = spread_matrix(side)
    merged = jnp.zeros((mid, width), F32)
    coarse_merged = jnp.zeros((at.stacked - 2 * mid, width), F32)
    small = []
    scale_rows = []
    for k in range(2):
        tap = taps[k]
        scale_row = scale[k : k + 1, :]
        r = lax.rsqrt(jnp.mean(tap * tap, axis=-1, keepdims=True) + EPSILON)
        normed = (tap * r * scale_row).astype(BF16)
        pooled = dot(pool, normed[:fine]).astype(BF16)
        rows_k = jnp.concatenate([pooled, normed[fine:]], axis=0)
        put_halves(at.normed + k * at.stacked, rows_k)
        made[8 + k].wait()
        product = dot(rows_k, heads[k])
        weights_k = [merging[s, k : k + 1, :] for s in range(3)]
        merged = merged + weights_k[0] * product[:mid] + weights_k[1] * product[mid : 2 * mid]
        coarse_merged = coarse_merged + weights_k[2] * product[2 * mid :]
        small.append(jnp.sum(cot * product[:mid], axis=0, keepdims=True))
        small.append(jnp.sum(cot * product[mid : 2 * mid], axis=0, keepdims=True))
        small.append(jnp.sum(coarse_cot * product[2 * mid :], axis=0, keepdims=True))
        grads = head_cotangents(cot, coarse_cot, weights_k)
        back = dot_last(grads, heads[k])
        back = jnp.concatenate([spread(wide, 0.25 * back[:mid]), back[mid:]], axis=0)
        upstream = back * scale_row
        tap_grad = r * (
            upstream - tap * (r * r) * jnp.mean(upstream * tap, axis=-1, keepdims=True)
        )
        scale_rows.append(jnp.sum(back * tap * r, axis=0, keepdims=True))
        if k == 0:
            tap_grad_out[...] = tap_grad
    small.append(
        jnp.concatenate(scale_rows + [jnp.zeros((1, width - 2 * channels), F32)], axis=1)
    )
    small.append(jnp.zeros((1, width), F32))
    small = jnp.concatenate(small, axis=0)
    merged = merged + spread(spread_matrix(side // 2), coarse_merged)
    merged_out[...] = merged.astype(BF16)
    grad2 = (tap_grad.astype(BF16).astype(F32) * slope2 * gain[1:2, :]).astype(BF16)
    high = small.astype(BF16)
    both = jnp.concatenate([high.astype(F32), small - high.astype(F32)], axis=0).astype(BF16)
    for num in range(2):
        grad_out[num * rows : (num + 1) * rows, :] = grad2[:, num * half : (num + 1) * half]
    for target in (own_out, send_out):
        for num in range(2):
            target[at.grad[num] : at.grad[num] + rows, :] = grad2[:, num * half : (num + 1) * half]
        for num in range(at.lanes):
            lanes = slice(num * half, (num + 1) * half)
            target[at.cot + num * mid : at.cot + (num + 1) * mid, :] = cot_low[:, lanes]
            target[at.small + num * 16 : at.small + (num + 1) * 16, :] = both[:, lanes]
    pass_out[...] = own_out[pl.ds(pl.multiple_of((1 - pick) * at.skip, 16), at.span), :]


def section(dp, plan, features, trunk_weight, head_weight, cotangent, gain, shift, scale, merging):
    side = SIDE
    rows = rows_of(side)
    channels = features.shape[2]
    half = channels // 2
    width = head_weight.shape[2]
    mid = cotangent.shape[1]
    at = Layout(side, channels, width)
    vmem = spec(pltpu.VMEM)
    return call(
        partial(section_kernel, side, dp),
        "section",
        60,
        4200000000,
        (plan, features, trunk_weight, head_weight, cotangent, gain, shift, scale, merging),
        [spec(pltpu.SMEM)] + [spec(pl.ANY)] * 8,
        (
            jax.ShapeDtypeStruct((at.total, half), BF16),
            jax.ShapeDtypeStruct((at.total, half), BF16),
            jax.ShapeDtypeStruct((at.span, half), BF16),
            jax.ShapeDtypeStruct((2 * rows, half), BF16),
            jax.ShapeDtypeStruct((rows, channels), F32),
            jax.ShapeDtypeStruct((rows, channels), F32),
            jax.ShapeDtypeStruct((mid, width), BF16),
        ),
        (vmem,) * 7,
        [
            pltpu.VMEM((rows, channels), BF16),
            pltpu.VMEM((6, 3 * channels, channels), BF16),
            pltpu.VMEM((2, channels, width), BF16),
            pltpu.VMEM((mid, width), BF16),
            pltpu.VMEM(gain.shape, F32),
            pltpu.VMEM(shift.shape, F32),
            pltpu.VMEM(scale.shape, F32),
            pltpu.VMEM(merging.shape, F32),
            pltpu.VMEM((3, rows, channels), F32),
            pltpu.VMEM((rows, 3 * channels), BF16),
            pltpu.SemaphoreType.DMA((14,)),
        ],
    )


def back_kernel(side, layer, grad, trunk_weight, factor, *rest):
    if layer == 0:
        merged, own_out, send_out, weights, shifted, patch, sems = rest
    else:
        grad_out, weights, shifted, patch, sems = rest
    channels = trunk_weight.shape[2]
    half = channels // 2
    rows = rows_of(side)
    made = copies(
        [
            (trunk_weight.at[layer, pl.ds(num * 3 * channels, 3 * channels)], weights.at[num])
            for num in range(3)
        ],
        sems,
    )
    value = jnp.concatenate([grad[:rows, :], grad[rows:, :]], axis=1).astype(F32)
    column_shifts(value, side, shifted)
    total = jnp.zeros((rows, channels), F32)
    for a in range(3):
        for b in range(3):
            put_row_shift(patch, 0, b * channels, shifted, 2 - b, 2 - a, side)
        made[a].wait()
        for b in range(3):
            total = total + dot_last(
                patch[:, b * channels : (b + 1) * channels],
                weights[a, b * channels : (b + 1) * channels, :],
            )
    if layer == 1:
        low = (total * factor[...]).astype(BF16)
        grad_out[:rows, :] = low[:, :half]
        grad_out[rows:, :] = low[:, half:]
        return
    pipe = lax.axis_index("pipe")
    total = total + factor[...]
    left, right = total[:, :half], total[:, half:]
    own_out[...] = jnp.where(pipe == 0, left, right)
    sent = jnp.where(pipe == 0, right, left).astype(BF16)
    low_merged = merged[...]
    mid, width = low_merged.shape
    sent_merged = jnp.where(
        pipe == 0, low_merged[:, width // 2 :], low_merged[:, : width // 2]
    )
    for num in range(half // 128):
        send_out[num * rows : (num + 1) * rows, :] = sent[:, num * 128 : (num + 1) * 128]
    first = half // 128 * rows
    for num in range(width // 256):
        send_out[first + num * mid : first + (num + 1) * mid, :] = sent_merged[
            :, num * 128 : (num + 1) * 128
        ]


def back(layer, grad, trunk_weight, factor, merged=None, after=()):
    side = SIDE
    rows = rows_of(side)
    channels = trunk_weight.shape[2]
    half = channels // 2
    vmem = spec(pltpu.VMEM)
    in_specs = [vmem, spec(pl.ANY), vmem]
    operands = [grad, trunk_weight, factor]
    if layer == 0:
        in_specs.append(vmem)
        operands.append(merged)
        out_shape = (
            jax.ShapeDtypeStruct((rows, half), F32),
            jax.ShapeDtypeStruct((half // 128 * rows + merged.size // 256, 128), BF16),
        )
        out_specs = (vmem, vmem)
    else:
        out_shape = jax.ShapeDtypeStruct((2 * rows, half), BF16)
        out_specs = vmem
    return call(
        partial(back_kernel, side, layer),
        "back",
        46,
        1500000000,
        operands,
        in_specs,
        out_shape,
        out_specs,
        [
            pltpu.VMEM((3, 3 * channels, channels), BF16),
            pltpu.VMEM((3, rows, channels), F32),
            pltpu.VMEM((rows, 3 * channels), BF16),
            pltpu.SemaphoreType.DMA((3,)),
        ],
        after,
    )


def through(pairs, held, sems):
    coming = [
        pltpu.make_async_copy(source, slot, sems.at[num])
        for num, (source, slot, target) in enumerate(pairs)
    ]
    going = [
        pltpu.make_async_copy(slot, target, sems.at[len(pairs) + num])
        for num, (source, slot, target) in enumerate(pairs)
    ]
    for one in coming:
        one.start()
    for one, two in zip(coming, going):
        one.wait()
        two.start()
    for two in going:
        two.wait()


def move_kernel(moves, *refs):
    sources, out, held, sems = refs[:-3], refs[-3], refs[-2], refs[-1]
    through(
        [
            (sources[num].at[first()], held.at[pl.ds(place, count)], out.at[pl.ds(place, count)])
            for num, first, place, count in moves
        ],
        held,
        sems,
    )


def far_factors(dp, other, side, width, after):
    half = other.shape[1]
    at = Layout(side, 2 * half, width)

    def rows():
        pick = block_bits(dp, own_core(dp), LATE)[0]
        return pl.ds(pl.multiple_of((1 - pick) * at.skip, 16), at.span)

    return call(
        partial(move_kernel, [(0, rows, 0, at.span)]),
        "far_factors",
        4,
        120000000,
        (other,),
        [spec(pl.ANY)],
        jax.ShapeDtypeStruct((at.span, half), BF16),
        spec(pl.ANY),
        [pltpu.VMEM((at.span, half), BF16), pltpu.SemaphoreType.DMA((2,))],
        after,
    )


def first_factors(dp, own, other, own_grad, other_grad, side, width, after):
    half = other.shape[1]
    at = Layout(side, 2 * half, width)

    def feed():
        return pl.ds(at.feed, at.rows)

    def grad():
        pick = block_bits(dp, own_core(dp), EARLY)[0]
        return pl.ds(pl.multiple_of((1 - pick) * at.rows, 16), at.rows)

    return call(
        partial(
            move_kernel,
            [
                (num, (feed, feed, grad, grad)[num], num * at.rows, at.rows)
                for num in range(4)
            ],
        ),
        "first_factors",
        4,
        540000000,
        (own, other, own_grad, other_grad),
        [spec(pl.ANY)] * 4,
        jax.ShapeDtypeStruct((4 * at.rows, half), BF16),
        spec(pl.ANY),
        [pltpu.VMEM((4 * at.rows, half), BF16), pltpu.SemaphoreType.DMA((8,))],
        after,
    )


def put_trunk_blocks(dp, piece, send, keep, xs, gs, shifted, patch, side, wait_x, wait_g):
    rows = rows_of(side)
    half = xs.shape[1]
    quarter = half // 2
    _, second, third = block_bits(dp, own_core(dp), piece)
    for image in range(4):
        wait_g(image)
        column_shifts(gs[image * rows : (image + 1) * rows, :].astype(F32), side, shifted)
        for a in range(3):
            for b in range(3):
                put_row_shift(
                    patch, image * rows, (3 * a + b) * half, shifted, 2 - b, 2 - a, side
                )
    for image in range(4):
        wait_x(image)
    turned = xs[...].T
    for offset in range(9):
        product = dot(turned, patch[:, offset * half : (offset + 1) * half]).astype(BF16)
        left, right = product[:, :128], product[:, 128:]
        for target, value in (
            (keep, jnp.where(second == 0, left, right)),
            (send, jnp.where(second == 0, right, left)),
        ):
            upper, lower = value[:quarter], value[quarter:]
            row = offset * quarter
            target[row : row + quarter, :] = jnp.where(third == 0, upper, lower)
            row += 9 * quarter
            target[row : row + quarter, :] = jnp.where(third == 0, lower, upper)


def late_grads_kernel(
    side, dp, width, own, other, near, far, send, keep, xs, gs, shifted, patch, sems
):
    half = xs.shape[1]
    at = Layout(side, 2 * half, width)
    rows = at.rows
    pick = block_bits(dp, own_core(dp), LATE)[0]
    grad_at = pick * at.grad[1]
    pairs = []
    for num, source in enumerate((own, other, near, far)):
        back_by = 0 if num < 2 else pick * at.skip

        def some(first):
            return source.at[pl.ds(pl.multiple_of(first - back_by, 16), rows)]

        pairs += [
            (some(grad_at), gs.at[pl.ds(num * rows, rows)]),
            (some(at.act), xs.at[pl.ds(num * rows, rows)]),
        ]
    made = copies(pairs, sems)
    put_trunk_blocks(
        dp,
        LATE,
        send,
        keep,
        xs,
        gs,
        shifted,
        patch,
        side,
        lambda image: made[2 * image + 1].wait(),
        lambda image: made[2 * image].wait(),
    )


def split_pair(value):
    high = value.astype(BF16).astype(F32)
    return jnp.concatenate([high, value - high], axis=0).astype(BF16)


def trunk_scratch(rows, half):
    return [
        pltpu.VMEM((3, rows, half), F32),
        pltpu.VMEM((4 * rows, 9 * half), BF16),
    ]


def late_grads(dp, width, own, other, near, far, after):
    side = SIDE
    rows = rows_of(side)
    half = own.shape[1]
    vmem = spec(pltpu.VMEM)
    shape = jax.ShapeDtypeStruct((9 * half, 128), BF16)
    return call(
        partial(late_grads_kernel, side, dp, width),
        "late_grads",
        28,
        1440000000,
        (own, other, near, far),
        [spec(pl.ANY)] * 4,
        (shape, shape),
        (vmem, vmem),
        [
            pltpu.VMEM((4 * rows, half), BF16),
            pltpu.VMEM((4 * rows, half), BF16),
            *trunk_scratch(rows, half),
            pltpu.SemaphoreType.DMA((8,)),
        ],
        after,
    )


def early_grads_kernel(
    side, dp, width, own, other, own_g, other_g, far, send, keep, xs, gs, shifted, patch, sems
):
    half = xs.shape[1]
    at = Layout(side, 2 * half, width)
    rows = at.rows
    pick = block_bits(dp, own_core(dp), EARLY)[0]
    mine = pl.ds(pl.multiple_of(pick * rows, 16), rows)
    made = copies(
        [
            (own_g.at[mine], gs.at[pl.ds(0, rows)]),
            (other_g.at[mine], gs.at[pl.ds(rows, rows)]),
            (far.at[pl.ds(2 * rows, 2 * rows)], gs.at[pl.ds(2 * rows, 2 * rows)]),
            (own.at[pl.ds(at.feed, rows)], xs.at[pl.ds(0, rows)]),
            (other.at[pl.ds(at.feed, rows)], xs.at[pl.ds(rows, rows)]),
            (far.at[pl.ds(0, 2 * rows)], xs.at[pl.ds(2 * rows, 2 * rows)]),
        ],
        sems,
    )
    put_trunk_blocks(
        dp,
        EARLY,
        send,
        keep,
        xs,
        gs,
        shifted,
        patch,
        side,
        lambda image: made[3 + image].wait() if image < 3 else None,
        lambda image: made[image].wait() if image < 3 else None,
    )


def early_grads(dp, width, own, other, own_g, other_g, far, after):
    side = SIDE
    rows = rows_of(side)
    half = own.shape[1]
    vmem = spec(pltpu.VMEM)
    shape = jax.ShapeDtypeStruct((9 * half, 128), BF16)
    return call(
        partial(early_grads_kernel, side, dp, width),
        "early_grads",
        28,
        1140000000,
        (own, other, own_g, other_g, far),
        [spec(pl.ANY)] * 5,
        (shape, shape),
        (vmem, vmem),
        [
            pltpu.VMEM((4 * rows, half), BF16),
            pltpu.VMEM((4 * rows, half), BF16),
            *trunk_scratch(rows, half),
            pltpu.SemaphoreType.DMA((6,)),
        ],
        after,
    )


def head_grads_kernel(
    side, dp, is_own, own, other, merging_in, out, ns, cots, smalls, merging, sems
):
    half = ns.shape[1]
    width = merging.shape[2]
    at = Layout(side, 2 * half, width)
    mid = at.mid
    pick, second, third = block_bits(dp, own_core(dp), HEAD)
    tap = pick if is_own else 1 - pick
    first = pl.multiple_of(at.normed + tap * at.stacked, 16)
    pairs = [(merging_in, merging)]
    for num, source in enumerate((own, other)):
        pairs += [
            (source.at[pl.ds(at.cot, at.lanes * mid)], cots.at[num]),
            (source.at[pl.ds(first, at.stacked)], ns.at[pl.ds(num * at.stacked, at.stacked)]),
            (source.at[pl.ds(at.small, at.lanes * 16)], smalls.at[num]),
        ]
    made = copies(pairs, sems)
    made[0].wait()
    weights = [merging[s, pl.ds(tap, 1), :] for s in range(3)]
    sums = pool_matrix(side // 2, 1.0)
    grads = []
    for image in range(2):
        made[1 + 3 * image].wait()
        cot_low = jnp.concatenate(
            [cots[image, num * mid : (num + 1) * mid, :] for num in range(at.lanes)], axis=1
        )
        grads.append(head_cotangents(cot_low.astype(F32), dot(sums, cot_low), weights))
    made[2].wait()
    made[5].wait()
    product = dot(ns[...].T, jnp.concatenate(grads, axis=0)).astype(BF16)
    quarter = half // 2
    for lane in range(2):
        for num in range(width // 256):
            column = lane * (width // 2) + num * 128
            for part in range(2):
                row = pl.multiple_of(
                    (((lane ^ second) * 2 + (part ^ third)) * (width // 256) + num) * quarter,
                    quarter,
                )
                out[pl.ds(row, quarter), :] = product[
                    part * quarter : (part + 1) * quarter, column : column + 128
                ]
    made[3].wait()
    made[6].wait()
    total = smalls[0].astype(F32) + smalls[1].astype(F32)
    first = width // 128 * half
    for num in range(at.lanes):
        pair = split_pair(total[num * 16 : num * 16 + 8] + total[num * 16 + 8 : num * 16 + 16])
        for lane in range(half // 128):
            row = first + (num * (half // 128) + lane) * 16
            out[row : row + 16, :] = pair[:, lane * 128 : (lane + 1) * 128]


def head_grads(dp, is_own, own, other, merging, after):
    side = SIDE
    half = own.shape[1]
    width = merging.shape[2]
    at = Layout(side, 2 * half, width)
    return call(
        partial(head_grads_kernel, side, dp, is_own),
        "head_grads",
        16,
        570000000,
        (own, other, merging),
        [spec(pl.ANY)] * 3,
        jax.ShapeDtypeStruct((width // 128 * half + 16 * width // 128, 128), BF16),
        spec(pltpu.VMEM),
        [
            pltpu.VMEM((2 * at.stacked, half), BF16),
            pltpu.VMEM((2, at.lanes * at.mid, half), BF16),
            pltpu.VMEM((2, at.lanes * 16, half), BF16),
            pltpu.VMEM(merging.shape, F32),
            pltpu.SemaphoreType.DMA((7,)),
        ],
        after,
    )


def add_tails(one, two):
    count = one.shape[0] // 16
    one = one.astype(F32).reshape(count, 16, 128)
    two = two.astype(F32).reshape(count, 16, 128)
    total = (one[:, :8] + one[:, 8:]) + (two[:, :8] + two[:, 8:])
    high = total.astype(BF16).astype(F32)
    return jnp.concatenate([high, total - high], axis=1).reshape(count * 16, 128).astype(BF16)


def sum_kernel(tail, keep, received, *outs):
    rows = keep.shape[0] - tail
    size = rows // len(outs)
    for num, out in enumerate(outs):
        part = slice(num * size, (num + 1) * size)
        out[:size, :] = (keep[part, :].astype(F32) + received[part, :].astype(F32)).astype(BF16)
    if tail:
        total = add_tails(keep[rows:, :], received[rows:, :])
        for out in outs:
            out[size:, :] = total


def summed(keep, received, parts, tail, after):
    vmem = spec(pltpu.VMEM)
    shape = jax.ShapeDtypeStruct(((keep.shape[0] - tail) // parts + tail, 128), BF16)
    return call(
        partial(sum_kernel, tail),
        "summed",
        4,
        1024,
        (keep, received),
        [vmem, vmem],
        (shape,) * parts,
        (vmem,) * parts,
        (),
        after,
    )


def pair_kernel(one, two, out):
    rows = out.shape[0] // 2
    out[:rows, :] = one[:rows, :]
    out[rows:, :] = two[:rows, :]


def paired(one, two, rows, after):
    vmem = spec(pltpu.VMEM)
    return call(
        pair_kernel,
        "paired",
        4,
        1024,
        (one, two),
        [vmem, vmem],
        jax.ShapeDtypeStruct((2 * rows, 128), BF16),
        vmem,
        (),
        after,
    )


def widen_trunk_kernel(dp, layer, half, kinds, *refs):
    sources = refs[: len(kinds)]
    out, done, held, wide, sems_in, sems_out = refs[-6:]
    done[...] = jnp.zeros(done.shape, F32)
    quarter = half // 2
    size = 9 * quarter
    jobs = []
    coming = []
    for source, (is_other, is_new) in zip(sources, kinds):
        core = own_core(dp) ^ int(is_other)
        first, second, third = block_bits(dp, core, LATE if layer else EARLY)
        first = first ^ int(is_new)
        for part in range(2):
            for lane in range(2):
                row = pl.multiple_of(((lane ^ second) * 2 + part) * size, size)
                coming.append((source.at[pl.ds(row, size)], held.at[len(jobs), lane]))
            jobs.append((core * half + (part ^ third) * quarter, first * half))
    made = copies(coming, sems_in)
    going = []
    for num, (row, column) in enumerate(jobs):
        for lane in range(2):
            made[2 * num + lane].wait()
            for offset in range(9):
                wide[num, offset, :, lane * 128 : (lane + 1) * 128] = held[
                    num, lane, offset * quarter : (offset + 1) * quarter, :
                ].astype(F32)
        one = pltpu.make_async_copy(
            wide.at[num],
            out.at[
                layer,
                :,
                pl.ds(pl.multiple_of(row, quarter), quarter),
                pl.ds(pl.multiple_of(column, half), half),
            ],
            sems_out.at[num],
        )
        one.start()
        going.append(one)
    for one in going:
        one.wait()


def widen_trunk(dp, layer, layers, half, sources, kinds, before=None, after=()):
    hbm = spec(pl.ANY)
    operands = list(sources) + ([before] if before is not None else [])
    count = 2 * len(kinds)
    return call(
        partial(widen_trunk_kernel, dp, layer, half, kinds),
        "widen_trunk",
        24,
        870000000,
        operands,
        [hbm] * len(operands),
        (
            jax.ShapeDtypeStruct((layers, 9, 2 * half, 2 * half), F32),
            jax.ShapeDtypeStruct((8, 128), F32),
        ),
        (hbm, spec(pltpu.VMEM)),
        [
            pltpu.VMEM((count, 2, 9 * half // 2, 128), BF16),
            pltpu.VMEM((count, 9, half // 2, half), F32),
            pltpu.SemaphoreType.DMA((2 * count,)),
            pltpu.SemaphoreType.DMA((count,)),
        ],
        after,
        {len(sources): 0} if before is not None else None,
    )


def widen_heads_kernel(dp, half, kinds, *refs):
    sources = refs[: len(kinds)]
    out, done, held, wide, sems_in, sems_out = refs[-6:]
    done[...] = jnp.zeros(done.shape, F32)
    quarter = half // 2
    size = held.shape[2]
    width = wide.shape[2]
    jobs = []
    coming = []
    for source, (is_other, is_new) in zip(sources, kinds):
        core = own_core(dp) ^ int(is_other)
        first, second, third = block_bits(dp, core, HEAD)
        for lane in range(2):
            for part in range(2):
                row = pl.multiple_of(((lane ^ second) * 2 + (part ^ third)) * size, size)
                coming.append((source.at[pl.ds(row, size)], held.at[len(jobs), part]))
            jobs.append((first ^ int(is_new), core * half, lane * width))
    made = copies(coming, sems_in)
    going = []
    for num, (tap, row, column) in enumerate(jobs):
        for part in range(2):
            made[2 * num + part].wait()
            for piece in range(width // 128):
                wide[
                    num, part * quarter : (part + 1) * quarter, piece * 128 : (piece + 1) * 128
                ] = held[num, part, piece * quarter : (piece + 1) * quarter, :].astype(F32)
        one = pltpu.make_async_copy(
            wide.at[num],
            out.at[tap, pl.ds(pl.multiple_of(row, half), half), pl.ds(column, width)],
            sems_out.at[num],
        )
        one.start()
        going.append(one)
    for one in going:
        one.wait()


def widen_heads(dp, half, width, sources, kinds, before=None, after=()):
    hbm = spec(pl.ANY)
    operands = list(sources) + ([before] if before is not None else [])
    count = 2 * len(kinds)
    return call(
        partial(widen_heads_kernel, dp, half, kinds),
        "widen_heads",
        40,
        1320000000,
        operands,
        [hbm] * len(operands),
        (
            jax.ShapeDtypeStruct((2, 2 * half, width), F32),
            jax.ShapeDtypeStruct((8, 128), F32),
        ),
        (hbm, spec(pltpu.VMEM)),
        [
            pltpu.VMEM((count, 2, width // 256 * half // 2, 128), BF16),
            pltpu.VMEM((count, half, width // 2), F32),
            pltpu.SemaphoreType.DMA((2 * count,)),
            pltpu.SemaphoreType.DMA((count,)),
        ],
        after,
        {len(sources): 0} if before is not None else None,
    )


def finish_kernel(
    dp, at, plan, own_feed, merged, received, own_sum, other_sum,
    merged_out, feed_out, scale_out, merging_out, held, sems,
):
    tail = pl.ds(at, held.shape[1])
    made = copies([(own_sum.at[tail], held.at[0]), (other_sum.at[tail], held.at[1])], sems)
    pipe = lax.axis_index("pipe")
    rows, half = own_feed.shape
    mid, width = merged.shape
    slot = plan[0, pipe]
    feed_out[slot] = own_feed[...]
    for num in range(half // 128):
        feed_out[1 - slot, :, num * 128 : (num + 1) * 128] = received[
            num * rows : (num + 1) * rows, :
        ].astype(F32)
    low_merged = merged[...]
    merged_out[pipe] = jnp.where(
        pipe == 0, low_merged[:, : width // 2], low_merged[:, width // 2 :]
    )
    first = half // 128 * rows
    for num in range(width // 256):
        merged_out[1 - pipe, :, num * 128 : (num + 1) * 128] = received[
            first + num * mid : first + (num + 1) * mid, :
        ]
    for one in made:
        one.wait()
    low = jnp.where(own_core(dp) == 0, held[0], held[1]).astype(F32)
    for num in range(width // 128):
        lanes = slice(num * 128, (num + 1) * 128)
        block = low[num * 16 : num * 16 + 8] + low[num * 16 + 8 : num * 16 + 16]
        for k in range(2):
            for s in range(3):
                merging_out[s, k : k + 1, lanes] = block[3 * k + s : 3 * k + s + 1]
        for k in range(2):
            column = num * 128 - k * 2 * half
            if 0 <= column < 2 * half:
                scale_out[k : k + 1, column : column + 128] = block[6:7]


def finish(dp, plan, own_feed, merged, received, own_sum, other_sum, after):
    rows, half = own_feed.shape
    mid, width = merged.shape
    vmem = spec(pltpu.VMEM)
    tail = 16 * width // 128
    return call(
        partial(finish_kernel, dp, own_sum.shape[0] - tail),
        "finish",
        8,
        510000000,
        (plan, own_feed, merged, received, own_sum, other_sum),
        [spec(pltpu.SMEM), vmem, vmem, vmem, spec(pl.ANY), spec(pl.ANY)],
        (
            jax.ShapeDtypeStruct((2, mid, width // 2), BF16),
            jax.ShapeDtypeStruct((2, rows, half), F32),
            jax.ShapeDtypeStruct((2, 2 * half), F32),
            jax.ShapeDtypeStruct((3, 2, width), F32),
        ),
        (vmem,) * 4,
        [pltpu.VMEM((2, tail, 128), BF16), pltpu.SemaphoreType.DMA((2,))],
        after,
    )


class Sum:
    def __init__(self, swap, piece, last, send, keep, tail=0):
        self.swap = partial(swap, piece)
        self.tail = tail
        self.steps = [("scatter", stage) for stage in range(0 if piece == HEAD else 1, 3)]
        self.steps += [("whole", stage) for stage in range(3, last + 1)]
        self.steps += [("gather", stage) for stage in (2, 1, 0)]
        self.at = 0
        self.keep = keep
        self.come = self.swap(self.steps[0][1], send)

    def advance(self, *after):
        kind = self.steps[self.at][0]
        self.at += 1
        following, stage = self.steps[self.at]
        if kind == "gather":
            self.keep = paired(self.keep, self.come, self.keep.shape[0] - self.tail, after)
            self.tail = 0
            send = self.keep
        else:
            parts = 2 if following == "scatter" else 1
            made = summed(self.keep, self.come, parts, self.tail, after)
            self.keep = made[0]
            send = made[-1]
            if following == "gather":
                self.final = self.keep
        self.come = self.swap(stage, send)
        return self.keep


def body(
    features,
    plan,
    trunk_weight,
    trunk_gain,
    trunk_shift,
    head_weight,
    norm_scale,
    merging_weight,
    merged_cotangent,
):
    dp = lax.axis_size("dp")
    devices = lax.axis_size("pipe") * dp
    layers = trunk_weight.shape[0]
    channels = features.shape[2]
    half = channels // 2
    width = head_weight.shape[2]
    last = dp.bit_length() - 2
    weights = trunk_weight.reshape(layers, 9 * channels, channels)
    merging = jnp.transpose(merging_weight, (1, 0, 2))
    tail = 16 * width // 128

    def swap(piece, stage, block):
        bits = stage_bits(dp, piece)[stage]
        route = [(i, i ^ (1 << bits[i & 1])) for i in range(devices)]
        return lax.ppermute(block, AXES, route)

    def swap_cores(block):
        return lax.ppermute(block, AXES, [(i, i ^ 1) for i in range(devices)])

    own, send, passed, grad2, slope, tap_grad, merged = section(
        dp,
        plan,
        features,
        weights,
        head_weight,
        merged_cotangent,
        trunk_gain,
        trunk_shift,
        norm_scale,
        merging,
    )
    other = swap_cores(send)
    near = swap(LATE, 0, passed)
    passed = far_factors(dp, other, SIDE, width, ())
    far = swap(LATE, 0, passed)
    head_send = head_grads(dp, False, own, other, merging, (passed,))
    head_keep = head_grads(dp, True, own, other, merging, (head_send, near))
    head = Sum(swap, HEAD, last, head_send, head_keep, tail)
    grad1 = back(1, grad2, weights, slope, None, (head_keep, far))
    other_grad1 = swap_cores(grad1)
    passed = first_factors(dp, own, other, grad1, other_grad1, SIDE, width, ())
    first_far = swap(EARLY, 0, passed)
    token = head.advance(passed)
    late_blocks = late_grads(dp, width, own, other, near, far, (token,))
    late = Sum(swap, LATE, last, *late_blocks)
    token = head.advance(late.keep)
    early_blocks = early_grads(
        dp, width, own, other, grad1, other_grad1, first_far, (token,)
    )
    early = Sum(swap, EARLY, last, *early_blocks)
    pieces = {"H": head, "L": late, "E": early}

    def advance(order, *tokens):
        for name in order:
            tokens = (pieces[name].advance(*tokens),)
        return tokens[0]

    token = advance("LHELHE" + "LHE" * (last - 3), early.keep)
    own_feed, sent = back(0, grad1, weights, tap_grad, merged, (token,))
    received = lax.ppermute(sent, "pipe", [(0, 1), (1, 0)])
    token = advance("LHELH", own_feed)
    other_head = swap_cores(head.keep)
    other_sum = swap_cores(head.final)
    token = advance("EL", token)
    other_late = swap_cores(late.keep)
    merged_maps, features_grad, scale_grad, merging_grad = finish(
        dp, plan, own_feed, merged, received, head.final, other_sum, (token,)
    )
    token = advance("E", merged_maps)
    other_early = swap_cores(early.keep)
    kept = ((False, False), (True, False))
    came = ((False, True), (True, True))
    head_out, done = widen_heads(dp, half, width, (head.keep, other_head), kept, None, (token,))
    trunk_out, done = widen_trunk(
        dp, 1, layers, half, (late.keep, other_late), kept, None, (done,)
    )
    trunk_out, done = widen_trunk(
        dp, 0, layers, half, (early.keep, other_early), kept, trunk_out, (done, head.come)
    )
    head_out, done = widen_heads(
        dp, half, width, (head.come, swap_cores(head.come)), came, head_out, (done, late.come)
    )
    trunk_out, done = widen_trunk(
        dp, 1, layers, half, (late.come, swap_cores(late.come)), came, trunk_out, (done, early.come)
    )
    other_new = swap_cores(early.come)
    trunk_out, done = widen_trunk(dp, 0, layers, half, (early.come,), came[:1], trunk_out, (done,))
    trunk_out, done = widen_trunk(dp, 0, layers, half, (other_new,), came[1:], trunk_out, (done,))
    return (
        merged_maps,
        features_grad,
        trunk_out.reshape(trunk_weight.shape),
        head_out,
        scale_grad,
        jnp.transpose(merging_grad, (1, 0, 2)),
    )


def solution(mesh):
    placed = (P("dp", None, None), P("dp", None), P(), P(), P(), P(), P(), P(), P("dp", None, None))
    return jax.shard_map(
        body,
        mesh=mesh,
        in_specs=placed,
        out_specs=(P("dp", None, "pipe"), P("dp", None, "pipe"), P(), P(), P(), P()),
        check_vma=False,
    )
```

```python
from functools import partial

import jax
import jax.numpy as jnp
from jax import lax
from jax.experimental import pallas as pl
from jax.experimental.pallas import tpu as pltpu
from jax.sharding import PartitionSpec as P

SIDE = 16
EPSILON = 1e-06
F32 = jnp.float32
BF16 = jnp.bfloat16
AXES = ("pipe", "dp")
MIB = 1024 * 1024


def device_index(dp):
    return lax.axis_index("pipe") * dp + lax.axis_index("dp")


HEAD, LATE, EARLY = 0, 1, 2


def stage_bits(dp, piece):
    size = dp.bit_length() - 1
    one, two, three, four = 1, size, 2, 3
    if piece == HEAD:
        stages = [(two, three), (one, two), (three, one), (four, four)]
    elif piece == LATE:
        stages = [(two, three), (one, two), (three, one), (four, four)]
    else:
        stages = [(one, three), (two, one), (three, two), (four, four)]
    return stages + [(bit, bit) for bit in range(4, size)]


def block_bits(dp, core, piece):
    index = device_index(dp)
    return [
        jnp.where(core == 0, (index >> first) & 1, (index >> second) & 1)
        for first, second in stage_bits(dp, piece)[:3]
    ]


def own_core(dp):
    return device_index(dp) & 1


class Layout:
    def __init__(self, side, channels, width):
        rows = rows_of(side)
        self.rows = rows
        self.mid = (side // 2) ** 2
        self.stacked = 2 * self.mid + (side // 4) ** 2
        self.lanes = width // (channels // 2)
        self.act = rows
        self.skip = rows
        self.span = 2 * rows
        self.grad = (0, self.span)
        self.normed = self.span + rows
        self.cot = self.normed + 2 * self.stacked
        self.feed = self.cot + self.lanes * self.mid
        self.total = self.feed + rows


def spec(memory):
    return pl.BlockSpec(memory_space=memory)


def call(kernel, name, mib, cost, operands, in_specs, out_shape, out_specs, scratch=(), after=(), aliases=None):
    count = len(operands)
    extra = len(after)
    several = isinstance(out_shape, tuple)
    shapes = out_shape if several else (out_shape,)
    specs = out_specs if several else (out_specs,)

    def run(*refs):
        results = refs[count + extra :]
        mark = results[len(shapes)]
        kernel(*refs[:count], *results[: len(shapes)], *results[len(shapes) + 1 :])
        mark[...] = jnp.zeros(mark.shape, F32)

    *made, mark = pl.pallas_call(
        run,
        out_shape=(*shapes, jax.ShapeDtypeStruct((8, 128), F32)),
        in_specs=list(in_specs) + [spec(pl.ANY)] * extra,
        out_specs=(*specs, spec(pltpu.VMEM)),
        scratch_shapes=list(scratch),
        input_output_aliases=aliases or {},
        compiler_params=pltpu.CompilerParams(vmem_limit_bytes=mib * MIB),
        cost_estimate=pl.CostEstimate(flops=cost, bytes_accessed=1024, transcendentals=0),
        name=name,
    )(*operands, *after)
    return (tuple(made) if several else made[0]), mark


def grids(side):
    first = 0
    found = []
    for extent in (side, side // 2, side // 4):
        found.append((first, extent))
        first += extent * extent
    return found


def rows_of(side):
    return side * side + (side // 2) ** 2 + (side // 4) ** 2


def iota(shape, dim):
    return lax.broadcasted_iota(jnp.int32, shape, dim)


def edge_masks(side):
    row = iota((rows_of(side), 1), 0)
    first = jnp.zeros(row.shape, jnp.bool_)
    last = jnp.zeros(row.shape, jnp.bool_)
    for start, extent in grids(side):
        inside = (row >= start) & (row < start + extent * extent)
        column = (row - start) & (extent - 1)
        first = first | (inside & (column == 0))
        last = last | (inside & (column == extent - 1))
    return first, last


def column_shifts(value, side, low, high):
    first, last = edge_masks(side)
    rows = value.shape[0]
    fine = side * side
    for b, one in enumerate(
        (
            jnp.where(first, 0.0, pltpu.roll(value, 1, 0)),
            value,
            jnp.where(last, 0.0, pltpu.roll(value, rows - 1, 0)),
        )
    ):
        low[b] = one[:fine].astype(BF16)
        high[b] = one[fine:]


def put_row_shift(target, row_start, lane_start, low, high, b, a, side):
    width = low.shape[2]
    lanes = slice(lane_start, lane_start + width)
    fine = side * side
    for start, extent in grids(side):
        count = extent * extent
        row = row_start + start
        if start == 0:
            blank = jnp.zeros((extent, width), BF16)
            if a == 1:
                target[row : row + count, lanes] = low[b]
            elif a == 0:
                target[row : row + extent, lanes] = blank
                target[row + extent : row + count, lanes] = low[b, : count - extent, :]
            else:
                target[row : row + count - extent, lanes] = low[b, extent:, :]
                target[row + count - extent : row + count, lanes] = blank
            continue
        start -= fine
        if a == 1:
            part = high[b, start : start + count, :]
        elif extent % 8 == 0:
            blank = jnp.zeros((extent, width), F32)
            if a == 0:
                part = jnp.concatenate([blank, high[b, start : start + count - extent, :]], axis=0)
            else:
                part = jnp.concatenate([high[b, start + extent : start + count, :], blank], axis=0)
        else:
            whole = high[b, start : start + count, :]
            at = iota((count, 1), 0)
            if a == 0:
                part = jnp.where(at < extent, 0.0, pltpu.roll(whole, extent, 0))
            else:
                part = jnp.where(at >= count - extent, 0.0, pltpu.roll(whole, count - extent, 0))
        target[row : row + count, lanes] = part.astype(BF16)


def shift_scratch(side, width):
    fine = side * side
    return [
        pltpu.VMEM((3, fine, width), BF16),
        pltpu.VMEM((3, rows_of(side) - fine, width), F32),
    ]


def dot(left, right):
    return lax.dot_general(left, right, (((1,), (0,)), ((), ())), preferred_element_type=F32)


def dot_last(left, right):
    return lax.dot_general(left, right, (((1,), (1,)), ((), ())), preferred_element_type=F32)


def block_of(index, extent):
    bits = extent.bit_length() - 1
    return ((index >> (bits + 1)) << (bits - 1)) + ((index & (extent - 1)) >> 1)


def pool_matrix(extent, value):
    count = extent * extent
    shape = (count // 4, count)
    return jnp.where(block_of(iota(shape, 1), extent) == iota(shape, 0), value, 0.0).astype(BF16)


def spread_matrix(extent):
    count = extent * extent
    shape = (count, count // 4)
    return jnp.where(block_of(iota(shape, 0), extent) == iota(shape, 1), 1.0, 0.0).astype(BF16)


def spread(matrix, value):
    high = value.astype(BF16)
    low = (value - high.astype(F32)).astype(BF16)
    return dot(matrix, high) + dot(matrix, low)


def gelu_and_slope(z):
    root = 0.7978845608028654
    inner = root * (z + 0.044715 * z * z * z)
    t = jnp.tanh(inner)
    half = 0.5 * (1.0 + t)
    slope = half + 0.5 * z * (1.0 - t * t) * (root * (1.0 + 3 * 0.044715 * z * z))
    return z * half, slope


def head_cotangents(cot, coarse_cot, weights):
    return jnp.concatenate(
        [
            (weights[0] * cot).astype(BF16),
            (weights[1] * cot).astype(BF16),
            (weights[2] * coarse_cot).astype(BF16),
        ],
        axis=0,
    )


def copies(pairs, sems):
    made = [
        pltpu.make_async_copy(source, target, sems.at[num])
        for num, (source, target) in enumerate(pairs)
    ]
    for one in made:
        one.start()
    return made


def tap_norm(tap):
    return lax.rsqrt(jnp.mean(tap * tap, axis=-1, keepdims=True) + EPSILON)


def tap_backward(tap, r, scale_row, back, wide, mid):
    back = jnp.concatenate([spread(wide, 0.25 * back[:mid]), back[mid:]], axis=0)
    upstream = back * scale_row
    grad = r * (upstream - tap * (r * r) * jnp.mean(upstream * tap, axis=-1, keepdims=True))
    return grad, jnp.sum(back * tap * r, axis=0, keepdims=True)


def section_kernel(
    side,
    dp,
    plan,
    features,
    trunk_weight,
    head_weight,
    cotangent,
    gain_in,
    shift_in,
    scale_in,
    merging_in,
    own_out,
    send_out,
    pass_out,
    grad_out,
    slope_out,
    normed_out,
    scale_out,
    feed,
    weights,
    heads,
    cot_ref,
    gain,
    shift,
    scale,
    merging,
    low_shifted,
    high_shifted,
    patch,
    sems,
):
    rows = rows_of(side)
    fine = side * side
    channels = feed.shape[1]
    half = channels // 2
    width = heads.shape[1]
    at = Layout(side, channels, width)
    mid = at.mid
    pipe = lax.axis_index("pipe")
    core = own_core(dp)
    pick = block_bits(dp, core, LATE)[0]
    made = copies(
        [(features.at[plan[0, pipe]], feed)]
        + [
            (
                trunk_weight.at[num // 3, pl.ds(num % 3 * 3 * channels, 3 * channels)],
                weights.at[num],
            )
            for num in range(6)
        ]
        + [(cotangent.at[pipe], cot_ref), (head_weight.at[1], heads)]
        + [(gain_in, gain), (shift_in, shift), (scale_in, scale), (merging_in, merging)],
        sems,
    )
    made[0].wait()

    def conv(value, layer):
        column_shifts(value, side, low_shifted, high_shifted)
        total = jnp.zeros((rows, channels), F32)
        for a in range(3):
            for b in range(3):
                put_row_shift(patch, 0, b * channels, low_shifted, high_shifted, b, a, side)
            made[1 + 3 * layer + a].wait()
            total = total + dot(patch[...], weights[3 * layer + a])
        return total

    def put_halves(first, value):
        count = value.shape[0]
        left = value[:, :half]
        right = value[:, half:]
        own_out[first : first + count, :] = jnp.where(core == 0, left, right)
        send_out[first : first + count, :] = jnp.where(core == 0, right, left)

    low_feed = feed[...]
    feed_value = low_feed.astype(F32)
    put_halves(at.feed, low_feed)
    first_pre = conv(feed_value, 0)
    for num in range(9, 13):
        made[num].wait()
    act1, slope1 = gelu_and_slope(gain[0:1, :] * first_pre + shift[0:1, :])
    slope_out[...] = slope1 * gain[0:1, :]
    low_act = act1.astype(BF16)
    put_halves(at.act, low_act)
    z2 = gain[1:2, :] * conv(low_act.astype(F32), 1) + shift[1:2, :]
    trunk_out, slope2 = gelu_and_slope(z2)
    taps = [feed_value, trunk_out.astype(BF16).astype(F32)]

    pool = pool_matrix(side, 0.25)
    for k in range(2):
        tap = taps[k]
        r = tap_norm(tap)
        normed = (tap * r * scale[k : k + 1, :]).astype(BF16)
        pooled = dot(pool, normed[:fine]).astype(BF16)
        rows_k = jnp.concatenate([pooled, normed[fine:]], axis=0)
        put_halves(at.normed + k * at.stacked, rows_k)
        normed_out[k] = rows_k
    made[7].wait()
    cot_low = cot_ref[...]
    coarse_cot = dot(pool_matrix(side // 2, 1.0), cot_low)
    grads = head_cotangents(
        cot_low.astype(F32), coarse_cot, [merging[s, 1:2, :] for s in range(3)]
    )
    made[8].wait()
    tap_grad, scale_row = tap_backward(
        tap, r, scale[1:2, :], dot_last(grads, heads[...]), spread_matrix(side), mid
    )
    scale_out[...] = jnp.broadcast_to(scale_row, scale_out.shape)
    grad2 = (tap_grad.astype(BF16).astype(F32) * slope2 * gain[1:2, :]).astype(BF16)
    for num in range(2):
        grad_out[num * rows : (num + 1) * rows, :] = grad2[:, num * half : (num + 1) * half]
    for target in (own_out, send_out):
        for num in range(2):
            target[at.grad[num] : at.grad[num] + rows, :] = grad2[:, num * half : (num + 1) * half]
        for num in range(at.lanes):
            lanes = slice(num * half, (num + 1) * half)
            target[at.cot + num * mid : at.cot + (num + 1) * mid, :] = cot_low[:, lanes]
    pass_out[...] = own_out[pl.ds(pl.multiple_of((1 - pick) * at.skip, 16), at.span), :]


def section(dp, plan, features, trunk_weight, head_weight, cotangent, gain, shift, scale, merging):
    side = SIDE
    rows = rows_of(side)
    channels = features.shape[2]
    half = channels // 2
    width = head_weight.shape[2]
    mid = cotangent.shape[1]
    at = Layout(side, channels, width)
    vmem = spec(pltpu.VMEM)
    return call(
        partial(section_kernel, side, dp),
        "section",
        60,
        1150000000,
        (plan, features, trunk_weight, head_weight, cotangent, gain, shift, scale, merging),
        [spec(pltpu.SMEM)] + [spec(pltpu.HBM)] * 8,
        (
            jax.ShapeDtypeStruct((at.total, half), BF16),
            jax.ShapeDtypeStruct((at.total, half), BF16),
            jax.ShapeDtypeStruct((at.span, half), BF16),
            jax.ShapeDtypeStruct((2 * rows, half), BF16),
            jax.ShapeDtypeStruct((rows, channels), F32),
            jax.ShapeDtypeStruct((2, at.stacked, channels), BF16),
            jax.ShapeDtypeStruct((8, channels), F32),
        ),
        (vmem,) * 7,
        [
            pltpu.VMEM((rows, channels), BF16),
            pltpu.VMEM((6, 3 * channels, channels), BF16),
            pltpu.VMEM((channels, width), BF16),
            pltpu.VMEM((mid, width), BF16),
            pltpu.VMEM(gain.shape, F32),
            pltpu.VMEM(shift.shape, F32),
            pltpu.VMEM(scale.shape, F32),
            pltpu.VMEM(merging.shape, F32),
            *shift_scratch(side, channels),
            pltpu.VMEM((rows, 3 * channels), BF16),
            pltpu.SemaphoreType.DMA((13,)),
        ],
    )


def back_kernel(side, layer, grad_in, trunk_weight, factor_in, *rest):
    grad, factor, weights, low_shifted, high_shifted, patch, sems = rest[-7:]
    channels = trunk_weight.shape[2]
    half = channels // 2
    rows = rows_of(side)
    made = copies(
        [(grad_in, grad)]
        + [
            (trunk_weight.at[layer, pl.ds(num * channels, channels)], weights.at[num])
            for num in range(9)
        ]
        + [(factor_in, factor)],
        sems,
    )
    made[0].wait()
    value = jnp.concatenate([grad[:rows, :], grad[rows:, :]], axis=1).astype(F32)
    column_shifts(value, side, low_shifted, high_shifted)
    total = jnp.zeros((rows, channels), F32)
    for a in range(3):
        for b in range(3):
            put_row_shift(
                patch, 0, b * channels, low_shifted, high_shifted, 2 - b, 2 - a, side
            )
        for b in range(3):
            made[1 + 3 * a + b].wait()
            total = total + dot_last(
                patch[:, b * channels : (b + 1) * channels], weights[3 * a + b]
            )
    made[10].wait()
    if layer == 1:
        (grad_out,) = rest[:-7]
        low = (total * factor[...]).astype(BF16)
        grad_out[:rows, :] = low[:, :half]
        grad_out[rows:, :] = low[:, half:]
        return
    merged, own_out, send_out = rest[:-7]
    pipe = lax.axis_index("pipe")
    total = total + factor[...]
    left, right = total[:, :half], total[:, half:]
    own_out[...] = jnp.where(pipe == 0, left, right)
    sent = jnp.where(pipe == 0, right, left).astype(BF16)
    low_merged = merged[...]
    mid, width = low_merged.shape
    sent_merged = jnp.where(
        pipe == 0, low_merged[:, width // 2 :], low_merged[:, : width // 2]
    )
    for num in range(half // 128):
        send_out[num * rows : (num + 1) * rows, :] = sent[:, num * 128 : (num + 1) * 128]
    first = half // 128 * rows
    for num in range(width // 256):
        send_out[first + num * mid : first + (num + 1) * mid, :] = sent_merged[
            :, num * 128 : (num + 1) * 128
        ]


def back(layer, grad, trunk_weight, factor, merged=None, after=()):
    side = SIDE
    rows = rows_of(side)
    channels = trunk_weight.shape[2]
    half = channels // 2
    vmem = spec(pltpu.VMEM)
    hbm = spec(pl.ANY)
    in_specs = [hbm, spec(pltpu.HBM), hbm]
    operands = [grad, trunk_weight, factor]
    if layer == 0:
        in_specs.append(vmem)
        operands.append(merged)
        out_shape = (
            jax.ShapeDtypeStruct((rows, half), F32),
            jax.ShapeDtypeStruct((half // 128 * rows + merged.size // 256, 128), BF16),
        )
        out_specs = (vmem, vmem)
    else:
        out_shape = jax.ShapeDtypeStruct((2 * rows, half), BF16)
        out_specs = vmem
    return call(
        partial(back_kernel, side, layer),
        "back",
        60 if layer else 46,
        350000000,
        operands,
        in_specs,
        out_shape,
        out_specs,
        [
            pltpu.VMEM((2 * rows, half), BF16),
            pltpu.VMEM((rows, channels), F32),
            pltpu.VMEM((9, channels, channels), BF16),
            *shift_scratch(side, channels),
            pltpu.VMEM((rows, 3 * channels), BF16),
            pltpu.SemaphoreType.DMA((11,)),
        ],
        after,
    )


def move_kernel(moves, *refs):
    sources, out, sems = refs[:-2], refs[-2], refs[-1]
    made = copies(
        [
            (sources[num].at[first()], out.at[pl.ds(place, count)])
            for num, first, place, count in moves
        ],
        sems,
    )
    for one in made:
        one.wait()


def far_factors(dp, other, side, width, after):
    half = other.shape[1]
    at = Layout(side, 2 * half, width)

    def rows():
        pick = block_bits(dp, own_core(dp), LATE)[0]
        return pl.ds(pl.multiple_of((1 - pick) * at.skip, 16), at.span)

    return call(
        partial(move_kernel, [(0, rows, 0, at.span)]),
        "far_factors",
        4,
        30000000,
        (other,),
        [spec(pl.ANY)],
        jax.ShapeDtypeStruct((at.span, half), BF16),
        spec(pltpu.VMEM),
        [pltpu.SemaphoreType.DMA((1,))],
        after,
    )


def first_factors(dp, own, other, own_grad, other_grad, side, width, after):
    half = other.shape[1]
    at = Layout(side, 2 * half, width)

    def feed():
        return pl.ds(at.feed, at.rows)

    def grad():
        pick = block_bits(dp, own_core(dp), EARLY)[0]
        return pl.ds(pl.multiple_of((1 - pick) * at.rows, 16), at.rows)

    return call(
        partial(
            move_kernel,
            [
                (num, (feed, feed, grad, grad)[num], num * at.rows, at.rows)
                for num in range(4)
            ],
        ),
        "first_factors",
        4,
        90000000,
        (own, other, own_grad, other_grad),
        [spec(pl.ANY)] * 4,
        jax.ShapeDtypeStruct((4 * at.rows, half), BF16),
        spec(pltpu.VMEM),
        [pltpu.SemaphoreType.DMA((4,))],
        after,
    )


def put_trunk_blocks(dp, piece, send, keep, xs, gs, low, high, patch, side, wait_x, wait_g):
    rows = rows_of(side)
    half = xs.shape[1]
    quarter = half // 2
    _, second, third = block_bits(dp, own_core(dp), piece)
    for image in range(4):
        wait_g(image)
        column_shifts(gs[image * rows : (image + 1) * rows, :].astype(F32), side, low, high)
        for a in range(3):
            for b in range(3):
                put_row_shift(
                    patch, image * rows, (3 * a + b) * half, low, high, 2 - b, 2 - a, side
                )
    for image in range(4):
        wait_x(image)
    turned = xs[...].T
    for offset in range(9):
        product = dot(turned, patch[:, offset * half : (offset + 1) * half]).astype(BF16)
        left, right = product[:, :128], product[:, 128:]
        for target, value in (
            (keep, jnp.where(second == 0, left, right)),
            (send, jnp.where(second == 0, right, left)),
        ):
            upper, lower = value[:quarter], value[quarter:]
            row = offset * quarter
            target[row : row + quarter, :] = jnp.where(third == 0, upper, lower)
            row += 9 * quarter
            target[row : row + quarter, :] = jnp.where(third == 0, lower, upper)


def late_grads_kernel(
    side, dp, width, own, other, near, far, send, keep, xs, gs, low, high, patch, sems
):
    half = xs.shape[1]
    at = Layout(side, 2 * half, width)
    rows = at.rows
    pick = block_bits(dp, own_core(dp), LATE)[0]
    grad_at = pick * at.grad[1]
    pairs = []
    for num, source in enumerate((own, other, near, far)):
        back_by = 0 if num < 2 else pick * at.skip

        def some(first):
            return source.at[pl.ds(pl.multiple_of(first - back_by, 16), rows)]

        pairs += [
            (some(grad_at), gs.at[pl.ds(num * rows, rows)]),
            (some(at.act), xs.at[pl.ds(num * rows, rows)]),
        ]
    made = copies(pairs, sems)
    put_trunk_blocks(
        dp,
        LATE,
        send,
        keep,
        xs,
        gs,
        low,
        high,
        patch,
        side,
        lambda image: made[2 * image + 1].wait(),
        lambda image: made[2 * image].wait(),
    )


def split_pair(value):
    high = value.astype(BF16).astype(F32)
    return jnp.concatenate([high, value - high], axis=0).astype(BF16)


def trunk_scratch(rows, half):
    return shift_scratch(SIDE, half) + [pltpu.VMEM((4 * rows, 9 * half), BF16)]


def late_grads(dp, width, own, other, near, far, after):
    side = SIDE
    rows = rows_of(side)
    half = own.shape[1]
    vmem = spec(pltpu.VMEM)
    shape = jax.ShapeDtypeStruct((9 * half, 128), BF16)
    return call(
        partial(late_grads_kernel, side, dp, width),
        "late_grads",
        28,
        430000000,
        (own, other, near, far),
        [spec(pl.ANY)] * 4,
        (shape, shape),
        (vmem, vmem),
        [
            pltpu.VMEM((4 * rows, half), BF16),
            pltpu.VMEM((4 * rows, half), BF16),
            *trunk_scratch(rows, half),
            pltpu.SemaphoreType.DMA((8,)),
        ],
        after,
    )


def early_grads_kernel(
    side, dp, width, own, other, own_g, other_g, far, send, keep, xs, gs, low, high, patch, sems
):
    half = xs.shape[1]
    at = Layout(side, 2 * half, width)
    rows = at.rows
    pick = block_bits(dp, own_core(dp), EARLY)[0]
    mine = pl.ds(pl.multiple_of(pick * rows, 16), rows)
    made = copies(
        [
            (own_g.at[mine], gs.at[pl.ds(0, rows)]),
            (other_g.at[mine], gs.at[pl.ds(rows, rows)]),
            (far.at[pl.ds(2 * rows, 2 * rows)], gs.at[pl.ds(2 * rows, 2 * rows)]),
            (own.at[pl.ds(at.feed, rows)], xs.at[pl.ds(0, rows)]),
            (other.at[pl.ds(at.feed, rows)], xs.at[pl.ds(rows, rows)]),
            (far.at[pl.ds(0, 2 * rows)], xs.at[pl.ds(2 * rows, 2 * rows)]),
        ],
        sems,
    )
    put_trunk_blocks(
        dp,
        EARLY,
        send,
        keep,
        xs,
        gs,
        low,
        high,
        patch,
        side,
        lambda image: made[3 + image].wait() if image < 3 else None,
        lambda image: made[image].wait() if image < 3 else None,
    )


def early_grads(dp, width, own, other, own_g, other_g, far, after):
    side = SIDE
    rows = rows_of(side)
    half = own.shape[1]
    vmem = spec(pltpu.VMEM)
    shape = jax.ShapeDtypeStruct((9 * half, 128), BF16)
    return call(
        partial(early_grads_kernel, side, dp, width),
        "early_grads",
        28,
        370000000,
        (own, other, own_g, other_g, far),
        [spec(pl.ANY)] * 5,
        (shape, shape),
        (vmem, vmem),
        [
            pltpu.VMEM((4 * rows, half), BF16),
            pltpu.VMEM((4 * rows, half), BF16),
            *trunk_scratch(rows, half),
            pltpu.SemaphoreType.DMA((6,)),
        ],
        after,
    )


def head_grads_kernel(
    side,
    dp,
    plan,
    features,
    head_weight,
    normed_in,
    scale_in,
    last_scale_in,
    own,
    other,
    merging_in,
    send,
    keep,
    merged_out,
    tap_grad_out,
    feed,
    heads,
    normed,
    scale,
    last_scale,
    ns,
    cots,
    merging,
    sems,
):
    half = ns.shape[2]
    width = merging.shape[2]
    at = Layout(side, 2 * half, width)
    mid = at.mid
    quarter = half // 2
    pick, second, third = block_bits(dp, own_core(dp), HEAD)
    pairs = [(merging_in, merging)]
    for num, source in enumerate((own, other)):
        pairs += [
            (source.at[pl.ds(at.cot, at.lanes * mid)], cots.at[num]),
            (source.at[pl.ds(at.normed, 2 * at.stacked)], ns.at[num]),
        ]
    pairs += [(normed_in, normed), (head_weight.at[0], heads.at[0])]
    pairs += [(features.at[plan[0, lax.axis_index("pipe")]], feed), (scale_in, scale)]
    pairs += [(last_scale_in, last_scale), (head_weight.at[1], heads.at[1])]
    made = copies(pairs, sems)
    sums = pool_matrix(side // 2, 1.0)
    cotangents = []
    for image in range(2):
        made[1 + 2 * image].wait()
        cot_low = jnp.concatenate(
            [cots[image, num * mid : (num + 1) * mid, :] for num in range(at.lanes)], axis=1
        )
        cotangents.append((cot_low.astype(F32), dot(sums, cot_low)))
    for one in (made[0], made[2], made[4]):
        one.wait()
    for target, tap in ((send, 1 - pick), (keep, pick)):
        weights = [merging[s, pl.ds(tap, 1), :] for s in range(3)]
        grads = [head_cotangents(cot, coarse, weights) for cot, coarse in cotangents]
        first = pl.multiple_of(tap * at.stacked, 16)
        both = [ns[image, pl.ds(first, at.stacked), :] for image in range(2)]
        product = dot(
            jnp.concatenate(both, axis=0).T, jnp.concatenate(grads, axis=0)
        ).astype(BF16)
        for lane in range(2):
            for num in range(width // 256):
                column = lane * (width // 2) + num * 128
                for part in range(2):
                    row = ((lane ^ second) * 2 + (part ^ third)) * (width // 256) + num
                    target[pl.ds(pl.multiple_of(row * quarter, quarter), quarter), :] = product[
                        part * quarter : (part + 1) * quarter, column : column + 128
                    ]
    cot, coarse_cot = cotangents[0]
    merged = jnp.zeros((mid, width), F32)
    coarse_merged = jnp.zeros((at.stacked - 2 * mid, width), F32)
    small = []
    made[5].wait()
    for k in range(2):
        made[6 if k == 0 else 10].wait()
        weights = [merging[s, k : k + 1, :] for s in range(3)]
        product = dot(normed[k], heads[k])
        merged = merged + weights[0] * product[:mid] + weights[1] * product[mid : 2 * mid]
        coarse_merged = coarse_merged + weights[2] * product[2 * mid :]
        small.append(jnp.sum(cot * product[:mid], axis=0, keepdims=True))
        small.append(jnp.sum(cot * product[mid : 2 * mid], axis=0, keepdims=True))
        small.append(jnp.sum(coarse_cot * product[2 * mid :], axis=0, keepdims=True))
        if k == 0:
            for one in made[7:10]:
                one.wait()
            tap = feed[...].astype(F32)
            back = dot_last(head_cotangents(cot, coarse_cot, weights), heads[0])
            tap_grad_out[...], scale_row = tap_backward(
                tap, tap_norm(tap), scale[0:1, :], back, spread_matrix(side), mid
            )
    merged = merged + spread(spread_matrix(side // 2), coarse_merged)
    merged_out[...] = merged.astype(BF16)
    small.append(
        jnp.concatenate(
            [scale_row, last_scale[0:1, :], jnp.zeros((1, width - 4 * half), F32)], axis=1
        )
    )
    small.append(jnp.zeros((1, width), F32))
    pair = split_pair(jnp.concatenate(small, axis=0))
    first = width // 128 * half
    for num in range(width // 128):
        for target in (send, keep):
            target[first + num * 16 : first + (num + 1) * 16, :] = pair[
                :, num * 128 : (num + 1) * 128
            ]


def head_grads(
    dp, plan, features, head_weight, normed, scale, last_scale, own, other, merging, after
):
    side = SIDE
    rows = rows_of(side)
    half = own.shape[1]
    width = merging.shape[2]
    at = Layout(side, 2 * half, width)
    shape = jax.ShapeDtypeStruct((width // 128 * half + 16 * width // 128, 128), BF16)
    vmem = spec(pltpu.VMEM)
    return call(
        partial(head_grads_kernel, side, dp),
        "head_grads",
        40,
        610000000,
        (plan, features, head_weight, normed, scale, last_scale, own, other, merging),
        [spec(pltpu.SMEM), spec(pltpu.HBM), spec(pltpu.HBM), spec(pl.ANY), spec(pltpu.HBM)]
        + [spec(pl.ANY)] * 3
        + [spec(pltpu.HBM)],
        (
            shape,
            shape,
            jax.ShapeDtypeStruct((at.mid, width), BF16),
            jax.ShapeDtypeStruct((rows, 2 * half), F32),
        ),
        (vmem,) * 4,
        [
            pltpu.VMEM((rows, 2 * half), BF16),
            pltpu.VMEM((2, 2 * half, width), BF16),
            pltpu.VMEM((2, at.stacked, 2 * half), BF16),
            pltpu.VMEM(scale.shape, F32),
            pltpu.VMEM(last_scale.shape, F32),
            pltpu.VMEM((2, 2 * at.stacked, half), BF16),
            pltpu.VMEM((2, at.lanes * at.mid, half), BF16),
            pltpu.VMEM(merging.shape, F32),
            pltpu.SemaphoreType.DMA((11,)),
        ],
        after,
    )


def held_back(array, after):
    def kernel(*refs):
        pass

    hbm = spec(pl.ANY)
    shape = jax.ShapeDtypeStruct(array.shape, array.dtype)
    return call(kernel, "held_back", 4, 1024, (array,), [hbm], shape, hbm, (), after, {0: 0})


def add_tails(one, two):
    count = one.shape[0] // 16
    one = one.astype(F32).reshape(count, 16, 128)
    two = two.astype(F32).reshape(count, 16, 128)
    total = (one[:, :8] + one[:, 8:]) + (two[:, :8] + two[:, 8:])
    high = total.astype(BF16).astype(F32)
    return jnp.concatenate([high, total - high], axis=1).reshape(count * 16, 128).astype(BF16)


def sum_kernel(tail, keep, received, *outs):
    rows = keep.shape[0] - tail
    size = rows // len(outs)
    for num, out in enumerate(outs):
        part = slice(num * size, (num + 1) * size)
        out[:size, :] = (keep[part, :].astype(F32) + received[part, :].astype(F32)).astype(BF16)
    if tail:
        total = add_tails(keep[rows:, :], received[rows:, :])
        for out in outs:
            out[size:, :] = total


def summed(keep, received, parts, tail, after):
    vmem = spec(pltpu.VMEM)
    shape = jax.ShapeDtypeStruct(((keep.shape[0] - tail) // parts + tail, 128), BF16)
    return call(
        partial(sum_kernel, tail),
        "summed",
        4,
        10000000,
        (keep, received),
        [vmem, vmem],
        (shape,) * parts,
        (vmem,) * parts,
        (),
        after,
    )


def pair_kernel(one, two, out):
    rows = out.shape[0] // 2
    out[:rows, :] = one[:rows, :]
    out[rows:, :] = two[:rows, :]


def paired(one, two, rows, after):
    vmem = spec(pltpu.VMEM)
    return call(
        pair_kernel,
        "paired",
        4,
        10000000,
        (one, two),
        [vmem, vmem],
        jax.ShapeDtypeStruct((2 * rows, 128), BF16),
        vmem,
        (),
        after,
    )


def widen_trunk_kernel(dp, layer, half, kinds, *refs):
    sources = refs[: len(kinds)]
    out, held, wide, sems_in, sems_out = refs[-5:]
    quarter = half // 2
    size = 9 * quarter
    jobs = []
    coming = []
    for source, (is_other, is_new) in zip(sources, kinds):
        core = own_core(dp) ^ int(is_other)
        first, second, third = block_bits(dp, core, LATE if layer else EARLY)
        first = first ^ int(is_new)
        for part in range(2):
            for lane in range(2):
                row = pl.multiple_of(((lane ^ second) * 2 + part) * size, size)
                coming.append((source.at[pl.ds(row, size)], held.at[len(jobs), lane]))
            jobs.append((core * half + (part ^ third) * quarter, first * half))
    made = copies(coming, sems_in)
    going = []
    for num, (row, column) in enumerate(jobs):
        for lane in range(2):
            made[2 * num + lane].wait()
            for offset in range(9):
                wide[num, offset, :, lane * 128 : (lane + 1) * 128] = held[
                    num, lane, offset * quarter : (offset + 1) * quarter, :
                ].astype(F32)
        one = pltpu.make_async_copy(
            wide.at[num],
            out.at[
                layer,
                :,
                pl.ds(pl.multiple_of(row, quarter), quarter),
                pl.ds(pl.multiple_of(column, half), half),
            ],
            sems_out.at[num],
        )
        one.start()
        going.append(one)
    for one in going:
        one.wait()


def widen_trunk(dp, layer, layers, half, sources, kinds, before=None, after=()):
    hbm = spec(pl.ANY)
    operands = list(sources) + ([before] if before is not None else [])
    count = 2 * len(kinds)
    return call(
        partial(widen_trunk_kernel, dp, layer, half, kinds),
        "widen_trunk",
        24,
        290000000,
        operands,
        [hbm] * len(operands),
        jax.ShapeDtypeStruct((layers, 9, 2 * half, 2 * half), F32),
        hbm,
        [
            pltpu.VMEM((count, 2, 9 * half // 2, 128), BF16),
            pltpu.VMEM((count, 9, half // 2, half), F32),
            pltpu.SemaphoreType.DMA((2 * count,)),
            pltpu.SemaphoreType.DMA((count,)),
        ],
        after,
        {len(sources): 0} if before is not None else None,
    )


def widen_heads_kernel(dp, half, kinds, *refs):
    sources = refs[: len(kinds)]
    out, held, wide, sems_in, sems_out = refs[-5:]
    quarter = half // 2
    size = held.shape[2]
    width = wide.shape[2]
    jobs = []
    coming = []
    for source, (is_other, is_new) in zip(sources, kinds):
        core = own_core(dp) ^ int(is_other)
        first, second, third = block_bits(dp, core, HEAD)
        for lane in range(2):
            for part in range(2):
                row = pl.multiple_of(((lane ^ second) * 2 + (part ^ third)) * size, size)
                coming.append((source.at[pl.ds(row, size)], held.at[len(jobs), part]))
            jobs.append((first ^ int(is_new), core * half, lane * width))
    made = copies(coming, sems_in)
    going = []
    for num, (tap, row, column) in enumerate(jobs):
        for part in range(2):
            made[2 * num + part].wait()
            for piece in range(width // 128):
                wide[
                    num, part * quarter : (part + 1) * quarter, piece * 128 : (piece + 1) * 128
                ] = held[num, part, piece * quarter : (piece + 1) * quarter, :].astype(F32)
        one = pltpu.make_async_copy(
            wide.at[num],
            out.at[tap, pl.ds(pl.multiple_of(row, half), half), pl.ds(column, width)],
            sems_out.at[num],
        )
        one.start()
        going.append(one)
    for one in going:
        one.wait()


def widen_heads(dp, half, width, sources, kinds, before=None, after=()):
    hbm = spec(pl.ANY)
    operands = list(sources) + ([before] if before is not None else [])
    count = 2 * len(kinds)
    return call(
        partial(widen_heads_kernel, dp, half, kinds),
        "widen_heads",
        40,
        440000000,
        operands,
        [hbm] * len(operands),
        jax.ShapeDtypeStruct((2, 2 * half, width), F32),
        hbm,
        [
            pltpu.VMEM((count, 2, width // 256 * half // 2, 128), BF16),
            pltpu.VMEM((count, half, width // 2), F32),
            pltpu.SemaphoreType.DMA((2 * count,)),
            pltpu.SemaphoreType.DMA((count,)),
        ],
        after,
        {len(sources): 0} if before is not None else None,
    )


def finish_kernel(
    dp, tail, plan, own_feed, merged, received, own_sum, other_sum,
    merged_out, feed_out, scale_out, merging_out,
    feeds, maps, ours, theirs, scales, weights, sems,
):
    rows, half = own_feed.shape
    mid, width = merged.shape
    first = own_sum.shape[0] - tail
    pipe = lax.axis_index("pipe")
    slot = plan[0, pipe]
    made = copies(
        [
            (own_feed, feed_out.at[slot]),
            (own_sum.at[pl.ds(first, tail)], ours),
            (other_sum.at[pl.ds(first, tail)], theirs),
        ],
        sems,
    )
    for num in range(half // 128):
        feeds[:, num * 128 : (num + 1) * 128] = received[
            num * rows : (num + 1) * rows, :
        ].astype(F32)
    low_merged = merged[...]
    maps[0] = jnp.where(pipe == 0, low_merged[:, : width // 2], low_merged[:, width // 2 :])
    first = half // 128 * rows
    for num in range(width // 256):
        maps[1, :, num * 128 : (num + 1) * 128] = received[
            first + num * mid : first + (num + 1) * mid, :
        ]
    going = [
        pltpu.make_async_copy(feeds, feed_out.at[1 - slot], sems.at[3]),
        pltpu.make_async_copy(maps.at[0], merged_out.at[pipe], sems.at[4]),
        pltpu.make_async_copy(maps.at[1], merged_out.at[1 - pipe], sems.at[5]),
    ]
    for one in going:
        one.start()
    made[1].wait()
    made[2].wait()
    total = ours[...].astype(F32) + theirs[...].astype(F32)
    for num in range(width // 128):
        lanes = slice(num * 128, (num + 1) * 128)
        block = total[num * 16 : num * 16 + 8] + total[num * 16 + 8 : num * 16 + 16]
        for k in range(2):
            for s in range(3):
                weights[s, k : k + 1, lanes] = block[3 * k + s : 3 * k + s + 1]
            column = num * 128 - k * 2 * half
            if 0 <= column < 2 * half:
                scales[k : k + 1, column : column + 128] = block[6:7]
    going += [
        pltpu.make_async_copy(scales, scale_out, sems.at[6]),
        pltpu.make_async_copy(weights, merging_out, sems.at[7]),
    ]
    for one in going[3:]:
        one.start()
    for one in going + made[:1]:
        one.wait()


def finish(dp, plan, own_feed, merged, received, own_sum, other_sum, after):
    rows, half = own_feed.shape
    mid, width = merged.shape
    vmem = spec(pltpu.VMEM)
    hbm = spec(pl.ANY)
    tail = 16 * width // 128
    return call(
        partial(finish_kernel, dp, tail),
        "finish",
        8,
        170000000,
        (plan, own_feed, merged, received, own_sum, other_sum),
        [spec(pltpu.SMEM), hbm, vmem, vmem, hbm, hbm],
        (
            jax.ShapeDtypeStruct((2, mid, width // 2), BF16),
            jax.ShapeDtypeStruct((2, rows, half), F32),
            jax.ShapeDtypeStruct((2, 2 * half), F32),
            jax.ShapeDtypeStruct((3, 2, width), F32),
        ),
        (hbm,) * 4,
        [
            pltpu.VMEM((rows, half), F32),
            pltpu.VMEM((2, mid, width // 2), BF16),
            pltpu.VMEM((tail, 128), BF16),
            pltpu.VMEM((tail, 128), BF16),
            pltpu.VMEM((2, 2 * half), F32),
            pltpu.VMEM((3, 2, width), F32),
            pltpu.SemaphoreType.DMA((8,)),
        ],
        after,
    )


ORDER = (
    "back1",
    "far",
    "first",
    "head",
    "late",
    "early",
    "L2",
    "E2",
    "H1",
    "L3",
    "E3",
    "H2",
    "back0",
    "L4",
    "E4",
    "H3",
    "L5",
    "E5",
    "H4",
    "L6",
    "E6",
    "H5",
    "Lold_wide",
    "Eold_wide",
    "H6",
    "Lnew",
    "Lnew_own",
    "Enew",
    "Lnew_other",
    "Enew_own",
    "Hold_wide",
    "finish",
    "Hnew",
    "Enew_other",
    "Hnew_own",
    "Hnew_other",
)
WAITS = {"far": ("near",), "L6": ("feed",)}


class Sum:
    def __init__(self, swap, piece, last, send, keep, tail=0):
        self.swap = partial(swap, piece)
        self.tail = tail
        self.steps = [("scatter", stage) for stage in range(0 if piece == HEAD else 1, 3)]
        self.steps += [("whole", stage) for stage in range(3, last + 1)]
        self.steps += [("gather", stage) for stage in (2, 1, 0)]
        self.at = 0
        self.keep = keep
        self.come = self.swap(self.steps[0][1], send)

    def advance(self, after):
        kind = self.steps[self.at][0]
        self.at += 1
        following, stage = self.steps[self.at]
        if kind == "gather":
            rows = self.keep.shape[0] - self.tail
            self.keep, mark = paired(self.keep, self.come, rows, after)
            self.tail = 0
            send = self.keep
        else:
            parts = 2 if following == "scatter" else 1
            made, mark = summed(self.keep, self.come, parts, self.tail, after)
            self.keep = made[0]
            send = made[-1]
            if following == "gather":
                self.final = self.keep
        self.come = self.swap(stage, send)
        return mark


def body(
    features,
    plan,
    trunk_weight,
    trunk_gain,
    trunk_shift,
    head_weight,
    norm_scale,
    merging_weight,
    merged_cotangent,
):
    dp = lax.axis_size("dp")
    devices = lax.axis_size("pipe") * dp
    layers = trunk_weight.shape[0]
    channels = features.shape[2]
    half = channels // 2
    width = head_weight.shape[2]
    last = dp.bit_length() - 2
    weights = trunk_weight.reshape(layers, 9 * channels, channels)
    merging = jnp.transpose(merging_weight, (1, 0, 2))
    tail = 16 * width // 128

    def swap(piece, stage, block):
        bits = stage_bits(dp, piece)[stage]
        route = [(i, i ^ (1 << bits[i & 1])) for i in range(devices)]
        return lax.ppermute(block, AXES, route)

    def swap_cores(block):
        return lax.ppermute(block, AXES, [(i, i ^ 1) for i in range(devices)])

    (own, send, passed, grad2, slope, normed, last_scale), mark = section(
        dp,
        plan,
        features,
        weights,
        head_weight,
        merged_cotangent,
        trunk_gain,
        trunk_shift,
        norm_scale,
        merging,
    )
    other = swap_cores(send)
    near = swap(LATE, 0, passed)
    kept = ((False, False), (True, False))
    came = ((False, True), (True, True))
    got = {"before": None, "heads": None}
    pieces = {}

    def make_back1(after):
        got["grad1"], mark = back(1, grad2, weights, slope, None, after)
        got["other_grad1"] = swap_cores(got["grad1"])
        return mark

    def make_far(after):
        passed, mark = far_factors(dp, other, SIDE, width, after)
        got["far"] = swap(LATE, 0, passed)
        return mark

    def make_first(after):
        grads = (got["grad1"], got["other_grad1"])
        passed, mark = first_factors(dp, own, other, *grads, SIDE, width, after)
        got["first"] = swap(EARLY, 0, passed)
        return mark

    def make_head(after):
        blocks, mark = head_grads(
            dp,
            plan,
            features,
            head_weight,
            normed,
            norm_scale,
            last_scale,
            own,
            other,
            merging,
            after,
        )
        pieces["H"] = Sum(swap, HEAD, last, *blocks[:2], tail)
        got["maps"], got["tap_grad"] = blocks[2:]
        return mark

    def make_late(after):
        blocks, mark = late_grads(dp, width, own, other, near, got["far"], after)
        pieces["L"] = Sum(swap, LATE, last, *blocks)
        return mark

    def make_early(after):
        grads = (got["grad1"], got["other_grad1"])
        blocks, mark = early_grads(dp, width, own, other, *grads, got["first"], after)
        pieces["E"] = Sum(swap, EARLY, last, *blocks)
        return mark

    def make_back0(after):
        (got["feed"], sent), mark = back(
            0, got["grad1"], weights, got["tap_grad"], got["maps"], after
        )
        got["received"] = lax.ppermute(sent, "pipe", [(0, 1), (1, 0)])
        return mark

    def make_finish(after):
        sums = (pieces["H"].final, swap_cores(pieces["H"].final))
        got["finish"], mark = finish(
            dp, plan, got["feed"], got["maps"], got["received"], *sums, after
        )
        return mark

    def widen(name, sources, kinds, after):
        if name == "H":
            got["heads"], mark = widen_heads(
                dp, half, width, sources, kinds, got["heads"], after
            )
        else:
            layer = 1 if name == "L" else 0
            got["before"], mark = widen_trunk(
                dp, layer, layers, half, sources, kinds, got["before"], after
            )
        return mark

    make = {
        "back1": make_back1,
        "far": make_far,
        "first": make_first,
        "head": make_head,
        "late": make_late,
        "early": make_early,
        "back0": make_back0,
        "finish": make_finish,
    }
    for step in ORDER:
        name, kind = step[0], step[1:]
        waits = [mark]
        for which in WAITS.get(step, ()):
            come = {"near": near, "far": got.get("far"), "first": got.get("first")}
            come["feed"] = got.get("received")
            waits.append(pieces[which].come if which in pieces else come[which])
        if step in make:
            mark = make[step](waits)
        elif kind == "new":
            pieces[name].come, mark = held_back(pieces[name].come, waits)
            got[name] = swap_cores(pieces[name].come)
        elif kind == "old_wide":
            sources = (pieces[name].keep, swap_cores(pieces[name].keep))
            mark = widen(name, sources, kept, waits)
        elif kind == "new_wide":
            mark = widen(name, (pieces[name].come, got[name]), came, waits)
        elif kind == "new_own":
            mark = widen(name, (pieces[name].come,), came[:1], waits)
        elif kind == "new_other":
            mark = widen(name, (got[name],), came[1:], waits)
        else:
            mark = pieces[name].advance(waits)
            if kind == "4":
                for _ in range(3, last):
                    mark = pieces[name].advance([mark])
    merged_maps, features_grad, scale_grad, merging_grad = got["finish"]
    return (
        merged_maps,
        features_grad,
        got["before"].reshape(trunk_weight.shape),
        got["heads"],
        scale_grad,
        jnp.transpose(merging_grad, (1, 0, 2)),
    )


def solution(mesh):
    placed = (P("dp", None, None), P("dp", None), P(), P(), P(), P(), P(), P(), P("dp", None, None))
    return jax.shard_map(
        body,
        mesh=mesh,
        in_specs=placed,
        out_specs=(P("dp", None, "pipe"), P("dp", None, "pipe"), P(), P(), P(), P()),
        check_vma=False,
    )
```

```python
from functools import partial

import jax
import jax.numpy as jnp
from jax import lax
from jax.experimental import pallas as pl
from jax.experimental.pallas import tpu as pltpu
from jax.sharding import PartitionSpec as P

SIDE = 16
EPSILON = 1e-06
F32 = jnp.float32
BF16 = jnp.bfloat16
AXES = ("pipe", "dp")
MIB = 1024 * 1024


def device_index(dp):
    return lax.axis_index("pipe") * dp + lax.axis_index("dp")


HEAD, LATE, EARLY = 0, 1, 2


def stage_bits(dp, piece):
    size = dp.bit_length() - 1
    one, two, three, four = 1, size, 2, 3
    if piece == HEAD:
        stages = [(two, three), (one, two), (three, one), (four, four)]
    elif piece == LATE:
        stages = [(two, three), (one, two), (three, one), (four, four)]
    else:
        stages = [(one, three), (two, one), (three, two), (four, four)]
    return stages + [(bit, bit) for bit in range(4, size)]


def block_bits(dp, core, piece):
    index = device_index(dp)
    return [
        jnp.where(core == 0, (index >> first) & 1, (index >> second) & 1)
        for first, second in stage_bits(dp, piece)[:3]
    ]


def own_core(dp):
    return device_index(dp) & 1


class Layout:
    def __init__(self, side, channels, width):
        rows = rows_of(side)
        self.rows = rows
        self.mid = (side // 2) ** 2
        self.stacked = 2 * self.mid + (side // 4) ** 2
        self.lanes = width // (channels // 2)
        self.act = rows
        self.skip = rows
        self.span = 2 * rows
        self.grad = (0, self.span)
        self.normed = self.span + rows
        self.cot = self.normed + 2 * self.stacked
        self.feed = self.cot + self.lanes * self.mid
        self.total = self.feed + rows


def spec(memory):
    return pl.BlockSpec(memory_space=memory)


def call(kernel, name, mib, cost, operands, in_specs, out_shape, out_specs, scratch=(), after=(), aliases=None):
    count = len(operands)
    extra = len(after)
    several = isinstance(out_shape, tuple)
    shapes = out_shape if several else (out_shape,)
    specs = out_specs if several else (out_specs,)

    def run(*refs):
        results = refs[count + extra :]
        mark = results[len(shapes)]
        kernel(*refs[:count], *results[: len(shapes)], *results[len(shapes) + 1 :])
        mark[...] = jnp.zeros(mark.shape, F32)

    *made, mark = pl.pallas_call(
        run,
        out_shape=(*shapes, jax.ShapeDtypeStruct((8, 128), F32)),
        in_specs=list(in_specs) + [spec(pl.ANY)] * extra,
        out_specs=(*specs, spec(pltpu.VMEM)),
        scratch_shapes=list(scratch),
        input_output_aliases=aliases or {},
        compiler_params=pltpu.CompilerParams(vmem_limit_bytes=mib * MIB),
        cost_estimate=pl.CostEstimate(flops=cost, bytes_accessed=1024, transcendentals=0),
        name=name,
    )(*operands, *after)
    return (tuple(made) if several else made[0]), mark


def grids(side):
    first = 0
    found = []
    for extent in (side, side // 2, side // 4):
        found.append((first, extent))
        first += extent * extent
    return found


def rows_of(side):
    return side * side + (side // 2) ** 2 + (side // 4) ** 2


def iota(shape, dim):
    return lax.broadcasted_iota(jnp.int32, shape, dim)


def edge_masks(side):
    row = iota((rows_of(side), 1), 0)
    first = jnp.zeros(row.shape, jnp.bool_)
    last = jnp.zeros(row.shape, jnp.bool_)
    for start, extent in grids(side):
        inside = (row >= start) & (row < start + extent * extent)
        column = (row - start) & (extent - 1)
        first = first | (inside & (column == 0))
        last = last | (inside & (column == extent - 1))
    return first, last


def column_shifts(value, side, low, high):
    first, last = edge_masks(side)
    rows = value.shape[0]
    fine = side * side
    for b, one in enumerate(
        (
            jnp.where(first, 0.0, pltpu.roll(value, 1, 0)),
            value,
            jnp.where(last, 0.0, pltpu.roll(value, rows - 1, 0)),
        )
    ):
        low[b] = one[:fine].astype(BF16)
        high[b] = one[fine:]


def put_row_shift(target, row_start, lane_start, low, high, b, a, side):
    width = low.shape[2]
    lanes = slice(lane_start, lane_start + width)
    fine = side * side
    for start, extent in grids(side):
        count = extent * extent
        row = row_start + start
        if start == 0:
            blank = jnp.zeros((extent, width), BF16)
            if a == 1:
                target[row : row + count, lanes] = low[b]
            elif a == 0:
                target[row : row + extent, lanes] = blank
                target[row + extent : row + count, lanes] = low[b, : count - extent, :]
            else:
                target[row : row + count - extent, lanes] = low[b, extent:, :]
                target[row + count - extent : row + count, lanes] = blank
            continue
        start -= fine
        if a == 1:
            part = high[b, start : start + count, :]
        elif extent % 8 == 0:
            blank = jnp.zeros((extent, width), F32)
            if a == 0:
                part = jnp.concatenate([blank, high[b, start : start + count - extent, :]], axis=0)
            else:
                part = jnp.concatenate([high[b, start + extent : start + count, :], blank], axis=0)
        else:
            whole = high[b, start : start + count, :]
            at = iota((count, 1), 0)
            if a == 0:
                part = jnp.where(at < extent, 0.0, pltpu.roll(whole, extent, 0))
            else:
                part = jnp.where(at >= count - extent, 0.0, pltpu.roll(whole, count - extent, 0))
        target[row : row + count, lanes] = part.astype(BF16)


def shift_scratch(side, width):
    fine = side * side
    return [
        pltpu.VMEM((3, fine, width), BF16),
        pltpu.VMEM((3, rows_of(side) - fine, width), F32),
    ]


def dot(left, right):
    return lax.dot_general(left, right, (((1,), (0,)), ((), ())), preferred_element_type=F32)


def dot_last(left, right):
    return lax.dot_general(left, right, (((1,), (1,)), ((), ())), preferred_element_type=F32)


def block_of(index, extent):
    bits = extent.bit_length() - 1
    return ((index >> (bits + 1)) << (bits - 1)) + ((index & (extent - 1)) >> 1)


def pool_matrix(extent, value):
    count = extent * extent
    shape = (count // 4, count)
    return jnp.where(block_of(iota(shape, 1), extent) == iota(shape, 0), value, 0.0).astype(BF16)


def spread_matrix(extent):
    count = extent * extent
    shape = (count, count // 4)
    return jnp.where(block_of(iota(shape, 0), extent) == iota(shape, 1), 1.0, 0.0).astype(BF16)


def spread(matrix, value):
    high = value.astype(BF16)
    low = (value - high.astype(F32)).astype(BF16)
    return dot(matrix, high) + dot(matrix, low)


def gelu_and_slope(z):
    root = 0.7978845608028654
    inner = root * (z + 0.044715 * z * z * z)
    t = jnp.tanh(inner)
    half = 0.5 * (1.0 + t)
    slope = half + 0.5 * z * (1.0 - t * t) * (root * (1.0 + 3 * 0.044715 * z * z))
    return z * half, slope


def head_cotangents(cot, coarse_cot, weights):
    return jnp.concatenate(
        [
            (weights[0] * cot).astype(BF16),
            (weights[1] * cot).astype(BF16),
            (weights[2] * coarse_cot).astype(BF16),
        ],
        axis=0,
    )


def copies(pairs, sems):
    made = [
        pltpu.make_async_copy(source, target, sems.at[num])
        for num, (source, target) in enumerate(pairs)
    ]
    for one in made:
        one.start()
    return made


def tap_norm(tap):
    return lax.rsqrt(jnp.mean(tap * tap, axis=-1, keepdims=True) + EPSILON)


def tap_backward(tap, r, scale_row, back, wide, mid):
    back = jnp.concatenate([spread(wide, 0.25 * back[:mid]), back[mid:]], axis=0)
    upstream = back * scale_row
    grad = r * (upstream - tap * (r * r) * jnp.mean(upstream * tap, axis=-1, keepdims=True))
    return grad, jnp.sum(back * tap * r, axis=0, keepdims=True)


def section_kernel(
    side,
    dp,
    plan,
    features,
    trunk_weight,
    head_weight,
    cotangent,
    gain_in,
    shift_in,
    scale_in,
    merging_in,
    own_out,
    send_out,
    pass_out,
    grad_out,
    slope_out,
    normed_out,
    scale_out,
    feed,
    weights,
    heads,
    cot_ref,
    gain,
    shift,
    scale,
    merging,
    low_shifted,
    high_shifted,
    patch,
    sems,
):
    rows = rows_of(side)
    fine = side * side
    channels = feed.shape[1]
    half = channels // 2
    width = heads.shape[1]
    at = Layout(side, channels, width)
    mid = at.mid
    pipe = lax.axis_index("pipe")
    core = own_core(dp)
    pick = block_bits(dp, core, LATE)[0]
    made = copies(
        [(features.at[plan[0, pipe]], feed)]
        + [
            (
                trunk_weight.at[num // 3, pl.ds(num % 3 * 3 * channels, 3 * channels)],
                weights.at[num],
            )
            for num in range(6)
        ]
        + [(cotangent.at[pipe], cot_ref), (head_weight.at[1], heads)]
        + [(gain_in, gain), (shift_in, shift), (scale_in, scale), (merging_in, merging)],
        sems,
    )
    made[0].wait()

    def conv(value, layer):
        column_shifts(value, side, low_shifted, high_shifted)
        total = jnp.zeros((rows, channels), F32)
        for a in range(3):
            for b in range(3):
                put_row_shift(patch, 0, b * channels, low_shifted, high_shifted, b, a, side)
            made[1 + 3 * layer + a].wait()
            total = total + dot(patch[...], weights[3 * layer + a])
        return total

    def put_halves(first, value):
        count = value.shape[0]
        left = value[:, :half]
        right = value[:, half:]
        own_out[first : first + count, :] = jnp.where(core == 0, left, right)
        send_out[first : first + count, :] = jnp.where(core == 0, right, left)

    low_feed = feed[...]
    feed_value = low_feed.astype(F32)
    put_halves(at.feed, low_feed)
    first_pre = conv(feed_value, 0)
    for num in range(9, 13):
        made[num].wait()
    act1, slope1 = gelu_and_slope(gain[0:1, :] * first_pre + shift[0:1, :])
    slope_out[...] = slope1 * gain[0:1, :]
    low_act = act1.astype(BF16)
    put_halves(at.act, low_act)
    z2 = gain[1:2, :] * conv(low_act.astype(F32), 1) + shift[1:2, :]
    trunk_out, slope2 = gelu_and_slope(z2)
    taps = [feed_value, trunk_out.astype(BF16).astype(F32)]

    pool = pool_matrix(side, 0.25)
    for k in range(2):
        tap = taps[k]
        r = tap_norm(tap)
        normed = (tap * r * scale[k : k + 1, :]).astype(BF16)
        pooled = dot(pool, normed[:fine]).astype(BF16)
        rows_k = jnp.concatenate([pooled, normed[fine:]], axis=0)
        put_halves(at.normed + k * at.stacked, rows_k)
        normed_out[k] = rows_k
    made[7].wait()
    cot_low = cot_ref[...]
    coarse_cot = dot(pool_matrix(side // 2, 1.0), cot_low)
    grads = head_cotangents(
        cot_low.astype(F32), coarse_cot, [merging[s, 1:2, :] for s in range(3)]
    )
    made[8].wait()
    tap_grad, scale_row = tap_backward(
        tap, r, scale[1:2, :], dot_last(grads, heads[...]), spread_matrix(side), mid
    )
    scale_out[...] = jnp.broadcast_to(scale_row, scale_out.shape)
    grad2 = (tap_grad.astype(BF16).astype(F32) * slope2 * gain[1:2, :]).astype(BF16)
    for num in range(2):
        grad_out[num * rows : (num + 1) * rows, :] = grad2[:, num * half : (num + 1) * half]
    for target in (own_out, send_out):
        for num in range(2):
            target[at.grad[num] : at.grad[num] + rows, :] = grad2[:, num * half : (num + 1) * half]
        for num in range(at.lanes):
            lanes = slice(num * half, (num + 1) * half)
            target[at.cot + num * mid : at.cot + (num + 1) * mid, :] = cot_low[:, lanes]
    pass_out[...] = own_out[pl.ds(pl.multiple_of((1 - pick) * at.skip, 16), at.span), :]


def section(dp, plan, features, trunk_weight, head_weight, cotangent, gain, shift, scale, merging):
    side = SIDE
    rows = rows_of(side)
    channels = features.shape[2]
    half = channels // 2
    width = head_weight.shape[2]
    mid = cotangent.shape[1]
    at = Layout(side, channels, width)
    vmem = spec(pltpu.VMEM)
    return call(
        partial(section_kernel, side, dp),
        "section",
        60,
        1150000000,
        (plan, features, trunk_weight, head_weight, cotangent, gain, shift, scale, merging),
        [spec(pltpu.SMEM)] + [spec(pltpu.HBM)] * 8,
        (
            jax.ShapeDtypeStruct((at.total, half), BF16),
            jax.ShapeDtypeStruct((at.total, half), BF16),
            jax.ShapeDtypeStruct((at.span, half), BF16),
            jax.ShapeDtypeStruct((2 * rows, half), BF16),
            jax.ShapeDtypeStruct((rows, channels), F32),
            jax.ShapeDtypeStruct((2, at.stacked, channels), BF16),
            jax.ShapeDtypeStruct((8, channels), F32),
        ),
        (vmem,) * 7,
        [
            pltpu.VMEM((rows, channels), BF16),
            pltpu.VMEM((6, 3 * channels, channels), BF16),
            pltpu.VMEM((channels, width), BF16),
            pltpu.VMEM((mid, width), BF16),
            pltpu.VMEM(gain.shape, F32),
            pltpu.VMEM(shift.shape, F32),
            pltpu.VMEM(scale.shape, F32),
            pltpu.VMEM(merging.shape, F32),
            *shift_scratch(side, channels),
            pltpu.VMEM((rows, 3 * channels), BF16),
            pltpu.SemaphoreType.DMA((13,)),
        ],
    )


def back_kernel(side, layer, grad_in, trunk_weight, factor_in, *rest):
    grad, factor, weights, low_shifted, high_shifted, patch, sems = rest[-7:]
    channels = trunk_weight.shape[2]
    half = channels // 2
    rows = rows_of(side)
    made = copies(
        [(grad_in, grad)]
        + [
            (trunk_weight.at[layer, pl.ds(num * channels, channels)], weights.at[num])
            for num in range(9)
        ]
        + [(factor_in, factor)],
        sems,
    )
    made[0].wait()
    value = jnp.concatenate([grad[:rows, :], grad[rows:, :]], axis=1).astype(F32)
    column_shifts(value, side, low_shifted, high_shifted)
    total = jnp.zeros((rows, channels), F32)
    for a in range(3):
        for b in range(3):
            put_row_shift(
                patch, 0, b * channels, low_shifted, high_shifted, 2 - b, 2 - a, side
            )
        for b in range(3):
            made[1 + 3 * a + b].wait()
            total = total + dot_last(
                patch[:, b * channels : (b + 1) * channels], weights[3 * a + b]
            )
    made[10].wait()
    if layer == 1:
        (grad_out,) = rest[:-7]
        low = (total * factor[...]).astype(BF16)
        grad_out[:rows, :] = low[:, :half]
        grad_out[rows:, :] = low[:, half:]
        return
    merged, own_out, send_out = rest[:-7]
    pipe = lax.axis_index("pipe")
    total = total + factor[...]
    left, right = total[:, :half], total[:, half:]
    own_out[...] = jnp.where(pipe == 0, left, right)
    sent = jnp.where(pipe == 0, right, left).astype(BF16)
    low_merged = merged[...]
    mid, width = low_merged.shape
    sent_merged = jnp.where(
        pipe == 0, low_merged[:, width // 2 :], low_merged[:, : width // 2]
    )
    for num in range(half // 128):
        send_out[num * rows : (num + 1) * rows, :] = sent[:, num * 128 : (num + 1) * 128]
    first = half // 128 * rows
    for num in range(width // 256):
        send_out[first + num * mid : first + (num + 1) * mid, :] = sent_merged[
            :, num * 128 : (num + 1) * 128
        ]


def back(layer, grad, trunk_weight, factor, merged=None, after=()):
    side = SIDE
    rows = rows_of(side)
    channels = trunk_weight.shape[2]
    half = channels // 2
    vmem = spec(pltpu.VMEM)
    hbm = spec(pl.ANY)
    in_specs = [hbm, spec(pltpu.HBM), hbm]
    operands = [grad, trunk_weight, factor]
    if layer == 0:
        in_specs.append(vmem)
        operands.append(merged)
        out_shape = (
            jax.ShapeDtypeStruct((rows, half), F32),
            jax.ShapeDtypeStruct((half // 128 * rows + merged.size // 256, 128), BF16),
        )
        out_specs = (vmem, vmem)
    else:
        out_shape = jax.ShapeDtypeStruct((2 * rows, half), BF16)
        out_specs = vmem
    return call(
        partial(back_kernel, side, layer),
        "back",
        60 if layer else 46,
        350000000,
        operands,
        in_specs,
        out_shape,
        out_specs,
        [
            pltpu.VMEM((2 * rows, half), BF16),
            pltpu.VMEM((rows, channels), F32),
            pltpu.VMEM((9, channels, channels), BF16),
            *shift_scratch(side, channels),
            pltpu.VMEM((rows, 3 * channels), BF16),
            pltpu.SemaphoreType.DMA((11,)),
        ],
        after,
    )


def move_kernel(moves, *refs):
    sources, out, sems = refs[:-2], refs[-2], refs[-1]
    made = copies(
        [
            (sources[num].at[first()], out.at[pl.ds(place, count)])
            for num, first, place, count in moves
        ],
        sems,
    )
    for one in made:
        one.wait()


def far_factors(dp, other, side, width, after):
    half = other.shape[1]
    at = Layout(side, 2 * half, width)

    def rows():
        pick = block_bits(dp, own_core(dp), LATE)[0]
        return pl.ds(pl.multiple_of((1 - pick) * at.skip, 16), at.span)

    return call(
        partial(move_kernel, [(0, rows, 0, at.span)]),
        "far_factors",
        4,
        30000000,
        (other,),
        [spec(pl.ANY)],
        jax.ShapeDtypeStruct((at.span, half), BF16),
        spec(pltpu.VMEM),
        [pltpu.SemaphoreType.DMA((1,))],
        after,
    )


def first_factors(dp, own, other, own_grad, other_grad, side, width, after):
    half = other.shape[1]
    at = Layout(side, 2 * half, width)

    def feed():
        return pl.ds(at.feed, at.rows)

    def grad():
        pick = block_bits(dp, own_core(dp), EARLY)[0]
        return pl.ds(pl.multiple_of((1 - pick) * at.rows, 16), at.rows)

    return call(
        partial(
            move_kernel,
            [
                (num, (feed, feed, grad, grad)[num], num * at.rows, at.rows)
                for num in range(4)
            ],
        ),
        "first_factors",
        4,
        90000000,
        (own, other, own_grad, other_grad),
        [spec(pl.ANY)] * 4,
        jax.ShapeDtypeStruct((4 * at.rows, half), BF16),
        spec(pltpu.VMEM),
        [pltpu.SemaphoreType.DMA((4,))],
        after,
    )


def put_trunk_blocks(dp, piece, send, keep, xs, gs, low, high, patch, side, wait_x, wait_g):
    rows = rows_of(side)
    half = xs.shape[1]
    quarter = half // 2
    _, second, third = block_bits(dp, own_core(dp), piece)
    for image in range(4):
        wait_g(image)
        column_shifts(gs[image * rows : (image + 1) * rows, :].astype(F32), side, low, high)
        for a in range(3):
            for b in range(3):
                put_row_shift(
                    patch, image * rows, (3 * a + b) * half, low, high, 2 - b, 2 - a, side
                )
    for image in range(4):
        wait_x(image)
    turned = xs[...].T
    for offset in range(9):
        product = dot(turned, patch[:, offset * half : (offset + 1) * half]).astype(BF16)
        left, right = product[:, :128], product[:, 128:]
        for target, value in (
            (keep, jnp.where(second == 0, left, right)),
            (send, jnp.where(second == 0, right, left)),
        ):
            upper, lower = value[:quarter], value[quarter:]
            row = offset * quarter
            target[row : row + quarter, :] = jnp.where(third == 0, upper, lower)
            row += 9 * quarter
            target[row : row + quarter, :] = jnp.where(third == 0, lower, upper)


def late_grads_kernel(
    side, dp, width, own, other, near, far, send, keep, xs, gs, low, high, patch, sems
):
    half = xs.shape[1]
    at = Layout(side, 2 * half, width)
    rows = at.rows
    pick = block_bits(dp, own_core(dp), LATE)[0]
    grad_at = pick * at.grad[1]
    pairs = []
    for num, source in enumerate((own, other, near, far)):
        back_by = 0 if num < 2 else pick * at.skip

        def some(first):
            return source.at[pl.ds(pl.multiple_of(first - back_by, 16), rows)]

        pairs += [
            (some(grad_at), gs.at[pl.ds(num * rows, rows)]),
            (some(at.act), xs.at[pl.ds(num * rows, rows)]),
        ]
    made = copies(pairs, sems)
    put_trunk_blocks(
        dp,
        LATE,
        send,
        keep,
        xs,
        gs,
        low,
        high,
        patch,
        side,
        lambda image: made[2 * image + 1].wait(),
        lambda image: made[2 * image].wait(),
    )


def split_pair(value):
    high = value.astype(BF16).astype(F32)
    return jnp.concatenate([high, value - high], axis=0).astype(BF16)


def trunk_scratch(rows, half):
    return shift_scratch(SIDE, half) + [pltpu.VMEM((4 * rows, 9 * half), BF16)]


def late_grads(dp, width, own, other, near, far, after):
    side = SIDE
    rows = rows_of(side)
    half = own.shape[1]
    vmem = spec(pltpu.VMEM)
    shape = jax.ShapeDtypeStruct((9 * half, 128), BF16)
    return call(
        partial(late_grads_kernel, side, dp, width),
        "late_grads",
        28,
        430000000,
        (own, other, near, far),
        [spec(pl.ANY)] * 4,
        (shape, shape),
        (vmem, vmem),
        [
            pltpu.VMEM((4 * rows, half), BF16),
            pltpu.VMEM((4 * rows, half), BF16),
            *trunk_scratch(rows, half),
            pltpu.SemaphoreType.DMA((8,)),
        ],
        after,
    )


def early_grads_kernel(
    side, dp, width, own, other, own_g, other_g, far, send, keep, xs, gs, low, high, patch, sems
):
    half = xs.shape[1]
    at = Layout(side, 2 * half, width)
    rows = at.rows
    pick = block_bits(dp, own_core(dp), EARLY)[0]
    mine = pl.ds(pl.multiple_of(pick * rows, 16), rows)
    made = copies(
        [
            (own_g.at[mine], gs.at[pl.ds(0, rows)]),
            (other_g.at[mine], gs.at[pl.ds(rows, rows)]),
            (far.at[pl.ds(2 * rows, 2 * rows)], gs.at[pl.ds(2 * rows, 2 * rows)]),
            (own.at[pl.ds(at.feed, rows)], xs.at[pl.ds(0, rows)]),
            (other.at[pl.ds(at.feed, rows)], xs.at[pl.ds(rows, rows)]),
            (far.at[pl.ds(0, 2 * rows)], xs.at[pl.ds(2 * rows, 2 * rows)]),
        ],
        sems,
    )
    put_trunk_blocks(
        dp,
        EARLY,
        send,
        keep,
        xs,
        gs,
        low,
        high,
        patch,
        side,
        lambda image: made[3 + image].wait() if image < 3 else None,
        lambda image: made[image].wait() if image < 3 else None,
    )


def early_grads(dp, width, own, other, own_g, other_g, far, after):
    side = SIDE
    rows = rows_of(side)
    half = own.shape[1]
    vmem = spec(pltpu.VMEM)
    shape = jax.ShapeDtypeStruct((9 * half, 128), BF16)
    return call(
        partial(early_grads_kernel, side, dp, width),
        "early_grads",
        28,
        370000000,
        (own, other, own_g, other_g, far),
        [spec(pl.ANY)] * 5,
        (shape, shape),
        (vmem, vmem),
        [
            pltpu.VMEM((4 * rows, half), BF16),
            pltpu.VMEM((4 * rows, half), BF16),
            *trunk_scratch(rows, half),
            pltpu.SemaphoreType.DMA((6,)),
        ],
        after,
    )


def head_grads_kernel(
    side,
    dp,
    plan,
    features,
    head_weight,
    normed_in,
    scale_in,
    last_scale_in,
    own,
    other,
    merging_in,
    send,
    keep,
    merged_out,
    tap_grad_out,
    feed,
    heads,
    normed,
    scale,
    last_scale,
    ns,
    cots,
    merging,
    sems,
):
    half = ns.shape[2]
    width = merging.shape[2]
    at = Layout(side, 2 * half, width)
    mid = at.mid
    quarter = half // 2
    pick, second, third = block_bits(dp, own_core(dp), HEAD)
    pairs = [(merging_in, merging)]
    for num, source in enumerate((own, other)):
        pairs += [
            (source.at[pl.ds(at.cot, at.lanes * mid)], cots.at[num]),
            (source.at[pl.ds(at.normed, 2 * at.stacked)], ns.at[num]),
        ]
    pairs += [(normed_in, normed), (head_weight.at[0], heads.at[0])]
    pairs += [(features.at[plan[0, lax.axis_index("pipe")]], feed), (scale_in, scale)]
    pairs += [(last_scale_in, last_scale), (head_weight.at[1], heads.at[1])]
    made = copies(pairs, sems)
    sums = pool_matrix(side // 2, 1.0)
    cotangents = []
    for image in range(2):
        made[1 + 2 * image].wait()
        cot_low = jnp.concatenate(
            [cots[image, num * mid : (num + 1) * mid, :] for num in range(at.lanes)], axis=1
        )
        cotangents.append((cot_low.astype(F32), dot(sums, cot_low)))
    for one in (made[0], made[2], made[4]):
        one.wait()
    for target, tap in ((send, 1 - pick), (keep, pick)):
        weights = [merging[s, pl.ds(tap, 1), :] for s in range(3)]
        grads = [head_cotangents(cot, coarse, weights) for cot, coarse in cotangents]
        first = pl.multiple_of(tap * at.stacked, 16)
        both = [ns[image, pl.ds(first, at.stacked), :] for image in range(2)]
        product = dot(
            jnp.concatenate(both, axis=0).T, jnp.concatenate(grads, axis=0)
        ).astype(BF16)
        for lane in range(2):
            for num in range(width // 256):
                column = lane * (width // 2) + num * 128
                for part in range(2):
                    row = ((lane ^ second) * 2 + (part ^ third)) * (width // 256) + num
                    target[pl.ds(pl.multiple_of(row * quarter, quarter), quarter), :] = product[
                        part * quarter : (part + 1) * quarter, column : column + 128
                    ]
    cot, coarse_cot = cotangents[0]
    merged = jnp.zeros((mid, width), F32)
    coarse_merged = jnp.zeros((at.stacked - 2 * mid, width), F32)
    small = []
    made[5].wait()
    for k in range(2):
        made[6 if k == 0 else 10].wait()
        weights = [merging[s, k : k + 1, :] for s in range(3)]
        product = dot(normed[k], heads[k])
        merged = merged + weights[0] * product[:mid] + weights[1] * product[mid : 2 * mid]
        coarse_merged = coarse_merged + weights[2] * product[2 * mid :]
        small.append(jnp.sum(cot * product[:mid], axis=0, keepdims=True))
        small.append(jnp.sum(cot * product[mid : 2 * mid], axis=0, keepdims=True))
        small.append(jnp.sum(coarse_cot * product[2 * mid :], axis=0, keepdims=True))
        if k == 0:
            for one in made[7:10]:
                one.wait()
            tap = feed[...].astype(F32)
            back = dot_last(head_cotangents(cot, coarse_cot, weights), heads[0])
            tap_grad_out[...], scale_row = tap_backward(
                tap, tap_norm(tap), scale[0:1, :], back, spread_matrix(side), mid
            )
    merged = merged + spread(spread_matrix(side // 2), coarse_merged)
    merged_out[...] = merged.astype(BF16)
    small.append(
        jnp.concatenate(
            [scale_row, last_scale[0:1, :], jnp.zeros((1, width - 4 * half), F32)], axis=1
        )
    )
    small.append(jnp.zeros((1, width), F32))
    pair = split_pair(jnp.concatenate(small, axis=0))
    first = width // 128 * half
    for num in range(width // 128):
        for target in (send, keep):
            target[first + num * 16 : first + (num + 1) * 16, :] = pair[
                :, num * 128 : (num + 1) * 128
            ]


def head_grads(
    dp, plan, features, head_weight, normed, scale, last_scale, own, other, merging, after
):
    side = SIDE
    rows = rows_of(side)
    half = own.shape[1]
    width = merging.shape[2]
    at = Layout(side, 2 * half, width)
    shape = jax.ShapeDtypeStruct((width // 128 * half + 16 * width // 128, 128), BF16)
    vmem = spec(pltpu.VMEM)
    return call(
        partial(head_grads_kernel, side, dp),
        "head_grads",
        40,
        610000000,
        (plan, features, head_weight, normed, scale, last_scale, own, other, merging),
        [spec(pltpu.SMEM), spec(pltpu.HBM), spec(pltpu.HBM), spec(pl.ANY), spec(pltpu.HBM)]
        + [spec(pl.ANY)] * 3
        + [spec(pltpu.HBM)],
        (
            shape,
            shape,
            jax.ShapeDtypeStruct((at.mid, width), BF16),
            jax.ShapeDtypeStruct((rows, 2 * half), F32),
        ),
        (vmem,) * 4,
        [
            pltpu.VMEM((rows, 2 * half), BF16),
            pltpu.VMEM((2, 2 * half, width), BF16),
            pltpu.VMEM((2, at.stacked, 2 * half), BF16),
            pltpu.VMEM(scale.shape, F32),
            pltpu.VMEM(last_scale.shape, F32),
            pltpu.VMEM((2, 2 * at.stacked, half), BF16),
            pltpu.VMEM((2, at.lanes * at.mid, half), BF16),
            pltpu.VMEM(merging.shape, F32),
            pltpu.SemaphoreType.DMA((11,)),
        ],
        after,
    )


def held_back(array, after):
    def kernel(*refs):
        pass

    hbm = spec(pl.ANY)
    shape = jax.ShapeDtypeStruct(array.shape, array.dtype)
    return call(kernel, "held_back", 4, 1024, (array,), [hbm], shape, hbm, (), after, {0: 0})


def add_tails(one, two):
    count = one.shape[0] // 16
    one = one.astype(F32).reshape(count, 16, 128)
    two = two.astype(F32).reshape(count, 16, 128)
    total = (one[:, :8] + one[:, 8:]) + (two[:, :8] + two[:, 8:])
    high = total.astype(BF16).astype(F32)
    return jnp.concatenate([high, total - high], axis=1).reshape(count * 16, 128).astype(BF16)


def sum_kernel(tail, keep, received, *outs):
    rows = keep.shape[0] - tail
    size = rows // len(outs)
    for num, out in enumerate(outs):
        part = slice(num * size, (num + 1) * size)
        out[:size, :] = (keep[part, :].astype(F32) + received[part, :].astype(F32)).astype(BF16)
    if tail:
        total = add_tails(keep[rows:, :], received[rows:, :])
        for out in outs:
            out[size:, :] = total


def summed(keep, received, parts, tail, after):
    vmem = spec(pltpu.VMEM)
    shape = jax.ShapeDtypeStruct(((keep.shape[0] - tail) // parts + tail, 128), BF16)
    return call(
        partial(sum_kernel, tail),
        "summed",
        4,
        10000000,
        (keep, received),
        [vmem, vmem],
        (shape,) * parts,
        (vmem,) * parts,
        (),
        after,
    )


def pair_kernel(one, two, out):
    rows = out.shape[0] // 2
    out[:rows, :] = one[:rows, :]
    out[rows:, :] = two[:rows, :]


def paired(one, two, rows, after):
    vmem = spec(pltpu.VMEM)
    return call(
        pair_kernel,
        "paired",
        4,
        10000000,
        (one, two),
        [vmem, vmem],
        jax.ShapeDtypeStruct((2 * rows, 128), BF16),
        vmem,
        (),
        after,
    )


def widen_trunk_kernel(dp, layer, half, kinds, *refs):
    sources = refs[: len(kinds)]
    out, held, wide, sems_in, sems_out = refs[-5:]
    quarter = half // 2
    size = 9 * quarter
    jobs = []
    coming = []
    for source, (is_other, is_new) in zip(sources, kinds):
        core = own_core(dp) ^ int(is_other)
        first, second, third = block_bits(dp, core, LATE if layer else EARLY)
        first = first ^ int(is_new)
        for part in range(2):
            for lane in range(2):
                row = pl.multiple_of(((lane ^ second) * 2 + part) * size, size)
                coming.append((source.at[pl.ds(row, size)], held.at[len(jobs), lane]))
            jobs.append((core * half + (part ^ third) * quarter, first * half))
    made = copies(coming, sems_in)
    going = []
    for num, (row, column) in enumerate(jobs):
        for lane in range(2):
            made[2 * num + lane].wait()
            for offset in range(9):
                wide[num, offset, :, lane * 128 : (lane + 1) * 128] = held[
                    num, lane, offset * quarter : (offset + 1) * quarter, :
                ].astype(F32)
        one = pltpu.make_async_copy(
            wide.at[num],
            out.at[
                layer,
                :,
                pl.ds(pl.multiple_of(row, quarter), quarter),
                pl.ds(pl.multiple_of(column, half), half),
            ],
            sems_out.at[num],
        )
        one.start()
        going.append(one)
    for one in going:
        one.wait()


def widen_trunk(dp, layer, layers, half, sources, kinds, before=None, after=()):
    hbm = spec(pl.ANY)
    operands = list(sources) + ([before] if before is not None else [])
    count = 2 * len(kinds)
    return call(
        partial(widen_trunk_kernel, dp, layer, half, kinds),
        "widen_trunk",
        24,
        290000000,
        operands,
        [hbm] * len(operands),
        jax.ShapeDtypeStruct((layers, 9, 2 * half, 2 * half), F32),
        hbm,
        [
            pltpu.VMEM((count, 2, 9 * half // 2, 128), BF16),
            pltpu.VMEM((count, 9, half // 2, half), F32),
            pltpu.SemaphoreType.DMA((2 * count,)),
            pltpu.SemaphoreType.DMA((count,)),
        ],
        after,
        {len(sources): 0} if before is not None else None,
    )


def widen_heads_kernel(dp, half, kinds, *refs):
    sources = refs[: len(kinds)]
    out, held, wide, sems_in, sems_out = refs[-5:]
    quarter = half // 2
    size = held.shape[2]
    width = wide.shape[2]
    jobs = []
    coming = []
    for source, (is_other, is_new) in zip(sources, kinds):
        core = own_core(dp) ^ int(is_other)
        first, second, third = block_bits(dp, core, HEAD)
        for lane in range(2):
            for part in range(2):
                row = pl.multiple_of(((lane ^ second) * 2 + (part ^ third)) * size, size)
                coming.append((source.at[pl.ds(row, size)], held.at[len(jobs), part]))
            jobs.append((first ^ int(is_new), core * half, lane * width))
    made = copies(coming, sems_in)
    going = []
    for num, (tap, row, column) in enumerate(jobs):
        for part in range(2):
            made[2 * num + part].wait()
            for piece in range(width // 128):
                wide[
                    num, part * quarter : (part + 1) * quarter, piece * 128 : (piece + 1) * 128
                ] = held[num, part, piece * quarter : (piece + 1) * quarter, :].astype(F32)
        one = pltpu.make_async_copy(
            wide.at[num],
            out.at[tap, pl.ds(pl.multiple_of(row, half), half), pl.ds(column, width)],
            sems_out.at[num],
        )
        one.start()
        going.append(one)
    for one in going:
        one.wait()


def widen_heads(dp, half, width, sources, kinds, before=None, after=()):
    hbm = spec(pl.ANY)
    operands = list(sources) + ([before] if before is not None else [])
    count = 2 * len(kinds)
    return call(
        partial(widen_heads_kernel, dp, half, kinds),
        "widen_heads",
        40,
        440000000,
        operands,
        [hbm] * len(operands),
        jax.ShapeDtypeStruct((2, 2 * half, width), F32),
        hbm,
        [
            pltpu.VMEM((count, 2, width // 256 * half // 2, 128), BF16),
            pltpu.VMEM((count, half, width // 2), F32),
            pltpu.SemaphoreType.DMA((2 * count,)),
            pltpu.SemaphoreType.DMA((count,)),
        ],
        after,
        {len(sources): 0} if before is not None else None,
    )


def finish_kernel(
    dp, tail, plan, own_feed, merged, received, own_sum, other_sum,
    merged_out, feed_out, scale_out, merging_out,
    feeds, maps, ours, theirs, scales, weights, sems,
):
    rows, half = own_feed.shape
    mid, width = merged.shape
    first = own_sum.shape[0] - tail
    pipe = lax.axis_index("pipe")
    slot = plan[0, pipe]
    made = copies(
        [
            (own_feed, feed_out.at[slot]),
            (own_sum.at[pl.ds(first, tail)], ours),
            (other_sum.at[pl.ds(first, tail)], theirs),
        ],
        sems,
    )
    for num in range(half // 128):
        feeds[:, num * 128 : (num + 1) * 128] = received[
            num * rows : (num + 1) * rows, :
        ].astype(F32)
    low_merged = merged[...]
    maps[0] = jnp.where(pipe == 0, low_merged[:, : width // 2], low_merged[:, width // 2 :])
    first = half // 128 * rows
    for num in range(width // 256):
        maps[1, :, num * 128 : (num + 1) * 128] = received[
            first + num * mid : first + (num + 1) * mid, :
        ]
    going = [
        pltpu.make_async_copy(feeds, feed_out.at[1 - slot], sems.at[3]),
        pltpu.make_async_copy(maps.at[0], merged_out.at[pipe], sems.at[4]),
        pltpu.make_async_copy(maps.at[1], merged_out.at[1 - pipe], sems.at[5]),
    ]
    for one in going:
        one.start()
    made[1].wait()
    made[2].wait()
    total = ours[...].astype(F32) + theirs[...].astype(F32)
    for num in range(width // 128):
        lanes = slice(num * 128, (num + 1) * 128)
        block = total[num * 16 : num * 16 + 8] + total[num * 16 + 8 : num * 16 + 16]
        for k in range(2):
            for s in range(3):
                weights[s, k : k + 1, lanes] = block[3 * k + s : 3 * k + s + 1]
            column = num * 128 - k * 2 * half
            if 0 <= column < 2 * half:
                scales[k : k + 1, column : column + 128] = block[6:7]
    going += [
        pltpu.make_async_copy(scales, scale_out, sems.at[6]),
        pltpu.make_async_copy(weights, merging_out, sems.at[7]),
    ]
    for one in going[3:]:
        one.start()
    for one in going + made[:1]:
        one.wait()


def finish(dp, plan, own_feed, merged, received, own_sum, other_sum, after):
    rows, half = own_feed.shape
    mid, width = merged.shape
    vmem = spec(pltpu.VMEM)
    hbm = spec(pl.ANY)
    tail = 16 * width // 128
    return call(
        partial(finish_kernel, dp, tail),
        "finish",
        8,
        170000000,
        (plan, own_feed, merged, received, own_sum, other_sum),
        [spec(pltpu.SMEM), hbm, vmem, vmem, hbm, hbm],
        (
            jax.ShapeDtypeStruct((2, mid, width // 2), BF16),
            jax.ShapeDtypeStruct((2, rows, half), F32),
            jax.ShapeDtypeStruct((2, 2 * half), F32),
            jax.ShapeDtypeStruct((3, 2, width), F32),
        ),
        (hbm,) * 4,
        [
            pltpu.VMEM((rows, half), F32),
            pltpu.VMEM((2, mid, width // 2), BF16),
            pltpu.VMEM((tail, 128), BF16),
            pltpu.VMEM((tail, 128), BF16),
            pltpu.VMEM((2, 2 * half), F32),
            pltpu.VMEM((3, 2, width), F32),
            pltpu.SemaphoreType.DMA((8,)),
        ],
        after,
    )


ORDER = (
    "back1",
    "far",
    "first",
    "head",
    "late",
    "early",
    "L2",
    "E2",
    "H1",
    "L3",
    "E3",
    "H2",
    "back0",
    "L4",
    "E4",
    "H3",
    "L5",
    "E5",
    "H4",
    "L6",
    "E6",
    "H5",
    "Lold_wide",
    "Eold_wide",
    "H6",
    "Lnew",
    "Lnew_own",
    "Hold_wide",
    "Enew",
    "Lnew_other",
    "Enew_own",
    "finish",
    "Hnew",
    "Enew_other",
    "Hnew_own",
    "Hnew_other",
)
WAITS = {"far": ("near",), "L6": ("feed",)}


class Sum:
    def __init__(self, swap, piece, last, send, keep, tail=0):
        self.swap = partial(swap, piece)
        self.tail = tail
        self.steps = [("scatter", stage) for stage in range(0 if piece == HEAD else 1, 3)]
        self.steps += [("whole", stage) for stage in range(3, last + 1)]
        self.steps += [("gather", stage) for stage in (2, 1, 0)]
        self.at = 0
        self.keep = keep
        self.come = self.swap(self.steps[0][1], send)

    def advance(self, after):
        kind = self.steps[self.at][0]
        self.at += 1
        following, stage = self.steps[self.at]
        if kind == "gather":
            rows = self.keep.shape[0] - self.tail
            self.keep, mark = paired(self.keep, self.come, rows, after)
            self.tail = 0
            send = self.keep
        else:
            parts = 2 if following == "scatter" else 1
            made, mark = summed(self.keep, self.come, parts, self.tail, after)
            self.keep = made[0]
            send = made[-1]
            if following == "gather":
                self.final = self.keep
        self.come = self.swap(stage, send)
        return mark


def body(
    features,
    plan,
    trunk_weight,
    trunk_gain,
    trunk_shift,
    head_weight,
    norm_scale,
    merging_weight,
    merged_cotangent,
):
    dp = lax.axis_size("dp")
    devices = lax.axis_size("pipe") * dp
    layers = trunk_weight.shape[0]
    channels = features.shape[2]
    half = channels // 2
    width = head_weight.shape[2]
    last = dp.bit_length() - 2
    weights = trunk_weight.reshape(layers, 9 * channels, channels)
    merging = jnp.transpose(merging_weight, (1, 0, 2))
    tail = 16 * width // 128

    def swap(piece, stage, block):
        bits = stage_bits(dp, piece)[stage]
        route = [(i, i ^ (1 << bits[i & 1])) for i in range(devices)]
        return lax.ppermute(block, AXES, route)

    def swap_cores(block):
        return lax.ppermute(block, AXES, [(i, i ^ 1) for i in range(devices)])

    (own, send, passed, grad2, slope, normed, last_scale), mark = section(
        dp,
        plan,
        features,
        weights,
        head_weight,
        merged_cotangent,
        trunk_gain,
        trunk_shift,
        norm_scale,
        merging,
    )
    other = swap_cores(send)
    near = swap(LATE, 0, passed)
    kept = ((False, False), (True, False))
    came = ((False, True), (True, True))
    got = {"before": None, "heads": None}
    pieces = {}

    def make_back1(after):
        got["grad1"], mark = back(1, grad2, weights, slope, None, after)
        got["other_grad1"] = swap_cores(got["grad1"])
        return mark

    def make_far(after):
        passed, mark = far_factors(dp, other, SIDE, width, after)
        got["far"] = swap(LATE, 0, passed)
        return mark

    def make_first(after):
        grads = (got["grad1"], got["other_grad1"])
        passed, mark = first_factors(dp, own, other, *grads, SIDE, width, after)
        got["first"] = swap(EARLY, 0, passed)
        return mark

    def make_head(after):
        blocks, mark = head_grads(
            dp,
            plan,
            features,
            head_weight,
            normed,
            norm_scale,
            last_scale,
            own,
            other,
            merging,
            after,
        )
        pieces["H"] = Sum(swap, HEAD, last, *blocks[:2], tail)
        got["maps"], got["tap_grad"] = blocks[2:]
        return mark

    def make_late(after):
        blocks, mark = late_grads(dp, width, own, other, near, got["far"], after)
        pieces["L"] = Sum(swap, LATE, last, *blocks)
        return mark

    def make_early(after):
        grads = (got["grad1"], got["other_grad1"])
        blocks, mark = early_grads(dp, width, own, other, *grads, got["first"], after)
        pieces["E"] = Sum(swap, EARLY, last, *blocks)
        return mark

    def make_back0(after):
        (got["feed"], sent), mark = back(
            0, got["grad1"], weights, got["tap_grad"], got["maps"], after
        )
        got["received"] = lax.ppermute(sent, "pipe", [(0, 1), (1, 0)])
        return mark

    def make_finish(after):
        sums = (pieces["H"].final, swap_cores(pieces["H"].final))
        got["finish"], mark = finish(
            dp, plan, got["feed"], got["maps"], got["received"], *sums, after
        )
        return mark

    def widen(name, sources, kinds, after):
        if name == "H":
            got["heads"], mark = widen_heads(
                dp, half, width, sources, kinds, got["heads"], after
            )
        else:
            layer = 1 if name == "L" else 0
            got["before"], mark = widen_trunk(
                dp, layer, layers, half, sources, kinds, got["before"], after
            )
        return mark

    make = {
        "back1": make_back1,
        "far": make_far,
        "first": make_first,
        "head": make_head,
        "late": make_late,
        "early": make_early,
        "back0": make_back0,
        "finish": make_finish,
    }
    for step in ORDER:
        name, kind = step[0], step[1:]
        waits = [mark]
        for which in WAITS.get(step, ()):
            come = {"near": near, "far": got.get("far"), "first": got.get("first")}
            come["feed"] = got.get("received")
            waits.append(pieces[which].come if which in pieces else come[which])
        if step in make:
            mark = make[step](waits)
        elif kind == "new":
            pieces[name].come, mark = held_back(pieces[name].come, waits)
            got[name] = swap_cores(pieces[name].come)
        elif kind == "old_wide":
            sources = (pieces[name].keep, swap_cores(pieces[name].keep))
            mark = widen(name, sources, kept, waits)
        elif kind == "new_wide":
            mark = widen(name, (pieces[name].come, got[name]), came, waits)
        elif kind == "new_own":
            mark = widen(name, (pieces[name].come,), came[:1], waits)
        elif kind == "new_other":
            mark = widen(name, (got[name],), came[1:], waits)
        else:
            mark = pieces[name].advance(waits)
            if kind == "4":
                for _ in range(3, last):
                    mark = pieces[name].advance([mark])
    merged_maps, features_grad, scale_grad, merging_grad = got["finish"]
    return (
        merged_maps,
        features_grad,
        got["before"].reshape(trunk_weight.shape),
        got["heads"],
        scale_grad,
        jnp.transpose(merging_grad, (1, 0, 2)),
    )


def solution(mesh):
    placed = (P("dp", None, None), P("dp", None), P(), P(), P(), P(), P(), P(), P("dp", None, None))
    return jax.shard_map(
        body,
        mesh=mesh,
        in_specs=placed,
        out_specs=(P("dp", None, "pipe"), P("dp", None, "pipe"), P(), P(), P(), P()),
        check_vma=False,
    )
```

```python
from functools import partial

import jax
import jax.numpy as jnp
from jax import lax
from jax.experimental import pallas as pl
from jax.experimental.pallas import tpu as pltpu
from jax.sharding import PartitionSpec as P

SIDE = 16
EPSILON = 1e-06
F32 = jnp.float32
BF16 = jnp.bfloat16
AXES = ("pipe", "dp")
MIB = 1024 * 1024


def device_index(dp):
    return lax.axis_index("pipe") * dp + lax.axis_index("dp")


HEAD, LATE, EARLY = 0, 1, 2


def stage_bits(dp, piece):
    size = dp.bit_length() - 1
    one, two, three, four = 1, size, 2, 3
    if piece == HEAD:
        stages = [(two, three), (one, two), (three, one), (four, four)]
    elif piece == LATE:
        stages = [(two, three), (one, two), (three, one), (four, four)]
    else:
        stages = [(one, three), (two, one), (three, two), (four, four)]
    return stages + [(bit, bit) for bit in range(4, size)]


def block_bits(dp, core, piece):
    index = device_index(dp)
    return [
        jnp.where(core == 0, (index >> first) & 1, (index >> second) & 1)
        for first, second in stage_bits(dp, piece)[:3]
    ]


def own_core(dp):
    return device_index(dp) & 1


class Layout:
    def __init__(self, side, channels, width):
        rows = rows_of(side)
        self.rows = rows
        self.mid = (side // 2) ** 2
        self.stacked = 2 * self.mid + (side // 4) ** 2
        self.lanes = width // (channels // 2)
        self.act = rows
        self.skip = rows
        self.span = 2 * rows
        self.grad = (0, self.span)
        self.normed = self.span + rows
        self.cot = self.normed + 2 * self.stacked
        self.feed = self.cot + self.lanes * self.mid
        self.total = self.feed + rows


def spec(memory):
    return pl.BlockSpec(memory_space=memory)


def call(kernel, name, mib, cost, operands, in_specs, out_shape, out_specs, scratch=(), after=(), aliases=None):
    count = len(operands)
    extra = len(after)
    several = isinstance(out_shape, tuple)
    shapes = out_shape if several else (out_shape,)
    specs = out_specs if several else (out_specs,)

    def run(*refs):
        results = refs[count + extra :]
        mark = results[len(shapes)]
        kernel(*refs[:count], *results[: len(shapes)], *results[len(shapes) + 1 :])
        mark[...] = jnp.zeros(mark.shape, F32)

    *made, mark = pl.pallas_call(
        run,
        out_shape=(*shapes, jax.ShapeDtypeStruct((8, 128), F32)),
        in_specs=list(in_specs) + [spec(pl.ANY)] * extra,
        out_specs=(*specs, spec(pltpu.VMEM)),
        scratch_shapes=list(scratch),
        input_output_aliases=aliases or {},
        compiler_params=pltpu.CompilerParams(vmem_limit_bytes=mib * MIB),
        cost_estimate=pl.CostEstimate(flops=cost, bytes_accessed=1024, transcendentals=0),
        name=name,
    )(*operands, *after)
    return (tuple(made) if several else made[0]), mark


def grids(side):
    first = 0
    found = []
    for extent in (side, side // 2, side // 4):
        found.append((first, extent))
        first += extent * extent
    return found


def rows_of(side):
    return side * side + (side // 2) ** 2 + (side // 4) ** 2


def iota(shape, dim):
    return lax.broadcasted_iota(jnp.int32, shape, dim)


def edge_masks(side):
    row = iota((rows_of(side), 1), 0)
    first = jnp.zeros(row.shape, jnp.bool_)
    last = jnp.zeros(row.shape, jnp.bool_)
    for start, extent in grids(side):
        inside = (row >= start) & (row < start + extent * extent)
        column = (row - start) & (extent - 1)
        first = first | (inside & (column == 0))
        last = last | (inside & (column == extent - 1))
    return first, last


def column_shifts(value, side, low, high):
    first, last = edge_masks(side)
    rows = value.shape[0]
    fine = side * side
    for b, one in enumerate(
        (
            jnp.where(first, 0.0, pltpu.roll(value, 1, 0)),
            value,
            jnp.where(last, 0.0, pltpu.roll(value, rows - 1, 0)),
        )
    ):
        low[b] = one[:fine].astype(BF16)
        high[b] = one[fine:]


def put_row_shift(target, row_start, lane_start, low, high, b, a, side):
    width = low.shape[2]
    lanes = slice(lane_start, lane_start + width)
    fine = side * side
    for start, extent in grids(side):
        count = extent * extent
        row = row_start + start
        if start == 0:
            blank = jnp.zeros((extent, width), BF16)
            if a == 1:
                target[row : row + count, lanes] = low[b]
            elif a == 0:
                target[row : row + extent, lanes] = blank
                target[row + extent : row + count, lanes] = low[b, : count - extent, :]
            else:
                target[row : row + count - extent, lanes] = low[b, extent:, :]
                target[row + count - extent : row + count, lanes] = blank
            continue
        start -= fine
        if a == 1:
            part = high[b, start : start + count, :]
        elif extent % 8 == 0:
            blank = jnp.zeros((extent, width), F32)
            if a == 0:
                part = jnp.concatenate([blank, high[b, start : start + count - extent, :]], axis=0)
            else:
                part = jnp.concatenate([high[b, start + extent : start + count, :], blank], axis=0)
        else:
            whole = high[b, start : start + count, :]
            at = iota((count, 1), 0)
            if a == 0:
                part = jnp.where(at < extent, 0.0, pltpu.roll(whole, extent, 0))
            else:
                part = jnp.where(at >= count - extent, 0.0, pltpu.roll(whole, count - extent, 0))
        target[row : row + count, lanes] = part.astype(BF16)


def shift_scratch(side, width):
    fine = side * side
    return [
        pltpu.VMEM((3, fine, width), BF16),
        pltpu.VMEM((3, rows_of(side) - fine, width), F32),
    ]


def dot(left, right):
    return lax.dot_general(left, right, (((1,), (0,)), ((), ())), preferred_element_type=F32)


def dot_last(left, right):
    return lax.dot_general(left, right, (((1,), (1,)), ((), ())), preferred_element_type=F32)


def block_of(index, extent):
    bits = extent.bit_length() - 1
    return ((index >> (bits + 1)) << (bits - 1)) + ((index & (extent - 1)) >> 1)


def pool_matrix(extent, value):
    count = extent * extent
    shape = (count // 4, count)
    return jnp.where(block_of(iota(shape, 1), extent) == iota(shape, 0), value, 0.0).astype(BF16)


def spread_matrix(extent):
    count = extent * extent
    shape = (count, count // 4)
    return jnp.where(block_of(iota(shape, 0), extent) == iota(shape, 1), 1.0, 0.0).astype(BF16)


def spread(matrix, value):
    high = value.astype(BF16)
    low = (value - high.astype(F32)).astype(BF16)
    return dot(matrix, high) + dot(matrix, low)


def gelu_and_slope(z):
    root = 0.7978845608028654
    inner = root * (z + 0.044715 * z * z * z)
    t = jnp.tanh(inner)
    half = 0.5 * (1.0 + t)
    slope = half + 0.5 * z * (1.0 - t * t) * (root * (1.0 + 3 * 0.044715 * z * z))
    return z * half, slope


def head_cotangents(cot, coarse_cot, weights):
    return jnp.concatenate(
        [
            (weights[0] * cot).astype(BF16),
            (weights[1] * cot).astype(BF16),
            (weights[2] * coarse_cot).astype(BF16),
        ],
        axis=0,
    )


def copies(pairs, sems):
    made = [
        pltpu.make_async_copy(source, target, sems.at[num])
        for num, (source, target) in enumerate(pairs)
    ]
    for one in made:
        one.start()
    return made


def tap_norm(tap):
    return lax.rsqrt(jnp.mean(tap * tap, axis=-1, keepdims=True) + EPSILON)


def tap_backward(tap, r, scale_row, back, wide, mid):
    back = jnp.concatenate([spread(wide, 0.25 * back[:mid]), back[mid:]], axis=0)
    upstream = back * scale_row
    grad = r * (upstream - tap * (r * r) * jnp.mean(upstream * tap, axis=-1, keepdims=True))
    return grad, jnp.sum(back * tap * r, axis=0, keepdims=True)


def section_kernel(
    side,
    dp,
    plan,
    features,
    trunk_weight,
    head_weight,
    cotangent,
    gain_in,
    shift_in,
    scale_in,
    merging_in,
    own_out,
    send_out,
    pass_out,
    grad_out,
    slope_out,
    normed_out,
    scale_out,
    feed,
    weights,
    heads,
    cot_ref,
    gain,
    shift,
    scale,
    merging,
    low_shifted,
    high_shifted,
    patch,
    sems,
):
    rows = rows_of(side)
    fine = side * side
    channels = feed.shape[1]
    half = channels // 2
    width = heads.shape[1]
    at = Layout(side, channels, width)
    mid = at.mid
    pipe = lax.axis_index("pipe")
    core = own_core(dp)
    pick = block_bits(dp, core, LATE)[0]
    made = copies(
        [(features.at[plan[0, pipe]], feed)]
        + [
            (
                trunk_weight.at[num // 3, pl.ds(num % 3 * 3 * channels, 3 * channels)],
                weights.at[num],
            )
            for num in range(6)
        ]
        + [(cotangent.at[pipe], cot_ref), (head_weight.at[1], heads)]
        + [(gain_in, gain), (shift_in, shift), (scale_in, scale), (merging_in, merging)],
        sems,
    )
    made[0].wait()

    def conv(value, layer):
        column_shifts(value, side, low_shifted, high_shifted)
        total = jnp.zeros((rows, channels), F32)
        for a in range(3):
            for b in range(3):
                put_row_shift(patch, 0, b * channels, low_shifted, high_shifted, b, a, side)
            made[1 + 3 * layer + a].wait()
            total = total + dot(patch[...], weights[3 * layer + a])
        return total

    def put_halves(first, value):
        count = value.shape[0]
        left = value[:, :half]
        right = value[:, half:]
        own_out[first : first + count, :] = jnp.where(core == 0, left, right)
        send_out[first : first + count, :] = jnp.where(core == 0, right, left)

    low_feed = feed[...]
    feed_value = low_feed.astype(F32)
    put_halves(at.feed, low_feed)
    first_pre = conv(feed_value, 0)
    for num in range(9, 13):
        made[num].wait()
    act1, slope1 = gelu_and_slope(gain[0:1, :] * first_pre + shift[0:1, :])
    slope_out[...] = slope1 * gain[0:1, :]
    low_act = act1.astype(BF16)
    put_halves(at.act, low_act)
    z2 = gain[1:2, :] * conv(low_act.astype(F32), 1) + shift[1:2, :]
    trunk_out, slope2 = gelu_and_slope(z2)
    taps = [feed_value, trunk_out.astype(BF16).astype(F32)]

    pool = pool_matrix(side, 0.25)
    for k in range(2):
        tap = taps[k]
        r = tap_norm(tap)
        normed = (tap * r * scale[k : k + 1, :]).astype(BF16)
        pooled = dot(pool, normed[:fine]).astype(BF16)
        rows_k = jnp.concatenate([pooled, normed[fine:]], axis=0)
        put_halves(at.normed + k * at.stacked, rows_k)
        normed_out[k] = rows_k
    made[7].wait()
    cot_low = cot_ref[...]
    coarse_cot = dot(pool_matrix(side // 2, 1.0), cot_low)
    grads = head_cotangents(
        cot_low.astype(F32), coarse_cot, [merging[s, 1:2, :] for s in range(3)]
    )
    made[8].wait()
    tap_grad, scale_row = tap_backward(
        tap, r, scale[1:2, :], dot_last(grads, heads[...]), spread_matrix(side), mid
    )
    scale_out[...] = jnp.broadcast_to(scale_row, scale_out.shape)
    grad2 = (tap_grad.astype(BF16).astype(F32) * slope2 * gain[1:2, :]).astype(BF16)
    for num in range(2):
        grad_out[num * rows : (num + 1) * rows, :] = grad2[:, num * half : (num + 1) * half]
    for target in (own_out, send_out):
        for num in range(2):
            target[at.grad[num] : at.grad[num] + rows, :] = grad2[:, num * half : (num + 1) * half]
        for num in range(at.lanes):
            lanes = slice(num * half, (num + 1) * half)
            target[at.cot + num * mid : at.cot + (num + 1) * mid, :] = cot_low[:, lanes]
    pass_out[...] = own_out[pl.ds(pl.multiple_of((1 - pick) * at.skip, 16), at.span), :]


def section(dp, plan, features, trunk_weight, head_weight, cotangent, gain, shift, scale, merging):
    side = SIDE
    rows = rows_of(side)
    channels = features.shape[2]
    half = channels // 2
    width = head_weight.shape[2]
    mid = cotangent.shape[1]
    at = Layout(side, channels, width)
    vmem = spec(pltpu.VMEM)
    return call(
        partial(section_kernel, side, dp),
        "section",
        60,
        1150000000,
        (plan, features, trunk_weight, head_weight, cotangent, gain, shift, scale, merging),
        [spec(pltpu.SMEM)] + [spec(pltpu.HBM)] * 8,
        (
            jax.ShapeDtypeStruct((at.total, half), BF16),
            jax.ShapeDtypeStruct((at.total, half), BF16),
            jax.ShapeDtypeStruct((at.span, half), BF16),
            jax.ShapeDtypeStruct((2 * rows, half), BF16),
            jax.ShapeDtypeStruct((rows, channels), F32),
            jax.ShapeDtypeStruct((2, at.stacked, channels), BF16),
            jax.ShapeDtypeStruct((8, channels), F32),
        ),
        (vmem,) * 7,
        [
            pltpu.VMEM((rows, channels), BF16),
            pltpu.VMEM((6, 3 * channels, channels), BF16),
            pltpu.VMEM((channels, width), BF16),
            pltpu.VMEM((mid, width), BF16),
            pltpu.VMEM(gain.shape, F32),
            pltpu.VMEM(shift.shape, F32),
            pltpu.VMEM(scale.shape, F32),
            pltpu.VMEM(merging.shape, F32),
            *shift_scratch(side, channels),
            pltpu.VMEM((rows, 3 * channels), BF16),
            pltpu.SemaphoreType.DMA((13,)),
        ],
    )


def back_kernel(side, layer, grad_in, trunk_weight, factor_in, *rest):
    grad, factor, weights, low_shifted, high_shifted, patch, sems = rest[-7:]
    channels = trunk_weight.shape[2]
    half = channels // 2
    rows = rows_of(side)
    made = copies(
        [(grad_in, grad)]
        + [
            (trunk_weight.at[layer, pl.ds(num * channels, channels)], weights.at[num])
            for num in range(9)
        ]
        + [(factor_in, factor)],
        sems,
    )
    made[0].wait()
    value = jnp.concatenate([grad[:rows, :], grad[rows:, :]], axis=1).astype(F32)
    column_shifts(value, side, low_shifted, high_shifted)
    total = jnp.zeros((rows, channels), F32)
    for a in range(3):
        for b in range(3):
            put_row_shift(
                patch, 0, b * channels, low_shifted, high_shifted, 2 - b, 2 - a, side
            )
        for b in range(3):
            made[1 + 3 * a + b].wait()
            total = total + dot_last(
                patch[:, b * channels : (b + 1) * channels], weights[3 * a + b]
            )
    made[10].wait()
    if layer == 1:
        (grad_out,) = rest[:-7]
        low = (total * factor[...]).astype(BF16)
        grad_out[:rows, :] = low[:, :half]
        grad_out[rows:, :] = low[:, half:]
        return
    merged, own_out, send_out = rest[:-7]
    pipe = lax.axis_index("pipe")
    total = total + factor[...]
    left, right = total[:, :half], total[:, half:]
    own_out[...] = jnp.where(pipe == 0, left, right)
    sent = jnp.where(pipe == 0, right, left).astype(BF16)
    low_merged = merged[...]
    mid, width = low_merged.shape
    sent_merged = jnp.where(
        pipe == 0, low_merged[:, width // 2 :], low_merged[:, : width // 2]
    )
    for num in range(half // 128):
        send_out[num * rows : (num + 1) * rows, :] = sent[:, num * 128 : (num + 1) * 128]
    first = half // 128 * rows
    for num in range(width // 256):
        send_out[first + num * mid : first + (num + 1) * mid, :] = sent_merged[
            :, num * 128 : (num + 1) * 128
        ]


def back(layer, grad, trunk_weight, factor, merged=None, after=()):
    side = SIDE
    rows = rows_of(side)
    channels = trunk_weight.shape[2]
    half = channels // 2
    vmem = spec(pltpu.VMEM)
    hbm = spec(pl.ANY)
    in_specs = [hbm, spec(pltpu.HBM), hbm]
    operands = [grad, trunk_weight, factor]
    if layer == 0:
        in_specs.append(vmem)
        operands.append(merged)
        out_shape = (
            jax.ShapeDtypeStruct((rows, half), F32),
            jax.ShapeDtypeStruct((half // 128 * rows + merged.size // 256, 128), BF16),
        )
        out_specs = (vmem, vmem)
    else:
        out_shape = jax.ShapeDtypeStruct((2 * rows, half), BF16)
        out_specs = vmem
    return call(
        partial(back_kernel, side, layer),
        "back",
        60 if layer else 46,
        350000000,
        operands,
        in_specs,
        out_shape,
        out_specs,
        [
            pltpu.VMEM((2 * rows, half), BF16),
            pltpu.VMEM((rows, channels), F32),
            pltpu.VMEM((9, channels, channels), BF16),
            *shift_scratch(side, channels),
            pltpu.VMEM((rows, 3 * channels), BF16),
            pltpu.SemaphoreType.DMA((11,)),
        ],
        after,
    )


def move_kernel(moves, *refs):
    sources, out, sems = refs[:-2], refs[-2], refs[-1]
    made = copies(
        [
            (sources[num].at[first()], out.at[pl.ds(place, count)])
            for num, first, place, count in moves
        ],
        sems,
    )
    for one in made:
        one.wait()


def far_factors(dp, other, side, width, after):
    half = other.shape[1]
    at = Layout(side, 2 * half, width)

    def rows():
        pick = block_bits(dp, own_core(dp), LATE)[0]
        return pl.ds(pl.multiple_of((1 - pick) * at.skip, 16), at.span)

    return call(
        partial(move_kernel, [(0, rows, 0, at.span)]),
        "far_factors",
        4,
        30000000,
        (other,),
        [spec(pl.ANY)],
        jax.ShapeDtypeStruct((at.span, half), BF16),
        spec(pltpu.VMEM),
        [pltpu.SemaphoreType.DMA((1,))],
        after,
    )


def first_factors(dp, own, other, own_grad, other_grad, side, width, after):
    half = other.shape[1]
    at = Layout(side, 2 * half, width)

    def feed():
        return pl.ds(at.feed, at.rows)

    def grad():
        pick = block_bits(dp, own_core(dp), EARLY)[0]
        return pl.ds(pl.multiple_of((1 - pick) * at.rows, 16), at.rows)

    return call(
        partial(
            move_kernel,
            [
                (num, (feed, feed, grad, grad)[num], num * at.rows, at.rows)
                for num in range(4)
            ],
        ),
        "first_factors",
        4,
        90000000,
        (own, other, own_grad, other_grad),
        [spec(pl.ANY)] * 4,
        jax.ShapeDtypeStruct((4 * at.rows, half), BF16),
        spec(pltpu.VMEM),
        [pltpu.SemaphoreType.DMA((4,))],
        after,
    )


def put_trunk_blocks(dp, piece, send, keep, xs, gs, low, high, patch, side, wait_x, wait_g):
    rows = rows_of(side)
    half = xs.shape[1]
    quarter = half // 2
    _, second, third = block_bits(dp, own_core(dp), piece)
    for image in range(4):
        wait_g(image)
        column_shifts(gs[image * rows : (image + 1) * rows, :].astype(F32), side, low, high)
        for a in range(3):
            for b in range(3):
                put_row_shift(
                    patch, image * rows, (3 * a + b) * half, low, high, 2 - b, 2 - a, side
                )
    for image in range(4):
        wait_x(image)
    turned = xs[...].T
    for offset in range(9):
        product = dot(turned, patch[:, offset * half : (offset + 1) * half]).astype(BF16)
        left, right = product[:, :128], product[:, 128:]
        for target, value in (
            (keep, jnp.where(second == 0, left, right)),
            (send, jnp.where(second == 0, right, left)),
        ):
            upper, lower = value[:quarter], value[quarter:]
            row = offset * quarter
            target[row : row + quarter, :] = jnp.where(third == 0, upper, lower)
            row += 9 * quarter
            target[row : row + quarter, :] = jnp.where(third == 0, lower, upper)


def late_grads_kernel(
    side, dp, width, own, other, near, far, send, keep, xs, gs, low, high, patch, sems
):
    half = xs.shape[1]
    at = Layout(side, 2 * half, width)
    rows = at.rows
    pick = block_bits(dp, own_core(dp), LATE)[0]
    grad_at = pick * at.grad[1]
    pairs = []
    for num, source in enumerate((own, other, near, far)):
        back_by = 0 if num < 2 else pick * at.skip

        def some(first):
            return source.at[pl.ds(pl.multiple_of(first - back_by, 16), rows)]

        pairs += [
            (some(grad_at), gs.at[pl.ds(num * rows, rows)]),
            (some(at.act), xs.at[pl.ds(num * rows, rows)]),
        ]
    made = copies(pairs, sems)
    put_trunk_blocks(
        dp,
        LATE,
        send,
        keep,
        xs,
        gs,
        low,
        high,
        patch,
        side,
        lambda image: made[2 * image + 1].wait(),
        lambda image: made[2 * image].wait(),
    )


def split_pair(value):
    high = value.astype(BF16).astype(F32)
    return jnp.concatenate([high, value - high], axis=0).astype(BF16)


def trunk_scratch(rows, half):
    return shift_scratch(SIDE, half) + [pltpu.VMEM((4 * rows, 9 * half), BF16)]


def late_grads(dp, width, own, other, near, far, after):
    side = SIDE
    rows = rows_of(side)
    half = own.shape[1]
    vmem = spec(pltpu.VMEM)
    shape = jax.ShapeDtypeStruct((9 * half, 128), BF16)
    return call(
        partial(late_grads_kernel, side, dp, width),
        "late_grads",
        28,
        430000000,
        (own, other, near, far),
        [spec(pl.ANY)] * 4,
        (shape, shape),
        (vmem, vmem),
        [
            pltpu.VMEM((4 * rows, half), BF16),
            pltpu.VMEM((4 * rows, half), BF16),
            *trunk_scratch(rows, half),
            pltpu.SemaphoreType.DMA((8,)),
        ],
        after,
    )


def early_grads_kernel(
    side, dp, width, own, other, own_g, other_g, far, send, keep, xs, gs, low, high, patch, sems
):
    half = xs.shape[1]
    at = Layout(side, 2 * half, width)
    rows = at.rows
    pick = block_bits(dp, own_core(dp), EARLY)[0]
    mine = pl.ds(pl.multiple_of(pick * rows, 16), rows)
    made = copies(
        [
            (own_g.at[mine], gs.at[pl.ds(0, rows)]),
            (other_g.at[mine], gs.at[pl.ds(rows, rows)]),
            (far.at[pl.ds(2 * rows, 2 * rows)], gs.at[pl.ds(2 * rows, 2 * rows)]),
            (own.at[pl.ds(at.feed, rows)], xs.at[pl.ds(0, rows)]),
            (other.at[pl.ds(at.feed, rows)], xs.at[pl.ds(rows, rows)]),
            (far.at[pl.ds(0, 2 * rows)], xs.at[pl.ds(2 * rows, 2 * rows)]),
        ],
        sems,
    )
    put_trunk_blocks(
        dp,
        EARLY,
        send,
        keep,
        xs,
        gs,
        low,
        high,
        patch,
        side,
        lambda image: made[3 + image].wait() if image < 3 else None,
        lambda image: made[image].wait() if image < 3 else None,
    )


def early_grads(dp, width, own, other, own_g, other_g, far, after):
    side = SIDE
    rows = rows_of(side)
    half = own.shape[1]
    vmem = spec(pltpu.VMEM)
    shape = jax.ShapeDtypeStruct((9 * half, 128), BF16)
    return call(
        partial(early_grads_kernel, side, dp, width),
        "early_grads",
        28,
        370000000,
        (own, other, own_g, other_g, far),
        [spec(pl.ANY)] * 5,
        (shape, shape),
        (vmem, vmem),
        [
            pltpu.VMEM((4 * rows, half), BF16),
            pltpu.VMEM((4 * rows, half), BF16),
            *trunk_scratch(rows, half),
            pltpu.SemaphoreType.DMA((6,)),
        ],
        after,
    )


def head_grads_kernel(
    side,
    dp,
    plan,
    features,
    head_weight,
    normed_in,
    scale_in,
    last_scale_in,
    own,
    other,
    merging_in,
    send,
    keep,
    merged_out,
    tap_grad_out,
    feed,
    heads,
    normed,
    scale,
    last_scale,
    ns,
    cots,
    merging,
    sems,
):
    half = ns.shape[2]
    width = merging.shape[2]
    at = Layout(side, 2 * half, width)
    mid = at.mid
    quarter = half // 2
    pick, second, third = block_bits(dp, own_core(dp), HEAD)
    pairs = [(merging_in, merging)]
    for num, source in enumerate((own, other)):
        pairs += [
            (source.at[pl.ds(at.cot, at.lanes * mid)], cots.at[num]),
            (source.at[pl.ds(at.normed, 2 * at.stacked)], ns.at[num]),
        ]
    pairs += [(normed_in, normed), (head_weight.at[0], heads.at[0])]
    pairs += [(features.at[plan[0, lax.axis_index("pipe")]], feed), (scale_in, scale)]
    pairs += [(last_scale_in, last_scale), (head_weight.at[1], heads.at[1])]
    made = copies(pairs, sems)
    sums = pool_matrix(side // 2, 1.0)
    cotangents = []
    for image in range(2):
        made[1 + 2 * image].wait()
        cot_low = jnp.concatenate(
            [cots[image, num * mid : (num + 1) * mid, :] for num in range(at.lanes)], axis=1
        )
        cotangents.append((cot_low.astype(F32), dot(sums, cot_low)))
    for one in (made[0], made[2], made[4]):
        one.wait()
    for target, tap in ((send, 1 - pick), (keep, pick)):
        weights = [merging[s, pl.ds(tap, 1), :] for s in range(3)]
        grads = [head_cotangents(cot, coarse, weights) for cot, coarse in cotangents]
        first = pl.multiple_of(tap * at.stacked, 16)
        both = [ns[image, pl.ds(first, at.stacked), :] for image in range(2)]
        product = dot(
            jnp.concatenate(both, axis=0).T, jnp.concatenate(grads, axis=0)
        ).astype(BF16)
        for lane in range(2):
            for num in range(width // 256):
                column = lane * (width // 2) + num * 128
                for part in range(2):
                    row = ((lane ^ second) * 2 + (part ^ third)) * (width // 256) + num
                    target[pl.ds(pl.multiple_of(row * quarter, quarter), quarter), :] = product[
                        part * quarter : (part + 1) * quarter, column : column + 128
                    ]
    cot, coarse_cot = cotangents[0]
    merged = jnp.zeros((mid, width), F32)
    coarse_merged = jnp.zeros((at.stacked - 2 * mid, width), F32)
    small = []
    made[5].wait()
    for k in range(2):
        made[6 if k == 0 else 10].wait()
        weights = [merging[s, k : k + 1, :] for s in range(3)]
        product = dot(normed[k], heads[k])
        merged = merged + weights[0] * product[:mid] + weights[1] * product[mid : 2 * mid]
        coarse_merged = coarse_merged + weights[2] * product[2 * mid :]
        small.append(jnp.sum(cot * product[:mid], axis=0, keepdims=True))
        small.append(jnp.sum(cot * product[mid : 2 * mid], axis=0, keepdims=True))
        small.append(jnp.sum(coarse_cot * product[2 * mid :], axis=0, keepdims=True))
        if k == 0:
            for one in made[7:10]:
                one.wait()
            tap = feed[...].astype(F32)
            back = dot_last(head_cotangents(cot, coarse_cot, weights), heads[0])
            tap_grad_out[...], scale_row = tap_backward(
                tap, tap_norm(tap), scale[0:1, :], back, spread_matrix(side), mid
            )
    merged = merged + spread(spread_matrix(side // 2), coarse_merged)
    merged_out[...] = merged.astype(BF16)
    small.append(
        jnp.concatenate(
            [scale_row, last_scale[0:1, :], jnp.zeros((1, width - 4 * half), F32)], axis=1
        )
    )
    small.append(jnp.zeros((1, width), F32))
    pair = split_pair(jnp.concatenate(small, axis=0))
    first = width // 128 * half
    for num in range(width // 128):
        for target in (send, keep):
            target[first + num * 16 : first + (num + 1) * 16, :] = pair[
                :, num * 128 : (num + 1) * 128
            ]


def head_grads(
    dp, plan, features, head_weight, normed, scale, last_scale, own, other, merging, after
):
    side = SIDE
    rows = rows_of(side)
    half = own.shape[1]
    width = merging.shape[2]
    at = Layout(side, 2 * half, width)
    shape = jax.ShapeDtypeStruct((width // 128 * half + 16 * width // 128, 128), BF16)
    vmem = spec(pltpu.VMEM)
    return call(
        partial(head_grads_kernel, side, dp),
        "head_grads",
        40,
        610000000,
        (plan, features, head_weight, normed, scale, last_scale, own, other, merging),
        [spec(pltpu.SMEM), spec(pltpu.HBM), spec(pltpu.HBM), spec(pl.ANY), spec(pltpu.HBM)]
        + [spec(pl.ANY)] * 3
        + [spec(pltpu.HBM)],
        (
            shape,
            shape,
            jax.ShapeDtypeStruct((at.mid, width), BF16),
            jax.ShapeDtypeStruct((rows, 2 * half), F32),
        ),
        (vmem,) * 4,
        [
            pltpu.VMEM((rows, 2 * half), BF16),
            pltpu.VMEM((2, 2 * half, width), BF16),
            pltpu.VMEM((2, at.stacked, 2 * half), BF16),
            pltpu.VMEM(scale.shape, F32),
            pltpu.VMEM(last_scale.shape, F32),
            pltpu.VMEM((2, 2 * at.stacked, half), BF16),
            pltpu.VMEM((2, at.lanes * at.mid, half), BF16),
            pltpu.VMEM(merging.shape, F32),
            pltpu.SemaphoreType.DMA((11,)),
        ],
        after,
    )


def held_back(array, after):
    def kernel(*refs):
        pass

    hbm = spec(pl.ANY)
    shape = jax.ShapeDtypeStruct(array.shape, array.dtype)
    return call(kernel, "held_back", 4, 1024, (array,), [hbm], shape, hbm, (), after, {0: 0})


def add_tails(one, two):
    count = one.shape[0] // 16
    one = one.astype(F32).reshape(count, 16, 128)
    two = two.astype(F32).reshape(count, 16, 128)
    total = (one[:, :8] + one[:, 8:]) + (two[:, :8] + two[:, 8:])
    high = total.astype(BF16).astype(F32)
    return jnp.concatenate([high, total - high], axis=1).reshape(count * 16, 128).astype(BF16)


def sum_kernel(tail, keep, received, *outs):
    rows = keep.shape[0] - tail
    size = rows // len(outs)
    for num, out in enumerate(outs):
        part = slice(num * size, (num + 1) * size)
        out[:size, :] = (keep[part, :].astype(F32) + received[part, :].astype(F32)).astype(BF16)
    if tail:
        total = add_tails(keep[rows:, :], received[rows:, :])
        for out in outs:
            out[size:, :] = total


def summed(keep, received, parts, tail, after):
    vmem = spec(pltpu.VMEM)
    shape = jax.ShapeDtypeStruct(((keep.shape[0] - tail) // parts + tail, 128), BF16)
    return call(
        partial(sum_kernel, tail),
        "summed",
        4,
        10000000,
        (keep, received),
        [vmem, vmem],
        (shape,) * parts,
        (vmem,) * parts,
        (),
        after,
    )


def pair_kernel(one, two, out):
    rows = out.shape[0] // 2
    out[:rows, :] = one[:rows, :]
    out[rows:, :] = two[:rows, :]


def paired(one, two, rows, after):
    vmem = spec(pltpu.VMEM)
    return call(
        pair_kernel,
        "paired",
        4,
        10000000,
        (one, two),
        [vmem, vmem],
        jax.ShapeDtypeStruct((2 * rows, 128), BF16),
        vmem,
        (),
        after,
    )


def widen_trunk_kernel(dp, layer, half, kinds, *refs):
    sources = refs[: len(kinds)]
    out, held, wide, sems_in, sems_out = refs[-5:]
    quarter = half // 2
    size = 9 * quarter
    jobs = []
    coming = []
    for source, (is_other, is_new) in zip(sources, kinds):
        core = own_core(dp) ^ int(is_other)
        first, second, third = block_bits(dp, core, LATE if layer else EARLY)
        first = first ^ int(is_new)
        for part in range(2):
            for lane in range(2):
                row = pl.multiple_of(((lane ^ second) * 2 + part) * size, size)
                coming.append((source.at[pl.ds(row, size)], held.at[len(jobs), lane]))
            jobs.append((core * half + (part ^ third) * quarter, first * half))
    made = copies(coming, sems_in)
    going = []
    for num, (row, column) in enumerate(jobs):
        for lane in range(2):
            made[2 * num + lane].wait()
            for offset in range(9):
                wide[num, offset, :, lane * 128 : (lane + 1) * 128] = held[
                    num, lane, offset * quarter : (offset + 1) * quarter, :
                ].astype(F32)
        one = pltpu.make_async_copy(
            wide.at[num],
            out.at[
                layer,
                :,
                pl.ds(pl.multiple_of(row, quarter), quarter),
                pl.ds(pl.multiple_of(column, half), half),
            ],
            sems_out.at[num],
        )
        one.start()
        going.append(one)
    for one in going:
        one.wait()


def widen_trunk(dp, layer, layers, half, sources, kinds, before=None, after=()):
    hbm = spec(pl.ANY)
    operands = list(sources) + ([before] if before is not None else [])
    count = 2 * len(kinds)
    return call(
        partial(widen_trunk_kernel, dp, layer, half, kinds),
        "widen_trunk",
        24,
        290000000,
        operands,
        [hbm] * len(operands),
        jax.ShapeDtypeStruct((layers, 9, 2 * half, 2 * half), F32),
        hbm,
        [
            pltpu.VMEM((count, 2, 9 * half // 2, 128), BF16),
            pltpu.VMEM((count, 9, half // 2, half), F32),
            pltpu.SemaphoreType.DMA((2 * count,)),
            pltpu.SemaphoreType.DMA((count,)),
        ],
        after,
        {len(sources): 0} if before is not None else None,
    )


def widen_heads_kernel(dp, half, kinds, *refs):
    sources = refs[: len(kinds)]
    out, held, wide, sems_in, sems_out = refs[-5:]
    quarter = half // 2
    size = held.shape[2]
    width = wide.shape[2]
    jobs = []
    coming = []
    for source, (is_other, is_new) in zip(sources, kinds):
        core = own_core(dp) ^ int(is_other)
        first, second, third = block_bits(dp, core, HEAD)
        for lane in range(2):
            for part in range(2):
                row = pl.multiple_of(((lane ^ second) * 2 + (part ^ third)) * size, size)
                coming.append((source.at[pl.ds(row, size)], held.at[len(jobs), part]))
            jobs.append((first ^ int(is_new), core * half, lane * width))
    made = copies(coming, sems_in)
    going = []
    for num, (tap, row, column) in enumerate(jobs):
        for part in range(2):
            made[2 * num + part].wait()
            for piece in range(width // 128):
                wide[
                    num, part * quarter : (part + 1) * quarter, piece * 128 : (piece + 1) * 128
                ] = held[num, part, piece * quarter : (piece + 1) * quarter, :].astype(F32)
        one = pltpu.make_async_copy(
            wide.at[num],
            out.at[tap, pl.ds(pl.multiple_of(row, half), half), pl.ds(column, width)],
            sems_out.at[num],
        )
        one.start()
        going.append(one)
    for one in going:
        one.wait()


def widen_heads(dp, half, width, sources, kinds, before=None, after=()):
    hbm = spec(pl.ANY)
    operands = list(sources) + ([before] if before is not None else [])
    count = 2 * len(kinds)
    return call(
        partial(widen_heads_kernel, dp, half, kinds),
        "widen_heads",
        40,
        440000000,
        operands,
        [hbm] * len(operands),
        jax.ShapeDtypeStruct((2, 2 * half, width), F32),
        hbm,
        [
            pltpu.VMEM((count, 2, width // 256 * half // 2, 128), BF16),
            pltpu.VMEM((count, half, width // 2), F32),
            pltpu.SemaphoreType.DMA((2 * count,)),
            pltpu.SemaphoreType.DMA((count,)),
        ],
        after,
        {len(sources): 0} if before is not None else None,
    )


def finish_kernel(
    dp, tail, plan, own_feed, merged, received, own_sum, other_sum,
    merged_out, feed_out, scale_out, merging_out,
    feeds, maps, ours, theirs, scales, weights, sems,
):
    rows, half = own_feed.shape
    mid, width = merged.shape
    first = own_sum.shape[0] - tail
    pipe = lax.axis_index("pipe")
    slot = plan[0, pipe]
    made = copies(
        [
            (own_feed, feed_out.at[slot]),
            (own_sum.at[pl.ds(first, tail)], ours),
            (other_sum.at[pl.ds(first, tail)], theirs),
        ],
        sems,
    )
    for num in range(half // 128):
        feeds[:, num * 128 : (num + 1) * 128] = received[
            num * rows : (num + 1) * rows, :
        ].astype(F32)
    low_merged = merged[...]
    maps[0] = jnp.where(pipe == 0, low_merged[:, : width // 2], low_merged[:, width // 2 :])
    first = half // 128 * rows
    for num in range(width // 256):
        maps[1, :, num * 128 : (num + 1) * 128] = received[
            first + num * mid : first + (num + 1) * mid, :
        ]
    going = [
        pltpu.make_async_copy(feeds, feed_out.at[1 - slot], sems.at[3]),
        pltpu.make_async_copy(maps.at[0], merged_out.at[pipe], sems.at[4]),
        pltpu.make_async_copy(maps.at[1], merged_out.at[1 - pipe], sems.at[5]),
    ]
    for one in going:
        one.start()
    made[1].wait()
    made[2].wait()
    total = ours[...].astype(F32) + theirs[...].astype(F32)
    for num in range(width // 128):
        lanes = slice(num * 128, (num + 1) * 128)
        block = total[num * 16 : num * 16 + 8] + total[num * 16 + 8 : num * 16 + 16]
        for k in range(2):
            for s in range(3):
                weights[s, k : k + 1, lanes] = block[3 * k + s : 3 * k + s + 1]
            column = num * 128 - k * 2 * half
            if 0 <= column < 2 * half:
                scales[k : k + 1, column : column + 128] = block[6:7]
    going += [
        pltpu.make_async_copy(scales, scale_out, sems.at[6]),
        pltpu.make_async_copy(weights, merging_out, sems.at[7]),
    ]
    for one in going[3:]:
        one.start()
    for one in going + made[:1]:
        one.wait()


def finish(dp, plan, own_feed, merged, received, own_sum, other_sum, after):
    rows, half = own_feed.shape
    mid, width = merged.shape
    vmem = spec(pltpu.VMEM)
    hbm = spec(pl.ANY)
    tail = 16 * width // 128
    return call(
        partial(finish_kernel, dp, tail),
        "finish",
        8,
        170000000,
        (plan, own_feed, merged, received, own_sum, other_sum),
        [spec(pltpu.SMEM), hbm, vmem, vmem, hbm, hbm],
        (
            jax.ShapeDtypeStruct((2, mid, width // 2), BF16),
            jax.ShapeDtypeStruct((2, rows, half), F32),
            jax.ShapeDtypeStruct((2, 2 * half), F32),
            jax.ShapeDtypeStruct((3, 2, width), F32),
        ),
        (hbm,) * 4,
        [
            pltpu.VMEM((rows, half), F32),
            pltpu.VMEM((2, mid, width // 2), BF16),
            pltpu.VMEM((tail, 128), BF16),
            pltpu.VMEM((tail, 128), BF16),
            pltpu.VMEM((2, 2 * half), F32),
            pltpu.VMEM((3, 2, width), F32),
            pltpu.SemaphoreType.DMA((8,)),
        ],
        after,
    )


ORDER = (
    "back1",
    "far",
    "first",
    "head",
    "late",
    "early",
    "L2",
    "E2",
    "H1",
    "L3",
    "E3",
    "H2",
    "back0",
    "L4",
    "E4",
    "H3",
    "L5",
    "E5",
    "H4",
    "L6",
    "E6",
    "H5",
    "Lold_wide",
    "Eold_wide",
    "H6",
    "Lnew",
    "Lnew_own",
    "Hold_wide",
    "Enew",
    "Lnew_other",
    "Enew_own",
    "finish",
    "Hnew",
    "Enew_other",
    "Hnew_wide",
)
WAITS = {"far": ("near",), "L6": ("feed",)}


class Sum:
    def __init__(self, swap, piece, last, send, keep, tail=0):
        self.swap = partial(swap, piece)
        self.tail = tail
        self.steps = [("scatter", stage) for stage in range(0 if piece == HEAD else 1, 3)]
        self.steps += [("whole", stage) for stage in range(3, last + 1)]
        self.steps += [("gather", stage) for stage in (2, 1, 0)]
        self.at = 0
        self.keep = keep
        self.come = self.swap(self.steps[0][1], send)

    def advance(self, after):
        kind = self.steps[self.at][0]
        self.at += 1
        following, stage = self.steps[self.at]
        if kind == "gather":
            rows = self.keep.shape[0] - self.tail
            self.keep, mark = paired(self.keep, self.come, rows, after)
            self.tail = 0
            send = self.keep
        else:
            parts = 2 if following == "scatter" else 1
            made, mark = summed(self.keep, self.come, parts, self.tail, after)
            self.keep = made[0]
            send = made[-1]
            if following == "gather":
                self.final = self.keep
        self.come = self.swap(stage, send)
        return mark


def body(
    features,
    plan,
    trunk_weight,
    trunk_gain,
    trunk_shift,
    head_weight,
    norm_scale,
    merging_weight,
    merged_cotangent,
):
    dp = lax.axis_size("dp")
    devices = lax.axis_size("pipe") * dp
    layers = trunk_weight.shape[0]
    channels = features.shape[2]
    half = channels // 2
    width = head_weight.shape[2]
    last = dp.bit_length() - 2
    weights = trunk_weight.reshape(layers, 9 * channels, channels)
    merging = jnp.transpose(merging_weight, (1, 0, 2))
    tail = 16 * width // 128

    def swap(piece, stage, block):
        bits = stage_bits(dp, piece)[stage]
        route = [(i, i ^ (1 << bits[i & 1])) for i in range(devices)]
        return lax.ppermute(block, AXES, route)

    def swap_cores(block):
        return lax.ppermute(block, AXES, [(i, i ^ 1) for i in range(devices)])

    (own, send, passed, grad2, slope, normed, last_scale), mark = section(
        dp,
        plan,
        features,
        weights,
        head_weight,
        merged_cotangent,
        trunk_gain,
        trunk_shift,
        norm_scale,
        merging,
    )
    other = swap_cores(send)
    near = swap(LATE, 0, passed)
    kept = ((False, False), (True, False))
    came = ((False, True), (True, True))
    got = {"before": None, "heads": None}
    pieces = {}

    def make_back1(after):
        got["grad1"], mark = back(1, grad2, weights, slope, None, after)
        got["other_grad1"] = swap_cores(got["grad1"])
        return mark

    def make_far(after):
        passed, mark = far_factors(dp, other, SIDE, width, after)
        got["far"] = swap(LATE, 0, passed)
        return mark

    def make_first(after):
        grads = (got["grad1"], got["other_grad1"])
        passed, mark = first_factors(dp, own, other, *grads, SIDE, width, after)
        got["first"] = swap(EARLY, 0, passed)
        return mark

    def make_head(after):
        blocks, mark = head_grads(
            dp,
            plan,
            features,
            head_weight,
            normed,
            norm_scale,
            last_scale,
            own,
            other,
            merging,
            after,
        )
        pieces["H"] = Sum(swap, HEAD, last, *blocks[:2], tail)
        got["maps"], got["tap_grad"] = blocks[2:]
        return mark

    def make_late(after):
        blocks, mark = late_grads(dp, width, own, other, near, got["far"], after)
        pieces["L"] = Sum(swap, LATE, last, *blocks)
        return mark

    def make_early(after):
        grads = (got["grad1"], got["other_grad1"])
        blocks, mark = early_grads(dp, width, own, other, *grads, got["first"], after)
        pieces["E"] = Sum(swap, EARLY, last, *blocks)
        return mark

    def make_back0(after):
        (got["feed"], sent), mark = back(
            0, got["grad1"], weights, got["tap_grad"], got["maps"], after
        )
        got["received"] = lax.ppermute(sent, "pipe", [(0, 1), (1, 0)])
        return mark

    def make_finish(after):
        sums = (pieces["H"].final, swap_cores(pieces["H"].final))
        got["finish"], mark = finish(
            dp, plan, got["feed"], got["maps"], got["received"], *sums, after
        )
        return mark

    def widen(name, sources, kinds, after):
        if name == "H":
            got["heads"], mark = widen_heads(
                dp, half, width, sources, kinds, got["heads"], after
            )
        else:
            layer = 1 if name == "L" else 0
            got["before"], mark = widen_trunk(
                dp, layer, layers, half, sources, kinds, got["before"], after
            )
        return mark

    make = {
        "back1": make_back1,
        "far": make_far,
        "first": make_first,
        "head": make_head,
        "late": make_late,
        "early": make_early,
        "back0": make_back0,
        "finish": make_finish,
    }
    for step in ORDER:
        name, kind = step[0], step[1:]
        waits = [mark]
        for which in WAITS.get(step, ()):
            come = {"near": near, "far": got.get("far"), "first": got.get("first")}
            come["feed"] = got.get("received")
            waits.append(pieces[which].come if which in pieces else come[which])
        if step in make:
            mark = make[step](waits)
        elif kind == "new":
            pieces[name].come, mark = held_back(pieces[name].come, waits)
            got[name] = swap_cores(pieces[name].come)
        elif kind == "old_wide":
            sources = (pieces[name].keep, swap_cores(pieces[name].keep))
            mark = widen(name, sources, kept, waits)
        elif kind == "new_wide":
            mark = widen(name, (pieces[name].come, got[name]), came, waits)
        elif kind == "new_own":
            mark = widen(name, (pieces[name].come,), came[:1], waits)
        elif kind == "new_other":
            mark = widen(name, (got[name],), came[1:], waits)
        else:
            mark = pieces[name].advance(waits)
            if kind == "4":
                for _ in range(3, last):
                    mark = pieces[name].advance([mark])
    merged_maps, features_grad, scale_grad, merging_grad = got["finish"]
    return (
        merged_maps,
        features_grad,
        got["before"].reshape(trunk_weight.shape),
        got["heads"],
        scale_grad,
        jnp.transpose(merging_grad, (1, 0, 2)),
    )


def solution(mesh):
    placed = (P("dp", None, None), P("dp", None), P(), P(), P(), P(), P(), P(), P("dp", None, None))
    return jax.shard_map(
        body,
        mesh=mesh,
        in_specs=placed,
        out_specs=(P("dp", None, "pipe"), P("dp", None, "pipe"), P(), P(), P(), P()),
        check_vma=False,
    )
```
